32 devices in a mesh: row: 8 (over z, core), col: 4 (over y, x).
Axes of the slice: x: 2, y: 2, z: 4, core: 2. Of those that a mesh axis runs over, the one named last changes fastest.
Arguments:
- embed: bfloat16 [1024, 1024], P(('row', 'col')), may hold values from -0.1875 to 0.1875
- positives: int32 [1024, 4], P('row'), may hold values from 0 to 1023, as said below
- placement: int32 [1024], replicated, may hold values from 0 to 1023, as said below
Outputs:
- embed_grad: float32 [1024, 1024], P(('row', 'col'))
The draws below stay inside these ranges and needn't reach their ends.
Inputs may be any that keep to these rules, and one draw needn't show every extreme that they name: `positives`: each row names 4 different entities, none of them the entity placed at that row's position. `placement`: a permutation of the entity ids.
All inputs are finite; a program needn't handle non-finite values.
Results may differ from the reference program's by a relative error of at most 0.003.
Values may be sent and summed in bfloat16 or wider, within the bound.
No kernel may reach another device: no remote copies, remote signals or barrier semaphores. Data moves between devices by JAX's collectives and lax.ppermute only.
A program may use at most 64 MiB of HBM per device.

```python
import jax
import jax.numpy as jnp
from jax import lax

D = 1024
POS = 4
ENTITIES = 1024


def shared_layout(key):
    return jax.random.permutation(jax.random.fold_in(key, 7), jnp.arange(ENTITIES, dtype=jnp.int32)).astype(jnp.int32)


def draw_placement(key, part):
    return shared_layout(key)


def draw_positives(key, part):
    layout = shared_layout(key)
    entity_at = jnp.argsort(layout, stable=True).astype(jnp.int32)
    quarter = ENTITIES // POS
    jitter = jax.random.randint(jax.random.fold_in(key, 9), (ENTITIES, POS), 1, quarter, dtype=jnp.int32)
    offsets = jnp.arange(POS, dtype=jnp.int32)[None, :] * quarter + jitter
    return ((entity_at[:, None] + offsets) % ENTITIES).astype(jnp.int32)


def level_of(own_key, shape, shards, least, top_value):
    loudness, own = 1.0, jax.random.fold_in(own_key, 6)
    for dim, blocks in shards:
        draws = jnp.exp(jax.random.uniform(jax.random.fold_in(own, dim), (blocks,), jnp.float32, least / len(shards), top_value / len(shards)))
        loudness = loudness * jnp.repeat(draws, shape[dim] // blocks).reshape([-1 if axis == dim else 1 for axis in range(len(shape))])
    return loudness


def gaussian(key, dims, spread, limit, pieces=(), held_as=jnp.bfloat16):
    level = level_of(key, dims, pieces, -0.22, 0.18) if pieces else 1.0
    array = jax.random.normal(key, dims, jnp.float32) * spread * level
    return jnp.minimum(jnp.maximum(array, -limit), limit).astype(held_as)


def setup_inputs(seed: int = 0) -> dict:
    key_list = jax.random.split(jax.random.key(seed), 4)
    embed = gaussian(key_list[0], (ENTITIES, D), 0.03125, 0.1875, ((0, 32),))
    positives = draw_positives(jax.random.fold_in(key_list[3], 71), 0)
    placement = draw_placement(jax.random.fold_in(key_list[3], 71), 0)
    return {"embed": embed, "positives": positives, "placement": placement}


logistic_sharpness = 0.02

def positive_rank(matching_pair_affinity_lines):
    affinity_differences = (matching_pair_affinity_lines[:, None, :] - matching_pair_affinity_lines[:, :, None]) / logistic_sharpness
    return 0.5 + lax.optimization_barrier(jnp.sum(jax.nn.sigmoid(affinity_differences), axis=2))

def coefficients(matching_pair_affinity_lines, ranks, slopes, total):
    prank, pullback = jax.vjp(positive_rank, matching_pair_affinity_lines)
    factor = 1.0 / (matching_pair_affinity_lines.shape[1] * total)
    smoothed_ordering_slope = prank / (ranks * ranks) * factor
    prank_grad = -factor / ranks
    pulled = pullback(prank_grad)[0]
    ordering_coefficient_vector = smoothed_ordering_slope / logistic_sharpness
    extra = pulled - ordering_coefficient_vector * slopes
    return (ordering_coefficient_vector, extra)

def sigmoid_sums(cosine_affinity_matrix, matching_pair_affinity_lines, allowed):
    counts = []
    slopes = []
    for element_location in range(matching_pair_affinity_lines.shape[1]):
        difference_before_squash = jax.nn.sigmoid((cosine_affinity_matrix - matching_pair_affinity_lines[:, element_location:element_location + 1]) / logistic_sharpness)
        counts.append(lax.optimization_barrier(jnp.sum(jnp.where(allowed, difference_before_squash, 0.0), axis=1)))
        slopes.append(lax.optimization_barrier(jnp.sum(jnp.where(allowed, difference_before_squash * (1.0 - difference_before_squash), 0.0), axis=1)))
    return (jnp.stack(counts, axis=1), jnp.stack(slopes, axis=1))

def score_grads(cosine_affinity_matrix, matching_pair_affinity_lines, allowed, column_pos, targets, ordering_coefficient_vector, extra):
    dense = jnp.zeros(cosine_affinity_matrix.shape, jnp.float32)
    for element_location in range(matching_pair_affinity_lines.shape[1]):
        difference_before_squash = jax.nn.sigmoid((cosine_affinity_matrix - matching_pair_affinity_lines[:, element_location:element_location + 1]) / logistic_sharpness)
        dense = dense + ordering_coefficient_vector[:, element_location:element_location + 1] * jnp.where(allowed, difference_before_squash * (1.0 - difference_before_squash), 0.0)
    for element_location in range(matching_pair_affinity_lines.shape[1]):
        dense = dense + jnp.where(column_pos[None, :] == targets[:, element_location:element_location + 1], extra[:, element_location:element_location + 1], 0.0)
    return dense.astype(jnp.bfloat16)

def reference(embed, positives, placement):
    total = embed.shape[0]
    block_rows = math_block(total)
    targets_all = jnp.take(placement, positives).astype(jnp.int32)
    column_pos = jnp.arange(total, dtype=jnp.int32)

    def step(grad_cols, block):
        begin = (block * block_rows).astype(jnp.int32)
        rows = lax.dynamic_slice_in_dim(embed, begin, block_rows, 0)
        targets = lax.dynamic_slice_in_dim(targets_all, begin, block_rows, 0)
        cosine_affinity_matrix = jnp.einsum('ad,kd->ak', rows, embed, preferred_element_type=jnp.float32)
        own = begin + jnp.arange(block_rows, dtype=jnp.int32)
        allowed = column_pos[None, :] != own[:, None]
        matching_pair_affinity_lines = jnp.take_along_axis(cosine_affinity_matrix, targets, axis=1)
        counts, slopes = sigmoid_sums(cosine_affinity_matrix, matching_pair_affinity_lines, allowed)
        ranks = 0.5 + counts
        ordering_coefficient_vector, extra = coefficients(matching_pair_affinity_lines, ranks, slopes, total)
        grad_tile = score_grads(cosine_affinity_matrix, matching_pair_affinity_lines, allowed, column_pos, targets, ordering_coefficient_vector, extra)
        grad_rows = jnp.dot(grad_tile, embed, preferred_element_type=jnp.float32)
        grad_cols = grad_cols + lax.dot_general(grad_tile, rows, (((0,), (0,)), ((), ())), preferred_element_type=jnp.float32)
        return (grad_cols, grad_rows)
    blocks = jnp.arange(total // block_rows, dtype=jnp.int32)
    grad_cols, grad_rows = lax.scan(step, jnp.zeros(embed.shape, jnp.float32), blocks)
    return grad_rows.reshape(embed.shape) + grad_cols

def math_block(total):
    block_rows = 512
    while total % block_rows != 0:
        block_rows = block_rows // 2
    return block_rows
```

```python
import functools

import jax
import jax.numpy as jnp
from jax import lax
from jax.experimental import pallas as pl
from jax.experimental.pallas import tpu as pltpu
from jax.sharding import PartitionSpec as P

logistic_sharpness = 0.02
half_scale = 0.5 / logistic_sharpness
masked = -1e30
lane_block = 256
row_chunk = 64


def fold_rows(values):
    return jnp.sum(values.reshape(values.shape[0] // 8, 8, values.shape[1]), axis=0)


def lookup_rows(table_ref, ids):
    high = ids // 128
    low = ids % 128
    found = jnp.zeros(ids.shape, jnp.int32)
    for line in range(table_ref.shape[0]):
        entries = jnp.broadcast_to(table_ref[line : line + 1, :], ids.shape)
        picked = jnp.take_along_axis(entries, low, axis=1)
        found = jnp.where(high == line, picked, found)
    return found


def kernel(shard, width, pos_count, base_ref, packed_ref, table_ref, out_ref, score_ref, own_ref, stat_ref):
    total = packed_ref.shape[0]
    base = pl.multiple_of(base_ref[0], shard)
    embed_ref = packed_ref.at[:, 0:width]
    place = lax.broadcasted_iota(jnp.int32, (16, 128), 0)
    eye = (place == lax.broadcasted_iota(jnp.int32, (16, 128), 1)).astype(jnp.bfloat16)

    def target_step(block, carry):
        begin = pl.multiple_of(block * 128, 128)
        parts = lax.dot_general(
            eye,
            packed_ref[pl.ds(begin, 128), width : width + 128],
            (((1,), (1,)), ((), ())),
            preferred_element_type=jnp.float32,
        ).astype(jnp.int32)
        ids = parts[0:8, :] * 256 + parts[8:16, :]
        stat_ref[0:8, pl.ds(begin, 128)] = lookup_rows(table_ref, ids).astype(jnp.float32)
        return carry

    lax.fori_loop(0, total // 128, target_step, 0)

    def block_step(block, carry):
        start = pl.multiple_of(block * lane_block, lane_block)
        anchors = embed_ref[pl.ds(start, lane_block), :]
        targets = stat_ref[0:pos_count, pl.ds(start, lane_block)].astype(jnp.int32)
        index = lax.broadcasted_iota(jnp.int32, (row_chunk, lane_block), 0)
        lane = lax.broadcasted_iota(jnp.int32, (row_chunk, lane_block), 1)

        def score_step(chunk, sums):
            row = pl.multiple_of(chunk * row_chunk, row_chunk)
            scores = half_scale * lax.dot_general(
                embed_ref[pl.ds(row, row_chunk), :],
                anchors,
                (((1,), (1,)), ((), ())),
                preferred_element_type=jnp.float32,
            )
            scores = jnp.where(index + (row - start) == lane, masked, scores)
            score_ref[pl.ds(row, row_chunk), :] = scores
            return tuple(
                sums[m]
                + fold_rows(jnp.where(index == targets[m : m + 1, :] - row, scores, 0.0))
                for m in range(pos_count)
            )

        zero = jnp.zeros((8, lane_block), jnp.float32)
        sums = lax.fori_loop(0, total // row_chunk, score_step, (zero,) * pos_count)
        pos = [jnp.sum(part, axis=0, keepdims=True) for part in sums]

        def rank_step(chunk, sums):
            row = pl.multiple_of(chunk * row_chunk, row_chunk)
            scores = score_ref[pl.ds(row, row_chunk), :]
            out = []
            for m in range(pos_count):
                bent = jnp.tanh(scores - pos[m])
                out.append(sums[2 * m] + fold_rows(bent))
                out.append(sums[2 * m + 1] + fold_rows(bent * bent))
            return tuple(out)

        sums = lax.fori_loop(0, total // row_chunk, rank_step, (zero,) * (2 * pos_count))
        ranks = []
        slopes = []
        for m in range(pos_count):
            ranks.append(0.5 + 0.5 * (total + jnp.sum(sums[2 * m], axis=0, keepdims=True)))
            slopes.append(0.25 * (total - jnp.sum(sums[2 * m + 1], axis=0, keepdims=True)))
        own_ref[:, pl.ds(start, lane_block)] = score_ref[pl.ds(base, shard), :]

        factor = 1.0 / (pos_count * total)
        pulls = [-factor / ranks[m] for m in range(pos_count)]
        for m in range(pos_count):
            prank = 1.0
            pulled = 0.0
            for q in range(pos_count):
                if q != m:
                    bent = jnp.tanh(pos[q] - pos[m])
                    prank = prank + 0.5 * (1.0 + bent)
                    pulled = pulled + (pulls[q] - pulls[m]) * (0.25 * (1.0 - bent * bent))
            weight = prank / (ranks[m] * ranks[m]) * (factor / logistic_sharpness)
            extra = pulled / logistic_sharpness - weight * slopes[m]
            stat_ref[8 + m : 9 + m, pl.ds(start, lane_block)] = pos[m]
            stat_ref[16 + m : 17 + m, pl.ds(start, lane_block)] = 0.25 * weight
            stat_ref[24 + m : 25 + m, pl.ds(start, lane_block)] = extra
        return carry

    lax.fori_loop(0, total // lane_block, block_step, 0)

    scores = own_ref[...]
    lane = lax.broadcasted_iota(jnp.int32, (shard, total), 1)
    line = lax.broadcasted_iota(jnp.int32, (shard, total), 0) + base
    own_lane = pl.multiple_of(base // 128 * 128, 128)
    near = lax.broadcasted_iota(jnp.int32, (shard, 128), 1) + own_lane
    chosen = near == lax.broadcasted_iota(jnp.int32, (shard, 128), 0) + base

    def column(k):
        values = stat_ref[k : k + 1, pl.ds(own_lane, 128)]
        return jnp.sum(jnp.where(chosen, values, 0.0), axis=1, keepdims=True)

    grads = [jnp.zeros((shard, total), jnp.float32) for _ in range(2)]
    for m in range(pos_count):
        bent = jnp.tanh(scores - stat_ref[8 + m : 9 + m, :])
        grads[0] = grads[0] + stat_ref[16 + m : 17 + m, :] * (1.0 - bent * bent)
        bent = jnp.tanh(scores - column(8 + m))
        grads[1] = grads[1] + column(16 + m) * (1.0 - bent * bent)
    for m in range(pos_count):
        found = line == stat_ref[m : m + 1, :].astype(jnp.int32)
        grads[0] = grads[0] + jnp.where(found, stat_ref[24 + m : 25 + m, :], 0.0)
        found = lane == column(m).astype(jnp.int32)
        grads[1] = grads[1] + jnp.where(found, column(24 + m), 0.0)
    both = jnp.concatenate(grads, axis=0).astype(jnp.bfloat16)
    product = jnp.dot(both, embed_ref[...], preferred_element_type=jnp.float32)
    out_ref[...] = product[:shard, :] + product[shard:, :]


def body(embed, positives, placement):
    shard, width = embed.shape
    axes = ("row", "col")
    total = shard * lax.axis_size(axes)
    pos_count = positives.shape[1]
    ids = lax.dynamic_slice_in_dim(positives, lax.axis_index("col") * shard, shard, 0)
    tail = jnp.zeros((shard, 128), jnp.bfloat16)
    tail = tail.at[:, 0:pos_count].set((ids // 256).astype(jnp.bfloat16))
    tail = tail.at[:, 8 : 8 + pos_count].set((ids % 256).astype(jnp.bfloat16))
    packed = lax.all_gather(jnp.concatenate([embed, tail], axis=1), axes, axis=0, tiled=True)
    base = (lax.axis_index(axes) * shard).astype(jnp.int32).reshape(1)
    vmem = pl.BlockSpec(memory_space=pltpu.VMEM)
    return pl.pallas_call(
        functools.partial(kernel, shard, width, pos_count),
        out_shape=jax.ShapeDtypeStruct((shard, width), jnp.float32),
        in_specs=[pl.BlockSpec(memory_space=pltpu.SMEM), vmem, vmem],
        out_specs=vmem,
        scratch_shapes=[
            pltpu.VMEM((total, lane_block), jnp.float32),
            pltpu.VMEM((shard, total), jnp.float32),
            pltpu.VMEM((32, total), jnp.float32),
        ],
        compiler_params=pltpu.CompilerParams(vmem_limit_bytes=48 * 1024 * 1024),
        cost_estimate=pl.CostEstimate(
            flops=2 * total * total * width,
            bytes_accessed=2 * total * width,
            transcendentals=4 * total * total,
        ),
    )(base, packed, placement.reshape(-1, 128))


def solution(mesh):
    return jax.shard_map(
        body,
        mesh=mesh,
        in_specs=(P(("row", "col"), None), P("row", None), P()),
        out_specs=P(("row", "col"), None),
        check_vma=False,
    )
```

```python
import functools

import jax
import jax.numpy as jnp
from jax import lax
from jax.experimental import pallas as pl
from jax.experimental.pallas import tpu as pltpu
from jax.sharding import PartitionSpec as P

logistic_sharpness = 0.02
half_scale = 0.5 / logistic_sharpness
masked = -1e30
lane_block = 256
row_chunk = 256


def fold_rows(values):
    return jnp.sum(values.reshape(values.shape[0] // 8, 8, values.shape[1]), axis=0)


def lookup(table_ref, ids):
    low = ids % 128
    high = ids // 128
    found = jnp.zeros(ids.shape, jnp.int32)
    for line in range(table_ref.shape[0]):
        entries = jnp.broadcast_to(table_ref[line : line + 1, :], ids.shape)
        found = jnp.where(high == line, jnp.take_along_axis(entries, low, axis=1), found)
    return found


def kernel(cols, levels, shard, pos_count, *refs):
    place_ref, table_ref = refs[:2]
    lines = 2 * levels
    ids_refs = refs[2 : 2 + lines]
    blocks = refs[2 + lines : 2 + lines + 2 * cols]
    out_ref, embed_ref, score_ref, own_ref, target_ref, stat_ref, sems = refs[2 + lines + 2 * cols :]
    total = embed_ref.shape[0]
    me = place_ref[0]
    my_col = place_ref[1]

    copies = []
    for p in range(cols):
        for c in range(2):
            for d in range(levels):
                copies.append(
                    pltpu.make_async_copy(
                        blocks[p * 2 + c].at[d * shard : (d + 1) * shard, :],
                        embed_ref.at[pl.ds(((d * 2 + c) * cols + p) * shard, shard), :],
                        sems.at[len(copies)],
                    )
                )
    for copy in copies:
        copy.start()

    group = cols * shard
    for line in range(lines):
        for begin in range(0, group, 128):
            ids = ids_refs[line][:, begin : begin + 128]
            ids = jnp.concatenate([ids, ids], axis=0)
            found = lookup(table_ref, ids) ^ me
            lane = lax.broadcasted_iota(jnp.int32, found.shape, 1)
            found = jnp.take_along_axis(found, lane ^ (my_col % 128), axis=1)
            start = line * group + (begin ^ (my_col - my_col % 128))
            target_ref[:, pl.ds(pl.multiple_of(start, 128), 128)] = found
    for copy in copies:
        copy.wait()

    pair = lane_block // 128

    def score_chunk(anchors, start, buffer, chunk, picked):
        row = pl.multiple_of(chunk * row_chunk, row_chunk)
        scores = half_scale * lax.dot_general(
            embed_ref[pl.ds(row, row_chunk), :],
            anchors,
            (((1,), (1,)), ((), ())),
            preferred_element_type=jnp.float32,
        )
        index = lax.broadcasted_iota(jnp.int32, (row_chunk, lane_block), 0)
        lane = lax.broadcasted_iota(jnp.int32, (row_chunk, lane_block), 1)
        scores = jnp.where(index + (row - start) == lane, masked, scores)
        score_ref[buffer, pl.ds(row, row_chunk), :] = scores
        picked = list(picked)
        for half in range(pair):
            targets = target_ref[:, pl.ds(pl.multiple_of(start + half * 128, 128), 128)]
            near = (targets - row) >> 3
            sub = targets & 7
            for step in range(row_chunk // 8):
                tile = scores[step * 8 : (step + 1) * 8, half * 128 : (half + 1) * 128]
                tile = jnp.take_along_axis(tile, sub, axis=0)
                picked[half] = jnp.where(near == step, tile, picked[half])
        return tuple(picked)

    def rank_chunk(pos, buffer, chunk, sums):
        row = pl.multiple_of(chunk * row_chunk, row_chunk)
        sums = list(sums)
        for part in range(row_chunk // 64):
            scores = score_ref[buffer, pl.ds(row + part * 64, 64), :]
            for m in range(pos_count):
                bent = jnp.tanh(scores - pos[m])
                sums[2 * m] = sums[2 * m] + fold_rows(bent)
                sums[2 * m + 1] = sums[2 * m + 1] + fold_rows(bent * bent)
        return tuple(sums)

    chunks = total // row_chunk
    nothing = (jnp.zeros((8, 128), jnp.float32),) * pair
    zero = (jnp.zeros((8, lane_block), jnp.float32),) * (2 * pos_count)

    def split(picked):
        wide = jnp.concatenate(picked, axis=1)
        return tuple(wide[m : m + 1, :] for m in range(pos_count))

    def finish(start, buffer, pos, sums):
        ranks = []
        slopes = []
        for m in range(pos_count):
            ranks.append(0.5 + 0.5 * (total + jnp.sum(sums[2 * m], axis=0, keepdims=True)))
            slopes.append(0.25 * (total - jnp.sum(sums[2 * m + 1], axis=0, keepdims=True)))
        own_ref[:, pl.ds(start, lane_block)] = score_ref[buffer, 0:shard, :]
        factor = 1.0 / (pos_count * total)
        pulls = [-factor / ranks[m] for m in range(pos_count)]
        for m in range(pos_count):
            prank = 1.0
            pulled = 0.0
            for q in range(pos_count):
                if q != m:
                    bent = jnp.tanh(pos[q] - pos[m])
                    prank = prank + 0.5 * (1.0 + bent)
                    pulled = pulled + (pulls[q] - pulls[m]) * (0.25 * (1.0 - bent * bent))
            weight = prank / (ranks[m] * ranks[m]) * (factor / logistic_sharpness)
            extra = pulled / logistic_sharpness - weight * slopes[m]
            stat_ref[m : m + 1, pl.ds(start, lane_block)] = pos[m]
            stat_ref[8 + m : 9 + m, pl.ds(start, lane_block)] = 0.25 * weight
            stat_ref[16 + m : 17 + m, pl.ds(start, lane_block)] = extra

    first = embed_ref[0:lane_block, :]
    picked = lax.fori_loop(
        0, chunks, lambda chunk, have: score_chunk(first, 0, 0, chunk, have), nothing
    )

    def block_step(block, pos):
        start = pl.multiple_of(block * lane_block, lane_block)
        buffer = lax.rem(block, 2)
        following = pl.multiple_of(start + lane_block, lane_block)
        anchors = embed_ref[pl.ds(following, lane_block), :]

        def both(chunk, carry):
            picked, sums = carry
            picked = score_chunk(anchors, following, 1 - buffer, chunk, picked)
            return picked, rank_chunk(pos, buffer, chunk, sums)

        picked, sums = lax.fori_loop(0, chunks, both, (nothing, zero))
        finish(start, buffer, pos, sums)
        return split(picked)

    last = total // lane_block - 1
    pos = lax.fori_loop(0, last, block_step, split(picked))
    sums = lax.fori_loop(
        0, chunks, lambda chunk, have: rank_chunk(pos, last % 2, chunk, have), zero
    )
    finish(last * lane_block, last % 2, pos, sums)

    scores = own_ref[...]
    lane = lax.broadcasted_iota(jnp.int32, (shard, total), 1)
    line = lax.broadcasted_iota(jnp.int32, (shard, total), 0)
    columns = jnp.transpose(
        jnp.concatenate(
            [stat_ref[:, 0:128], target_ref[:, 0:128].astype(jnp.float32)], axis=0
        )
    )[0:shard, :]
    grads = [jnp.zeros((shard, total), jnp.float32) for _ in range(2)]
    for m in range(pos_count):
        bent = jnp.tanh(scores - stat_ref[m : m + 1, :])
        grads[0] = grads[0] + stat_ref[8 + m : 9 + m, :] * (1.0 - bent * bent)
        bent = jnp.tanh(scores - columns[:, m : m + 1])
        grads[1] = grads[1] + columns[:, 8 + m : 9 + m] * (1.0 - bent * bent)
    for m in range(pos_count):
        found = line == target_ref[m : m + 1, :]
        grads[0] = grads[0] + jnp.where(found, stat_ref[16 + m : 17 + m, :], 0.0)
        found = lane == columns[:, 24 + m : 25 + m].astype(jnp.int32)
        grads[1] = grads[1] + jnp.where(found, columns[:, 16 + m : 17 + m], 0.0)
    both = jnp.concatenate(grads, axis=0).astype(jnp.bfloat16)
    product = jnp.dot(both, embed_ref[...], preferred_element_type=jnp.float32)
    out_ref[...] = product[:shard, :] + product[shard:, :]


def body(embed, positives, placement):
    shard, width = embed.shape
    axes = ("row", "col")
    rows = lax.axis_size("row")
    cols = lax.axis_size("col")
    levels = rows // 2
    total = shard * rows * cols
    pos_count = positives.shape[1]

    def swap(array, axis, mask):
        size = lax.axis_size(axis)
        return lax.ppermute(array, axis, [(i, i ^ mask) for i in range(size)])

    tall = jnp.concatenate(
        [embed] + [swap(embed, "row", 2 * d) for d in range(1, levels)], axis=0
    )
    ids = positives.T
    ids = [ids] + [swap(ids, "row", line) for line in range(1, rows)]
    plane = [tall] + [swap(tall, "col", p) for p in range(1, cols)]
    blocks = []
    for part in plane:
        blocks += [part, swap(part, "row", 1)]

    place = jnp.stack([lax.axis_index(axes) * shard, lax.axis_index("col") * shard])
    vmem = pl.BlockSpec(memory_space=pltpu.VMEM)
    return pl.pallas_call(
        functools.partial(kernel, cols, levels, shard, pos_count),
        out_shape=jax.ShapeDtypeStruct((shard, width), jnp.float32),
        in_specs=[pl.BlockSpec(memory_space=pltpu.SMEM), vmem]
        + [vmem] * rows
        + [pl.BlockSpec(memory_space=pl.ANY)] * (2 * cols),
        out_specs=vmem,
        scratch_shapes=[
            pltpu.VMEM((total, width), jnp.bfloat16),
            pltpu.VMEM((2, total, lane_block), jnp.float32),
            pltpu.VMEM((shard, total), jnp.float32),
            pltpu.VMEM((8, total), jnp.int32),
            pltpu.VMEM((24, total), jnp.float32),
            pltpu.SemaphoreType.DMA((rows * cols,)),
        ],
        compiler_params=pltpu.CompilerParams(vmem_limit_bytes=50 * 1024 * 1024),
        cost_estimate=pl.CostEstimate(
            flops=2 * total * total * width,
            bytes_accessed=2 * total * width,
            transcendentals=4 * total * total,
        ),
    )(place.astype(jnp.int32), placement.reshape(-1, 128), *ids, *blocks)


def solution(mesh):
    return jax.shard_map(
        body,
        mesh=mesh,
        in_specs=(P(("row", "col"), None), P("row", None), P()),
        out_specs=P(("row", "col"), None),
        check_vma=False,
    )
```

```python
import functools

import jax
import jax.numpy as jnp
from jax import lax
from jax.experimental import pallas as pl
from jax.experimental.pallas import tpu as pltpu
from jax.sharding import PartitionSpec as P

logistic_sharpness = 0.02
half_scale = 0.5 / logistic_sharpness
masked = -1e30


def fold_rows(values):
    return jnp.sum(values.reshape(values.shape[0] // 8, 8, values.shape[1]), axis=0)


def lookup(table_ref, ids):
    low = ids % 128
    high = ids // 128
    found = jnp.zeros(ids.shape, jnp.int32)
    for line in range(table_ref.shape[0]):
        entries = jnp.broadcast_to(table_ref[line : line + 1, :], ids.shape)
        found = jnp.where(high == line, jnp.take_along_axis(entries, low, axis=1), found)
    return found


def kernel(cols, levels, shard, pos_count, lane_block, layout, *refs):
    place_ref, table_ref = refs[:2]
    ids_refs = refs[2:4]
    pieces = refs[4 : 4 + len(layout)]
    out_ref, embed_ref, score_ref, own_ref, target_ref, stat_ref = refs[4 + len(layout) :]
    total = embed_ref.shape[0]
    me = place_ref[0]
    my_col = place_ref[1]
    pair = lane_block // 128
    row_chunk = min(512, total)

    for piece, slots in zip(pieces, layout):
        for spot, slot in enumerate(slots):
            embed_ref[slot * shard : (slot + 1) * shard, :] = piece[spot * shard : (spot + 1) * shard, :]

    group = cols * shard
    for line in range(2 * levels):
        for begin in range(0, group, 128):
            level = line // 2 * pos_count
            ids = ids_refs[line % 2][level : level + pos_count, begin : begin + 128]
            ids = jnp.concatenate([ids, ids], axis=0)
            found = lookup(table_ref, ids) ^ me
            lane = lax.broadcasted_iota(jnp.int32, found.shape, 1)
            found = jnp.take_along_axis(found, lane ^ (my_col % 128), axis=1)
            start = line * group + (begin ^ (my_col - my_col % 128))
            target_ref[:, pl.ds(pl.multiple_of(start, 128), 128)] = found

    def score_chunk(anchors, start, buffer, chunk, picked):
        row = pl.multiple_of(chunk * row_chunk, row_chunk)
        scores = half_scale * lax.dot_general(
            embed_ref[pl.ds(row, row_chunk), :],
            anchors,
            (((1,), (1,)), ((), ())),
            preferred_element_type=jnp.float32,
        )
        score_ref[buffer, pl.ds(row, row_chunk), :] = scores
        picked = list(picked)
        for half in range(pair):
            targets = target_ref[:, pl.ds(pl.multiple_of(start + half * 128, 128), 128)]
            near = (targets - row) >> 3
            sub = targets & 7
            for step in range(row_chunk // 8):
                tile = scores[step * 8 : (step + 1) * 8, half * 128 : (half + 1) * 128]
                tile = jnp.take_along_axis(tile, sub, axis=0)
                picked[half] = jnp.where(near == step, tile, picked[half])
        return tuple(picked)

    def rank_chunk(pos, buffer, chunk, sums):
        row = pl.multiple_of(chunk * row_chunk, row_chunk)
        sums = list(sums)
        for half in range(pair):
            for part in range(row_chunk // 32):
                scores = score_ref[buffer, pl.ds(row + part * 32, 32), half * 128 : (half + 1) * 128]
                for m in range(pos_count):
                    at = (half * pos_count + m) * 2
                    bent = jnp.tanh(scores - pos[half][m])
                    sums[at] = sums[at] + fold_rows(bent)
                    sums[at + 1] = sums[at + 1] + fold_rows(bent * bent)
        return tuple(sums)

    chunks = total // row_chunk
    nothing = (jnp.zeros((8, 128), jnp.float32),) * pair
    zero = (jnp.zeros((8, 128), jnp.float32),) * (2 * pos_count * pair)

    def split(start, buffer, picked):
        inside = (buffer, pl.ds(start, lane_block), slice(None))
        index = lax.broadcasted_iota(jnp.int32, (lane_block, lane_block), 0)
        lane = lax.broadcasted_iota(jnp.int32, (lane_block, lane_block), 1)
        score_ref[inside] = jnp.where(index == lane, masked, score_ref[inside])
        return tuple(tuple(part[m : m + 1, :] for m in range(pos_count)) for part in picked)

    def finish(start, buffer, pos, sums):
        factor = 1.0 / (pos_count * total)
        for half in range(pair):
            lanes = pl.ds(pl.multiple_of(start + half * 128, 128), 128)
            spot = pos[half]
            ranks = []
            slopes = []
            for m in range(pos_count):
                at = (half * pos_count + m) * 2
                ranks.append(0.5 + 0.5 * (total + jnp.sum(sums[at], axis=0, keepdims=True)))
                slopes.append(0.25 * (total - jnp.sum(sums[at + 1], axis=0, keepdims=True)))
            own_ref[:, lanes] = score_ref[buffer, 0:shard, half * 128 : (half + 1) * 128]
            pulls = [-factor / ranks[m] for m in range(pos_count)]
            for m in range(pos_count):
                prank = 1.0
                pulled = 0.0
                for q in range(pos_count):
                    if q != m:
                        bent = jnp.tanh(spot[q] - spot[m])
                        prank = prank + 0.5 * (1.0 + bent)
                        pulled = pulled + (pulls[q] - pulls[m]) * (0.25 * (1.0 - bent * bent))
                weight = prank / (ranks[m] * ranks[m]) * (factor / logistic_sharpness)
                extra = pulled / logistic_sharpness - weight * slopes[m]
                stat_ref[m : m + 1, lanes] = spot[m]
                stat_ref[8 + m : 9 + m, lanes] = 0.25 * weight
                stat_ref[16 + m : 17 + m, lanes] = extra

    first = embed_ref[0:lane_block, :]
    picked = lax.fori_loop(
        0, chunks, lambda chunk, have: score_chunk(first, 0, 0, chunk, have), nothing
    )

    def block_step(block, pos):
        start = pl.multiple_of(block * lane_block, lane_block)
        buffer = lax.rem(block, 2)
        following = pl.multiple_of(start + lane_block, lane_block)
        anchors = embed_ref[pl.ds(following, lane_block), :]

        def both(chunk, carry):
            picked, sums = carry
            picked = score_chunk(anchors, following, 1 - buffer, chunk, picked)
            return picked, rank_chunk(pos, buffer, chunk, sums)

        picked, sums = lax.fori_loop(0, chunks, both, (nothing, zero))
        finish(start, buffer, pos, sums)
        return split(following, 1 - buffer, picked)

    last = total // lane_block - 1
    pos = lax.fori_loop(0, last, block_step, split(0, 0, picked))
    sums = lax.fori_loop(
        0, chunks, lambda chunk, have: rank_chunk(pos, last % 2, chunk, have), zero
    )
    finish(last * lane_block, last % 2, pos, sums)

    scores = own_ref[...]
    lane = lax.broadcasted_iota(jnp.int32, (shard, total), 1)
    line = lax.broadcasted_iota(jnp.int32, (shard, total), 0)
    columns = jnp.transpose(
        jnp.concatenate(
            [stat_ref[:, 0:128], target_ref[:, 0:128].astype(jnp.float32)], axis=0
        )
    )[0:shard, :]
    grads = [jnp.zeros((shard, total), jnp.float32) for _ in range(2)]
    for m in range(pos_count):
        bent = jnp.tanh(scores - stat_ref[m : m + 1, :])
        grads[0] = grads[0] + stat_ref[8 + m : 9 + m, :] * (1.0 - bent * bent)
        bent = jnp.tanh(scores - columns[:, m : m + 1])
        grads[1] = grads[1] + columns[:, 8 + m : 9 + m] * (1.0 - bent * bent)
    for m in range(pos_count):
        found = line == target_ref[m : m + 1, :]
        grads[0] = grads[0] + jnp.where(found, stat_ref[16 + m : 17 + m, :], 0.0)
        found = lane == columns[:, 24 + m : 25 + m].astype(jnp.int32)
        grads[1] = grads[1] + jnp.where(found, columns[:, 16 + m : 17 + m], 0.0)
    both = jnp.concatenate(grads, axis=0).astype(jnp.bfloat16)
    product = jnp.dot(both, embed_ref[...], preferred_element_type=jnp.float32)
    out_ref[...] = product[:shard, :] + product[shard:, :]


def body(embed, positives, placement):
    shard, width = embed.shape
    axes = ("row", "col")
    rows = lax.axis_size("row")
    cols = lax.axis_size("col")
    levels = rows // 2
    total = shard * rows * cols
    pos_count = positives.shape[1]
    lane_block = 256 if total <= 4096 else 128

    def swap(array, axis, mask):
        size = lax.axis_size(axis)
        return lax.ppermute(array, axis, [(i, i ^ mask) for i in range(size)])

    tall = jnp.concatenate(
        [embed] + [swap(embed, "row", 2 * d) for d in range(1, levels)], axis=0
    )
    ids = positives.T
    ids = jnp.concatenate([ids] + [swap(ids, "row", 2 * d) for d in range(1, levels)], axis=0)
    tall, ids = lax.optimization_barrier((tall, ids))

    half = levels // 2 * shard
    plane = {0: [tall]}
    for p in range(1, cols):
        low, high = p & -p, 1 << (p.bit_length() - 1)
        if low == high:
            plane[p] = [swap(tall, "col", p)]
        else:
            first, second = plane[p ^ low], plane[p ^ high]
            first = first[0][:half] if len(first) == 1 else first[0]
            second = second[0][half:] if len(second) == 1 else second[1]
            plane[p] = [swap(first, "col", low), swap(second, "col", high)]

    pieces = []
    layout = []
    for p in range(cols):
        level = 0
        for part in plane[p]:
            count = part.shape[0] // shard
            for c in range(2):
                pieces.append(part if c == 0 else swap(part, "row", 1))
                layout.append([((level + d) * 2 + c) * cols + p for d in range(count)])
            level += count

    place = jnp.stack([lax.axis_index(axes) * shard, lax.axis_index("col") * shard])
    vmem = pl.BlockSpec(memory_space=pltpu.VMEM)
    return pl.pallas_call(
        functools.partial(kernel, cols, levels, shard, pos_count, lane_block, layout),
        out_shape=jax.ShapeDtypeStruct((shard, width), jnp.float32),
        in_specs=[pl.BlockSpec(memory_space=pltpu.SMEM)] + [vmem] * (3 + len(pieces)),
        out_specs=vmem,
        scratch_shapes=[
            pltpu.VMEM((total, width), jnp.bfloat16),
            pltpu.VMEM((2, total, lane_block), jnp.float32),
            pltpu.VMEM((shard, total), jnp.float32),
            pltpu.VMEM((8, total), jnp.int32),
            pltpu.VMEM((24, total), jnp.float32),
        ],
        compiler_params=pltpu.CompilerParams(vmem_limit_bytes=4 * total * width + 8 * total * lane_block + (8 << 20)),
        cost_estimate=pl.CostEstimate(
            flops=2 * total * total * width,
            bytes_accessed=2 * total * width,
            transcendentals=4 * total * total,
        ),
    )(
        place.astype(jnp.int32),
        placement.reshape(-1, 128),
        ids,
        swap(ids, "row", 1),
        *pieces,
    )


def solution(mesh):
    return jax.shard_map(
        body,
        mesh=mesh,
        in_specs=(P(("row", "col"), None), P("row", None), P()),
        out_specs=P(("row", "col"), None),
        check_vma=False,
    )
```

```python
import functools

import jax
import jax.numpy as jnp
from jax import lax
from jax.experimental import pallas as pl
from jax.experimental.pallas import tpu as pltpu
from jax.sharding import PartitionSpec as P

logistic_sharpness = 0.02
half_scale = 0.5 / logistic_sharpness
masked = -1e30


def fold_rows(values):
    return jnp.sum(values.reshape(values.shape[0] // 8, 8, values.shape[1]), axis=0)


def lookup(table_ref, ids):
    low = ids % 128
    high = ids // 128
    found = jnp.zeros(ids.shape, jnp.int32)
    for line in range(table_ref.shape[0]):
        entries = jnp.broadcast_to(table_ref[line : line + 1, :], ids.shape)
        found = jnp.where(high == line, jnp.take_along_axis(entries, low, axis=1), found)
    return found


def kernel(cols, order, shard, pos_count, lane_block, layout, *refs):
    place_ref, table_ref = refs[:2]
    ids_refs = refs[2:4]
    pieces = refs[4 : 4 + len(layout)]
    out_ref, embed_ref, score_ref, own_ref, target_ref, stat_ref = refs[4 + len(layout) :]
    total = embed_ref.shape[0]
    me = place_ref[0]
    my_col = place_ref[1]
    pair = lane_block // 128
    row_chunk = min(512, total)

    for piece, slots in zip(pieces, layout):
        for spot, slot in enumerate(slots):
            embed_ref[slot * shard : (slot + 1) * shard, :] = piece[spot * shard : (spot + 1) * shard, :]

    group = cols * shard
    for line in range(2 * len(order)):
        for begin in range(0, group, 128):
            level = order.index(line // 2) * pos_count
            ids = ids_refs[line % 2][level : level + pos_count, begin : begin + 128]
            ids = jnp.concatenate([ids, ids], axis=0)
            found = lookup(table_ref, ids) ^ me
            lane = lax.broadcasted_iota(jnp.int32, found.shape, 1)
            found = jnp.take_along_axis(found, lane ^ (my_col % 128), axis=1)
            start = line * group + (begin ^ (my_col - my_col % 128))
            target_ref[:, pl.ds(pl.multiple_of(start, 128), 128)] = found

    def score_chunk(anchors, start, buffer, chunk, picked):
        row = pl.multiple_of(chunk * row_chunk, row_chunk)
        scores = half_scale * lax.dot_general(
            embed_ref[pl.ds(row, row_chunk), :],
            anchors,
            (((1,), (1,)), ((), ())),
            preferred_element_type=jnp.float32,
        )
        score_ref[buffer, pl.ds(row, row_chunk), :] = scores
        picked = list(picked)
        for half in range(pair):
            targets = target_ref[:, pl.ds(pl.multiple_of(start + half * 128, 128), 128)]
            near = (targets - row) >> 3
            sub = targets & 7
            for step in range(row_chunk // 8):
                tile = scores[step * 8 : (step + 1) * 8, half * 128 : (half + 1) * 128]
                tile = jnp.take_along_axis(tile, sub, axis=0)
                picked[half] = jnp.where(near == step, tile, picked[half])
        return tuple(picked)

    def rank_chunk(pos, buffer, chunk, sums):
        row = pl.multiple_of(chunk * row_chunk, row_chunk)
        sums = list(sums)
        for half in range(pair):
            for part in range(row_chunk // 32):
                scores = score_ref[buffer, pl.ds(row + part * 32, 32), half * 128 : (half + 1) * 128]
                for m in range(pos_count):
                    at = (half * pos_count + m) * 2
                    bent = jnp.tanh(scores - pos[half][m])
                    sums[at] = sums[at] + fold_rows(bent)
                    sums[at + 1] = sums[at + 1] + fold_rows(bent * bent)
        return tuple(sums)

    chunks = total // row_chunk
    nothing = (jnp.zeros((8, 128), jnp.float32),) * pair
    zero = (jnp.zeros((8, 128), jnp.float32),) * (2 * pos_count * pair)

    def split(start, buffer, picked):
        inside = (buffer, pl.ds(start, lane_block), slice(None))
        index = lax.broadcasted_iota(jnp.int32, (lane_block, lane_block), 0)
        lane = lax.broadcasted_iota(jnp.int32, (lane_block, lane_block), 1)
        score_ref[inside] = jnp.where(index == lane, masked, score_ref[inside])
        return tuple(tuple(part[m : m + 1, :] for m in range(pos_count)) for part in picked)

    def finish(start, buffer, pos, sums):
        factor = 1.0 / (pos_count * total)
        for half in range(pair):
            lanes = pl.ds(pl.multiple_of(start + half * 128, 128), 128)
            spot = pos[half]
            ranks = []
            slopes = []
            for m in range(pos_count):
                at = (half * pos_count + m) * 2
                ranks.append(0.5 + 0.5 * (total + jnp.sum(sums[at], axis=0, keepdims=True)))
                slopes.append(0.25 * (total - jnp.sum(sums[at + 1], axis=0, keepdims=True)))
            own_ref[:, lanes] = score_ref[buffer, 0:shard, half * 128 : (half + 1) * 128]
            pulls = [-factor / ranks[m] for m in range(pos_count)]
            for m in range(pos_count):
                prank = 1.0
                pulled = 0.0
                for q in range(pos_count):
                    if q != m:
                        bent = jnp.tanh(spot[q] - spot[m])
                        prank = prank + 0.5 * (1.0 + bent)
                        pulled = pulled + (pulls[q] - pulls[m]) * (0.25 * (1.0 - bent * bent))
                weight = prank / (ranks[m] * ranks[m]) * (factor / logistic_sharpness)
                extra = pulled / logistic_sharpness - weight * slopes[m]
                stat_ref[m : m + 1, lanes] = spot[m]
                stat_ref[8 + m : 9 + m, lanes] = 0.25 * weight
                stat_ref[16 + m : 17 + m, lanes] = extra

    first = embed_ref[0:lane_block, :]
    picked = lax.fori_loop(
        0, chunks, lambda chunk, have: score_chunk(first, 0, 0, chunk, have), nothing
    )

    def block_step(block, pos):
        start = pl.multiple_of(block * lane_block, lane_block)
        buffer = lax.rem(block, 2)
        following = pl.multiple_of(start + lane_block, lane_block)
        anchors = embed_ref[pl.ds(following, lane_block), :]

        def both(chunk, carry):
            picked, sums = carry
            picked = score_chunk(anchors, following, 1 - buffer, chunk, picked)
            return picked, rank_chunk(pos, buffer, chunk, sums)

        picked, sums = lax.fori_loop(0, chunks, both, (nothing, zero))
        finish(start, buffer, pos, sums)
        return split(following, 1 - buffer, picked)

    last = total // lane_block - 1
    pos = lax.fori_loop(0, last, block_step, split(0, 0, picked))
    sums = lax.fori_loop(
        0, chunks, lambda chunk, have: rank_chunk(pos, last % 2, chunk, have), zero
    )
    finish(last * lane_block, last % 2, pos, sums)

    scores = own_ref[...]
    lane = lax.broadcasted_iota(jnp.int32, (shard, total), 1)
    line = lax.broadcasted_iota(jnp.int32, (shard, total), 0)
    columns = jnp.transpose(
        jnp.concatenate(
            [stat_ref[:, 0:128], target_ref[:, 0:128].astype(jnp.float32)], axis=0
        )
    )[0:shard, :]
    grads = [jnp.zeros((shard, total), jnp.float32) for _ in range(2)]
    for m in range(pos_count):
        bent = jnp.tanh(scores - stat_ref[m : m + 1, :])
        grads[0] = grads[0] + stat_ref[8 + m : 9 + m, :] * (1.0 - bent * bent)
        bent = jnp.tanh(scores - columns[:, m : m + 1])
        grads[1] = grads[1] + columns[:, 8 + m : 9 + m] * (1.0 - bent * bent)
    for m in range(pos_count):
        found = line == target_ref[m : m + 1, :]
        grads[0] = grads[0] + jnp.where(found, stat_ref[16 + m : 17 + m, :], 0.0)
        found = lane == columns[:, 24 + m : 25 + m].astype(jnp.int32)
        grads[1] = grads[1] + jnp.where(found, columns[:, 16 + m : 17 + m], 0.0)
    both = jnp.concatenate(grads, axis=0).astype(jnp.bfloat16)
    product = jnp.dot(both, embed_ref[...], preferred_element_type=jnp.float32)
    out_ref[...] = product[:shard, :] + product[shard:, :]


def body(embed, positives, placement):
    shard, width = embed.shape
    axes = ("row", "col")
    rows = lax.axis_size("row")
    cols = lax.axis_size("col")
    levels = rows // 2
    total = shard * rows * cols
    pos_count = positives.shape[1]
    lane_block = 256 if total <= 4096 else 128

    def swap(array, axis, mask):
        size = lax.axis_size(axis)
        return lax.ppermute(array, axis, [(i, i ^ mask) for i in range(size)])

    order = [0]
    bits = [1 << b for b in reversed(range(levels.bit_length() - 1))]
    line = [swap(embed, "row", 2 * d) for d in range(1, levels)]

    def spread(ids):
        if bits:
            bit = bits.pop(0)
            order.extend([d ^ bit for d in order])
            return (jnp.concatenate([ids[0], swap(ids[0], "row", 2 * bit)], axis=0),)
        if len(ids) == 1:
            return (ids[0], swap(ids[0], "row", 1))
        return ids

    ids = spread((positives.T,))
    line, ids = lax.optimization_barrier((line, ids))
    tall = jnp.concatenate([embed] + line, axis=0)

    half = levels // 2 * shard
    plane = {0: [tall]}
    other = {}
    fresh = [0]
    for weight in range(1, (cols - 1).bit_count() + 1):
        coming = [p for p in range(1, cols) if p.bit_count() == weight]
        for p in coming:
            low, high = p & -p, 1 << (p.bit_length() - 1)
            if low == high:
                plane[p] = [swap(tall, "col", p)]
            else:
                first, second = plane[p ^ low], plane[p ^ high]
                first = first[0][:half] if len(first) == 1 else first[0]
                second = second[0][half:] if len(second) == 1 else second[1]
                plane[p] = [swap(first, "col", low), swap(second, "col", high)]
        ids = spread(ids)
        ready, ids = lax.optimization_barrier(([plane[p] for p in fresh], ids))
        for p, parts in zip(fresh, ready):
            other[p] = [swap(part, "row", 1) for part in parts]
        fresh = coming
        if weight < (cols - 1).bit_count():
            plane, other, ids = lax.optimization_barrier((plane, other, ids))
    while bits or len(ids) == 1:
        ids = spread(ids)
    for p in fresh:
        other[p] = [swap(part, "row", 1) for part in plane[p]]

    pieces = []
    layout = []
    for p in range(cols):
        for c, parts in enumerate((plane[p], other[p])):
            level = 0
            for part in parts:
                count = part.shape[0] // shard
                pieces.append(part)
                layout.append([((level + d) * 2 + c) * cols + p for d in range(count)])
                level += count

    place = jnp.stack([lax.axis_index(axes) * shard, lax.axis_index("col") * shard])
    vmem = pl.BlockSpec(memory_space=pltpu.VMEM)
    return pl.pallas_call(
        functools.partial(kernel, cols, order, shard, pos_count, lane_block, layout),
        out_shape=jax.ShapeDtypeStruct((shard, width), jnp.float32),
        in_specs=[pl.BlockSpec(memory_space=pltpu.SMEM)] + [vmem] * (3 + len(pieces)),
        out_specs=vmem,
        scratch_shapes=[
            pltpu.VMEM((total, width), jnp.bfloat16),
            pltpu.VMEM((2, total, lane_block), jnp.float32),
            pltpu.VMEM((shard, total), jnp.float32),
            pltpu.VMEM((8, total), jnp.int32),
            pltpu.VMEM((24, total), jnp.float32),
        ],
        compiler_params=pltpu.CompilerParams(vmem_limit_bytes=4 * total * width + 8 * total * lane_block + (8 << 20)),
        cost_estimate=pl.CostEstimate(
            flops=2 * total * total * width,
            bytes_accessed=2 * total * width,
            transcendentals=4 * total * total,
        ),
    )(
        place.astype(jnp.int32),
        placement.reshape(-1, 128),
        *ids,
        *pieces,
    )


def solution(mesh):
    return jax.shard_map(
        body,
        mesh=mesh,
        in_specs=(P(("row", "col"), None), P("row", None), P()),
        out_specs=P(("row", "col"), None),
        check_vma=False,
    )
```

```python
import functools

import jax
import jax.numpy as jnp
from jax import lax
from jax.experimental import pallas as pl
from jax.experimental.pallas import tpu as pltpu
from jax.sharding import PartitionSpec as P

logistic_sharpness = 0.02
half_scale = 0.5 / logistic_sharpness
masked = -1e30


def fold_rows(values):
    return jnp.sum(values.reshape(values.shape[0] // 8, 8, values.shape[1]), axis=0)


def lookup(table_ref, ids):
    low = ids % 128
    high = ids // 128
    found = jnp.zeros(ids.shape, jnp.int32)
    for line in range(table_ref.shape[0]):
        entries = jnp.broadcast_to(table_ref[line : line + 1, :], ids.shape)
        found = jnp.where(high == line, jnp.take_along_axis(entries, low, axis=1), found)
    return found


def kernel(
    order,
    shard,
    pos_count,
    lane_block,
    place_ref,
    table_ref,
    own_ids_ref,
    other_ids_ref,
    own_rows_ref,
    other_rows_ref,
    out_ref,
    embed_ref,
    score_ref,
    own_ref,
    target_ref,
    stat_ref,
):
    total = embed_ref.shape[0]
    me = place_ref[0]
    my_col = place_ref[1] * shard
    cols = own_rows_ref.shape[0]
    ids_refs = (own_ids_ref, other_ids_ref)
    pair = lane_block // 128
    row_chunk = min(512, total)

    for q in range(cols):
        p = q ^ place_ref[1]
        for c, rows_ref in enumerate((own_rows_ref, other_rows_ref)):
            for d in range(len(order)):
                start = ((d * 2 + c) * cols + p) * shard
                embed_ref[pl.ds(pl.multiple_of(start, shard), shard), :] = rows_ref[
                    q, d * shard : (d + 1) * shard, :
                ]

    group = cols * shard
    for line in range(2 * len(order)):
        for begin in range(0, group, 128):
            at = order.index(line // 2) * pos_count
            ids = ids_refs[line % 2][at : at + pos_count, begin : begin + 128]
            ids = jnp.concatenate([ids, ids], axis=0)
            found = lookup(table_ref, ids) ^ me
            lane = lax.broadcasted_iota(jnp.int32, found.shape, 1)
            found = jnp.take_along_axis(found, lane ^ (my_col % 128), axis=1)
            start = line * group + (begin ^ (my_col - my_col % 128))
            target_ref[:, pl.ds(pl.multiple_of(start, 128), 128)] = found

    def score_chunk(anchors, start, buffer, chunk, picked):
        row = pl.multiple_of(chunk * row_chunk, row_chunk)
        scores = half_scale * lax.dot_general(
            embed_ref[pl.ds(row, row_chunk), :],
            anchors,
            (((1,), (1,)), ((), ())),
            preferred_element_type=jnp.float32,
        )
        score_ref[buffer, pl.ds(row, row_chunk), :] = scores
        picked = list(picked)
        for half in range(pair):
            targets = target_ref[:, pl.ds(pl.multiple_of(start + half * 128, 128), 128)]
            near = (targets - row) >> 3
            sub = targets & 7
            for step in range(row_chunk // 8):
                tile = scores[step * 8 : (step + 1) * 8, half * 128 : (half + 1) * 128]
                tile = jnp.take_along_axis(tile, sub, axis=0)
                picked[half] = jnp.where(near == step, tile, picked[half])
        return tuple(picked)

    def rank_chunk(pos, buffer, chunk, sums):
        row = pl.multiple_of(chunk * row_chunk, row_chunk)
        sums = list(sums)
        for half in range(pair):
            for part in range(row_chunk // 32):
                scores = score_ref[buffer, pl.ds(row + part * 32, 32), half * 128 : (half + 1) * 128]
                for m in range(pos_count):
                    at = (half * pos_count + m) * 2
                    bent = jnp.tanh(scores - pos[half][m])
                    sums[at] = sums[at] + fold_rows(bent)
                    sums[at + 1] = sums[at + 1] + fold_rows(bent * bent)
        return tuple(sums)

    chunks = total // row_chunk
    nothing = (jnp.zeros((8, 128), jnp.float32),) * pair
    zero = (jnp.zeros((8, 128), jnp.float32),) * (2 * pos_count * pair)

    def split(start, buffer, picked):
        inside = (buffer, pl.ds(start, lane_block), slice(None))
        index = lax.broadcasted_iota(jnp.int32, (lane_block, lane_block), 0)
        lane = lax.broadcasted_iota(jnp.int32, (lane_block, lane_block), 1)
        score_ref[inside] = jnp.where(index == lane, masked, score_ref[inside])
        return tuple(tuple(part[m : m + 1, :] for m in range(pos_count)) for part in picked)

    def finish(start, buffer, pos, sums):
        factor = 1.0 / (pos_count * total)
        for half in range(pair):
            lanes = pl.ds(pl.multiple_of(start + half * 128, 128), 128)
            spot = pos[half]
            ranks = []
            slopes = []
            for m in range(pos_count):
                at = (half * pos_count + m) * 2
                ranks.append(0.5 + 0.5 * (total + jnp.sum(sums[at], axis=0, keepdims=True)))
                slopes.append(0.25 * (total - jnp.sum(sums[at + 1], axis=0, keepdims=True)))
            own_ref[:, lanes] = score_ref[buffer, 0:shard, half * 128 : (half + 1) * 128]
            pulls = [-factor / ranks[m] for m in range(pos_count)]
            for m in range(pos_count):
                prank = 1.0
                pulled = 0.0
                for q in range(pos_count):
                    if q != m:
                        bent = jnp.tanh(spot[q] - spot[m])
                        prank = prank + 0.5 * (1.0 + bent)
                        pulled = pulled + (pulls[q] - pulls[m]) * (0.25 * (1.0 - bent * bent))
                weight = prank / (ranks[m] * ranks[m]) * (factor / logistic_sharpness)
                extra = pulled / logistic_sharpness - weight * slopes[m]
                stat_ref[m : m + 1, lanes] = spot[m]
                stat_ref[8 + m : 9 + m, lanes] = 0.25 * weight
                stat_ref[16 + m : 17 + m, lanes] = extra

    first = embed_ref[0:lane_block, :]
    picked = lax.fori_loop(
        0, chunks, lambda chunk, have: score_chunk(first, 0, 0, chunk, have), nothing
    )

    def block_step(block, pos):
        start = pl.multiple_of(block * lane_block, lane_block)
        buffer = lax.rem(block, 2)
        following = pl.multiple_of(start + lane_block, lane_block)
        anchors = embed_ref[pl.ds(following, lane_block), :]

        def both(chunk, carry):
            picked, sums = carry
            picked = score_chunk(anchors, following, 1 - buffer, chunk, picked)
            return picked, rank_chunk(pos, buffer, chunk, sums)

        picked, sums = lax.fori_loop(0, chunks, both, (nothing, zero))
        finish(start, buffer, pos, sums)
        return split(following, 1 - buffer, picked)

    last = total // lane_block - 1
    pos = lax.fori_loop(0, last, block_step, split(0, 0, picked))
    sums = lax.fori_loop(
        0, chunks, lambda chunk, have: rank_chunk(pos, last % 2, chunk, have), zero
    )
    finish(last * lane_block, last % 2, pos, sums)

    scores = own_ref[...]
    lane = lax.broadcasted_iota(jnp.int32, (shard, total), 1)
    line = lax.broadcasted_iota(jnp.int32, (shard, total), 0)
    columns = jnp.transpose(
        jnp.concatenate(
            [stat_ref[:, 0:128], target_ref[:, 0:128].astype(jnp.float32)], axis=0
        )
    )[0:shard, :]
    grads = [jnp.zeros((shard, total), jnp.float32) for _ in range(2)]
    for m in range(pos_count):
        bent = jnp.tanh(scores - stat_ref[m : m + 1, :])
        grads[0] = grads[0] + stat_ref[8 + m : 9 + m, :] * (1.0 - bent * bent)
        bent = jnp.tanh(scores - columns[:, m : m + 1])
        grads[1] = grads[1] + columns[:, 8 + m : 9 + m] * (1.0 - bent * bent)
    for m in range(pos_count):
        found = line == target_ref[m : m + 1, :]
        grads[0] = grads[0] + jnp.where(found, stat_ref[16 + m : 17 + m, :], 0.0)
        found = lane == columns[:, 24 + m : 25 + m].astype(jnp.int32)
        grads[1] = grads[1] + jnp.where(found, columns[:, 16 + m : 17 + m], 0.0)
    both = jnp.concatenate(grads, axis=0).astype(jnp.bfloat16)
    product = jnp.dot(both, embed_ref[...], preferred_element_type=jnp.float32)
    out_ref[...] = product[:shard, :] + product[shard:, :]


def body(embed, positives, placement):
    shard, width = embed.shape
    axes = ("row", "col")
    rows = lax.axis_size("row")
    cols = lax.axis_size("col")
    levels = rows // 2
    total = shard * rows * cols
    pos_count = positives.shape[1]
    lane_block = 256 if total <= 4096 else 128

    def swap(array, axis, mask):
        size = lax.axis_size(axis)
        return lax.ppermute(array, axis, [(i, i ^ mask) for i in range(size)])

    order = [0]
    bits = [1 << b for b in reversed(range(levels.bit_length() - 1))]
    line = [swap(embed, "row", 2 * d) for d in range(1, levels)]
    ids = positives.T

    def spread(ids):
        bit = bits.pop(0)
        order.extend([d ^ bit for d in order])
        return jnp.concatenate([ids, swap(ids, "row", 2 * bit)], axis=0)

    if bits:
        ids = spread(ids)
    line, ids = lax.optimization_barrier((line, ids))
    tall = jnp.concatenate([embed] + line, axis=0)

    wide = jnp.broadcast_to(tall[None], (cols, *tall.shape))
    wide = lax.all_to_all(wide, "col", 0, 0)
    while bits:
        ids = spread(ids)
    wide, ids = lax.optimization_barrier((wide, ids))
    pieces = [ids, swap(ids, "row", 1), wide, swap(wide, "row", 1)]

    place = jnp.stack([lax.axis_index(axes) * shard, lax.axis_index("col")])
    vmem = pl.BlockSpec(memory_space=pltpu.VMEM)
    return pl.pallas_call(
        functools.partial(kernel, order, shard, pos_count, lane_block),
        out_shape=jax.ShapeDtypeStruct((shard, width), jnp.float32),
        in_specs=[pl.BlockSpec(memory_space=pltpu.SMEM)] + [vmem] * (1 + len(pieces)),
        out_specs=vmem,
        scratch_shapes=[
            pltpu.VMEM((total, width), jnp.bfloat16),
            pltpu.VMEM((2, total, lane_block), jnp.float32),
            pltpu.VMEM((shard, total), jnp.float32),
            pltpu.VMEM((8, total), jnp.int32),
            pltpu.VMEM((24, total), jnp.float32),
        ],
        compiler_params=pltpu.CompilerParams(vmem_limit_bytes=4 * total * width + 8 * total * lane_block + (16 << 20)),
        cost_estimate=pl.CostEstimate(
            flops=2 * total * total * width,
            bytes_accessed=2 * total * width,
            transcendentals=4 * total * total,
        ),
    )(
        place.astype(jnp.int32),
        placement.reshape(-1, 128),
        *pieces,
    )


def solution(mesh):
    return jax.shard_map(
        body,
        mesh=mesh,
        in_specs=(P(("row", "col"), None), P("row", None), P()),
        out_specs=P(("row", "col"), None),
        check_vma=False,
    )
```

```python
import functools

import jax
import jax.numpy as jnp
from jax import lax
from jax.experimental import pallas as pl
from jax.experimental.pallas import tpu as pltpu
from jax.sharding import PartitionSpec as P

logistic_sharpness = 0.02
half_scale = 0.5 / logistic_sharpness
masked = -1e30


def fold_rows(values):
    return jnp.sum(values.reshape(values.shape[0] // 8, 8, values.shape[1]), axis=0)


def lookup(table_ref, ids):
    low = ids % 128
    high = ids // 128
    found = jnp.zeros(ids.shape, jnp.int32)
    for line in range(table_ref.shape[0]):
        entries = jnp.broadcast_to(table_ref[line : line + 1, :], ids.shape)
        found = jnp.where(high == line, jnp.take_along_axis(entries, low, axis=1), found)
    return found


def kernel(cols, order, shard, pos_count, lane_block, layout, *refs):
    place_ref, table_ref = refs[:2]
    ids_refs = refs[2:4]
    pieces = refs[4 : 4 + len(layout)]
    out_ref, embed_ref, score_ref, own_ref, target_ref, stat_ref = refs[4 + len(layout) :]
    total = embed_ref.shape[0]
    me = place_ref[0]
    my_col = place_ref[1]
    pair = lane_block // 128
    row_chunk = min(512, total)

    for piece, (level, count, c, p, mirrored) in zip(pieces, layout):
        p = jnp.where(place_ref[2] == c, p, mirrored)
        for d in range(count):
            start = pl.multiple_of((((level + d) * 2 + c) * cols + p) * shard, shard)
            embed_ref[pl.ds(start, shard), :] = piece[d * shard : (d + 1) * shard, :]

    group = cols * shard
    for line in range(2 * len(order)):
        for begin in range(0, group, 128):
            level = order.index(line // 2) * pos_count
            ids = ids_refs[line % 2][level : level + pos_count, begin : begin + 128]
            ids = jnp.concatenate([ids, ids], axis=0)
            found = lookup(table_ref, ids) ^ me
            lane = lax.broadcasted_iota(jnp.int32, found.shape, 1)
            found = jnp.take_along_axis(found, lane ^ (my_col % 128), axis=1)
            start = line * group + (begin ^ (my_col - my_col % 128))
            target_ref[:, pl.ds(pl.multiple_of(start, 128), 128)] = found

    def score_chunk(anchors, start, buffer, chunk, picked):
        row = pl.multiple_of(chunk * row_chunk, row_chunk)
        scores = half_scale * lax.dot_general(
            embed_ref[pl.ds(row, row_chunk), :],
            anchors,
            (((1,), (1,)), ((), ())),
            preferred_element_type=jnp.float32,
        )
        score_ref[buffer, pl.ds(row, row_chunk), :] = scores
        picked = list(picked)
        for half in range(pair):
            targets = target_ref[:, pl.ds(pl.multiple_of(start + half * 128, 128), 128)]
            near = (targets - row) >> 3
            sub = targets & 7
            for step in range(row_chunk // 8):
                tile = scores[step * 8 : (step + 1) * 8, half * 128 : (half + 1) * 128]
                tile = jnp.take_along_axis(tile, sub, axis=0)
                picked[half] = jnp.where(near == step, tile, picked[half])
        return tuple(picked)

    def rank_chunk(pos, buffer, chunk, sums):
        row = pl.multiple_of(chunk * row_chunk, row_chunk)
        sums = list(sums)
        for half in range(pair):
            for part in range(row_chunk // 32):
                scores = score_ref[buffer, pl.ds(row + part * 32, 32), half * 128 : (half + 1) * 128]
                for m in range(pos_count):
                    at = (half * pos_count + m) * 2
                    bent = jnp.tanh(scores - pos[half][m])
                    sums[at] = sums[at] + fold_rows(bent)
                    sums[at + 1] = sums[at + 1] + fold_rows(bent * bent)
        return tuple(sums)

    chunks = total // row_chunk
    nothing = (jnp.zeros((8, 128), jnp.float32),) * pair
    zero = (jnp.zeros((8, 128), jnp.float32),) * (2 * pos_count * pair)

    def split(start, buffer, picked):
        inside = (buffer, pl.ds(start, lane_block), slice(None))
        index = lax.broadcasted_iota(jnp.int32, (lane_block, lane_block), 0)
        lane = lax.broadcasted_iota(jnp.int32, (lane_block, lane_block), 1)
        score_ref[inside] = jnp.where(index == lane, masked, score_ref[inside])
        return tuple(tuple(part[m : m + 1, :] for m in range(pos_count)) for part in picked)

    def finish(start, buffer, pos, sums):
        factor = 1.0 / (pos_count * total)
        for half in range(pair):
            lanes = pl.ds(pl.multiple_of(start + half * 128, 128), 128)
            spot = pos[half]
            ranks = []
            slopes = []
            for m in range(pos_count):
                at = (half * pos_count + m) * 2
                ranks.append(0.5 + 0.5 * (total + jnp.sum(sums[at], axis=0, keepdims=True)))
                slopes.append(0.25 * (total - jnp.sum(sums[at + 1], axis=0, keepdims=True)))
            own_ref[:, lanes] = score_ref[buffer, 0:shard, half * 128 : (half + 1) * 128]
            pulls = [-factor / ranks[m] for m in range(pos_count)]
            for m in range(pos_count):
                prank = 1.0
                pulled = 0.0
                for q in range(pos_count):
                    if q != m:
                        bent = jnp.tanh(spot[q] - spot[m])
                        prank = prank + 0.5 * (1.0 + bent)
                        pulled = pulled + (pulls[q] - pulls[m]) * (0.25 * (1.0 - bent * bent))
                weight = prank / (ranks[m] * ranks[m]) * (factor / logistic_sharpness)
                extra = pulled / logistic_sharpness - weight * slopes[m]
                stat_ref[m : m + 1, lanes] = spot[m]
                stat_ref[8 + m : 9 + m, lanes] = 0.25 * weight
                stat_ref[16 + m : 17 + m, lanes] = extra

    first = embed_ref[0:lane_block, :]
    picked = lax.fori_loop(
        0, chunks, lambda chunk, have: score_chunk(first, 0, 0, chunk, have), nothing
    )

    def block_step(block, pos):
        start = pl.multiple_of(block * lane_block, lane_block)
        buffer = lax.rem(block, 2)
        following = pl.multiple_of(start + lane_block, lane_block)
        anchors = embed_ref[pl.ds(following, lane_block), :]

        def both(chunk, carry):
            picked, sums = carry
            picked = score_chunk(anchors, following, 1 - buffer, chunk, picked)
            return picked, rank_chunk(pos, buffer, chunk, sums)

        picked, sums = lax.fori_loop(0, chunks, both, (nothing, zero))
        finish(start, buffer, pos, sums)
        return split(following, 1 - buffer, picked)

    last = total // lane_block - 1
    pos = lax.fori_loop(0, last, block_step, split(0, 0, picked))
    sums = lax.fori_loop(
        0, chunks, lambda chunk, have: rank_chunk(pos, last % 2, chunk, have), zero
    )
    finish(last * lane_block, last % 2, pos, sums)

    scores = own_ref[...]
    lane = lax.broadcasted_iota(jnp.int32, (shard, total), 1)
    line = lax.broadcasted_iota(jnp.int32, (shard, total), 0)
    columns = jnp.transpose(
        jnp.concatenate(
            [stat_ref[:, 0:128], target_ref[:, 0:128].astype(jnp.float32)], axis=0
        )
    )[0:shard, :]
    grads = [jnp.zeros((shard, total), jnp.float32) for _ in range(2)]
    for m in range(pos_count):
        bent = jnp.tanh(scores - stat_ref[m : m + 1, :])
        grads[0] = grads[0] + stat_ref[8 + m : 9 + m, :] * (1.0 - bent * bent)
        bent = jnp.tanh(scores - columns[:, m : m + 1])
        grads[1] = grads[1] + columns[:, 8 + m : 9 + m] * (1.0 - bent * bent)
    for m in range(pos_count):
        found = line == target_ref[m : m + 1, :]
        grads[0] = grads[0] + jnp.where(found, stat_ref[16 + m : 17 + m, :], 0.0)
        found = lane == columns[:, 24 + m : 25 + m].astype(jnp.int32)
        grads[1] = grads[1] + jnp.where(found, columns[:, 16 + m : 17 + m], 0.0)
    both = jnp.concatenate(grads, axis=0).astype(jnp.bfloat16)
    product = jnp.dot(both, embed_ref[...], preferred_element_type=jnp.float32)
    out_ref[...] = product[:shard, :] + product[shard:, :]


def body(embed, positives, placement):
    shard, width = embed.shape
    axes = ("row", "col")
    rows = lax.axis_size("row")
    cols = lax.axis_size("col")
    levels = rows // 2
    total = shard * rows * cols
    pos_count = positives.shape[1]
    lane_block = 256 if total <= 4096 else 128

    def swap(array, axis, mask):
        size = lax.axis_size(axis)
        return lax.ppermute(array, axis, [(i, i ^ mask) for i in range(size)])

    width_bits = cols.bit_length() - 1
    mirror = [sum(((p >> b) & 1) << (width_bits - 1 - b) for b in range(width_bits)) for p in range(cols)]

    def hop(array, p):
        pairs = []
        for row in range(rows):
            for col in range(cols):
                peer = col ^ (mirror[p] if row % 2 else p)
                pairs.append((row * cols + col, row * cols + peer))
        return lax.ppermute(array, axes, pairs)

    order = [0]
    bits = [1 << b for b in reversed(range(levels.bit_length() - 1))]

    def spread(ids):
        if not bits:
            return ids
        bit = bits.pop(0)
        order.extend([d ^ bit for d in order])
        return jnp.concatenate([ids, swap(ids, "row", 2 * bit)], axis=0)

    line = [swap(embed, "row", 2 * d) for d in range(1, levels)]
    ids = spread(positives.T)
    line, ids = lax.optimization_barrier((line, ids))
    tall = jnp.concatenate([embed] + line, axis=0)

    half = levels // 2 * shard
    plane = {0: [tall]}
    for weight in range(1, width_bits + 1):
        for p in range(cols):
            if p.bit_count() == weight:
                low, high = p & -p, 1 << (p.bit_length() - 1)
                if low == high:
                    plane[p] = [hop(tall, p)]
                    continue
                first, second = plane[p ^ high], plane[p ^ low]
                first = first[0][:half] if len(first) == 1 else first[0]
                second = second[0][half:] if len(second) == 1 else second[1]
                plane[p] = [hop(first, high), hop(second, low)]
    while bits:
        ids = spread(ids)

    far = plane[cols - 1]
    near = {p: plane[p] for p in range(cols - 1)}
    near, far[0], ids = lax.optimization_barrier((near, far[0], ids))
    plane = {**near, cols - 1: far}
    other = {p: [swap(part, "row", 1) for part in plane[p]] for p in range(cols)}
    ids = (ids, swap(ids, "row", 1))

    pieces = []
    layout = []
    for p in range(cols):
        for c, parts in enumerate((plane[p], other[p])):
            level = 0
            for part in parts:
                count = part.shape[0] // shard
                pieces.append(part)
                layout.append((level, count, c, p, mirror[p]))
                level += count

    place = jnp.stack(
        [lax.axis_index(axes) * shard, lax.axis_index("col") * shard, lax.axis_index("row") % 2]
    )
    vmem = pl.BlockSpec(memory_space=pltpu.VMEM)
    return pl.pallas_call(
        functools.partial(kernel, cols, order, shard, pos_count, lane_block, layout),
        out_shape=jax.ShapeDtypeStruct((shard, width), jnp.float32),
        in_specs=[pl.BlockSpec(memory_space=pltpu.SMEM)] + [vmem] * (3 + len(pieces)),
        out_specs=vmem,
        scratch_shapes=[
            pltpu.VMEM((total, width), jnp.bfloat16),
            pltpu.VMEM((2, total, lane_block), jnp.float32),
            pltpu.VMEM((shard, total), jnp.float32),
            pltpu.VMEM((8, total), jnp.int32),
            pltpu.VMEM((24, total), jnp.float32),
        ],
        compiler_params=pltpu.CompilerParams(vmem_limit_bytes=4 * total * width + 8 * total * lane_block + (16 << 20)),
        cost_estimate=pl.CostEstimate(
            flops=2 * total * total * width,
            bytes_accessed=2 * total * width,
            transcendentals=4 * total * total,
        ),
    )(
        place.astype(jnp.int32),
        placement.reshape(-1, 128),
        *ids,
        *pieces,
    )


def solution(mesh):
    return jax.shard_map(
        body,
        mesh=mesh,
        in_specs=(P(("row", "col"), None), P("row", None), P()),
        out_specs=P(("row", "col"), None),
        check_vma=False,
    )
```

```python
import functools

import jax
import jax.numpy as jnp
from jax import lax
from jax.experimental import pallas as pl
from jax.experimental.pallas import tpu as pltpu
from jax.sharding import PartitionSpec as P

logistic_sharpness = 0.02
half_scale = 0.5 / logistic_sharpness
masked = -1e30


def fold_rows(values):
    return jnp.sum(values.reshape(values.shape[0] // 8, 8, values.shape[1]), axis=0)


def lookup(table_ref, ids):
    low = ids % 128
    high = ids // 128
    found = jnp.zeros(ids.shape, jnp.int32)
    for line in range(table_ref.shape[0]):
        entries = jnp.broadcast_to(table_ref[line : line + 1, :], ids.shape)
        found = jnp.where(high == line, jnp.take_along_axis(entries, low, axis=1), found)
    return found


def kernel(cols, order, shard, pos_count, lane_block, layout, *refs):
    place_ref, table_ref = refs[:2]
    ids_refs = refs[2:4]
    pieces = refs[4 : 4 + len(layout)]
    out_ref, embed_ref, score_ref, own_ref, target_ref, stat_ref = refs[4 + len(layout) :]
    total = embed_ref.shape[0]
    me = place_ref[0]
    my_col = place_ref[1]
    pair = lane_block // 128
    row_chunk = min(512, total)

    for piece, slots in zip(pieces, layout):
        for spot, slot in enumerate(slots):
            embed_ref[slot * shard : (slot + 1) * shard, :] = piece[spot * shard : (spot + 1) * shard, :]

    group = cols * shard
    for line in range(2 * len(order)):
        for begin in range(0, group, 128):
            level = order.index(line // 2) * pos_count
            ids = ids_refs[line % 2][level : level + pos_count, begin : begin + 128]
            ids = jnp.concatenate([ids, ids], axis=0)
            found = lookup(table_ref, ids) ^ me
            lane = lax.broadcasted_iota(jnp.int32, found.shape, 1)
            found = jnp.take_along_axis(found, lane ^ (my_col % 128), axis=1)
            start = line * group + (begin ^ (my_col - my_col % 128))
            target_ref[:, pl.ds(pl.multiple_of(start, 128), 128)] = found

    def score_chunk(anchors, start, buffer, chunk, picked):
        row = pl.multiple_of(chunk * row_chunk, row_chunk)
        scores = half_scale * lax.dot_general(
            embed_ref[pl.ds(row, row_chunk), :],
            anchors,
            (((1,), (1,)), ((), ())),
            preferred_element_type=jnp.float32,
        )
        score_ref[buffer, pl.ds(row, row_chunk), :] = scores
        picked = list(picked)
        for half in range(pair):
            lanes = slice(half * 128, (half + 1) * 128)
            for m in range(pos_count):
                target = jnp.broadcast_to(
                    target_ref[m : m + 1, pl.ds(pl.multiple_of(start + half * 128, 128), 128)],
                    (8, 128),
                )
                odd = [(target & (8 << b)) != 0 for b in range(3)]
                near = (target - row) >> 6
                at = half * pos_count + m
                for step in range(row_chunk // 64):
                    tiles = [
                        scores[step * 64 + k * 8 : step * 64 + (k + 1) * 8, lanes] for k in range(8)
                    ]
                    for b in range(3):
                        tiles = [
                            jnp.where(odd[b], tiles[2 * k + 1], tiles[2 * k])
                            for k in range(len(tiles) // 2)
                        ]
                    picked[at] = jnp.where(near == step, tiles[0], picked[at])
        return tuple(picked)

    def rank_chunk(pos, buffer, chunk, sums):
        row = pl.multiple_of(chunk * row_chunk, row_chunk)
        sums = list(sums)
        for half in range(pair):
            for part in range(row_chunk // 32):
                scores = score_ref[buffer, pl.ds(row + part * 32, 32), half * 128 : (half + 1) * 128]
                for m in range(pos_count):
                    at = (half * pos_count + m) * 2
                    bent = jnp.tanh(scores - pos[half][m])
                    sums[at] = sums[at] + fold_rows(bent)
                    sums[at + 1] = sums[at + 1] + fold_rows(bent * bent)
        return tuple(sums)

    chunks = total // row_chunk
    nothing = (jnp.zeros((8, 128), jnp.float32),) * (pair * pos_count)
    zero = (jnp.zeros((8, 128), jnp.float32),) * (2 * pos_count * pair)

    def split(start, buffer, picked):
        inside = (buffer, pl.ds(start, lane_block), slice(None))
        index = lax.broadcasted_iota(jnp.int32, (lane_block, lane_block), 0)
        lane = lax.broadcasted_iota(jnp.int32, (lane_block, lane_block), 1)
        score_ref[inside] = jnp.where(index == lane, masked, score_ref[inside])
        sub = lax.broadcasted_iota(jnp.int32, (8, 128), 0)
        pos = []
        for half in range(pair):
            targets = target_ref[:, pl.ds(pl.multiple_of(start + half * 128, 128), 128)]
            parts = picked[half * pos_count : (half + 1) * pos_count]
            pos.append(
                tuple(
                    jnp.sum(
                        jnp.where(sub == (targets[m : m + 1, :] & 7), parts[m], 0.0),
                        axis=0,
                        keepdims=True,
                    )
                    for m in range(pos_count)
                )
            )
        return tuple(pos)

    def finish(start, buffer, pos, sums):
        factor = 1.0 / (pos_count * total)
        for half in range(pair):
            lanes = pl.ds(pl.multiple_of(start + half * 128, 128), 128)
            spot = pos[half]
            ranks = []
            slopes = []
            for m in range(pos_count):
                at = (half * pos_count + m) * 2
                ranks.append(0.5 + 0.5 * (total + jnp.sum(sums[at], axis=0, keepdims=True)))
                slopes.append(0.25 * (total - jnp.sum(sums[at + 1], axis=0, keepdims=True)))
            own_ref[:, lanes] = score_ref[buffer, 0:shard, half * 128 : (half + 1) * 128]
            pulls = [-factor / ranks[m] for m in range(pos_count)]
            for m in range(pos_count):
                prank = 1.0
                pulled = 0.0
                for q in range(pos_count):
                    if q != m:
                        bent = jnp.tanh(spot[q] - spot[m])
                        prank = prank + 0.5 * (1.0 + bent)
                        pulled = pulled + (pulls[q] - pulls[m]) * (0.25 * (1.0 - bent * bent))
                weight = prank / (ranks[m] * ranks[m]) * (factor / logistic_sharpness)
                extra = pulled / logistic_sharpness - weight * slopes[m]
                stat_ref[m : m + 1, lanes] = spot[m]
                stat_ref[8 + m : 9 + m, lanes] = 0.25 * weight
                stat_ref[16 + m : 17 + m, lanes] = extra

    first = embed_ref[0:lane_block, :]
    picked = lax.fori_loop(
        0, chunks, lambda chunk, have: score_chunk(first, 0, 0, chunk, have), nothing
    )

    def block_step(block, pos):
        start = pl.multiple_of(block * lane_block, lane_block)
        buffer = lax.rem(block, 2)
        following = pl.multiple_of(start + lane_block, lane_block)
        anchors = embed_ref[pl.ds(following, lane_block), :]

        def both(chunk, carry):
            picked, sums = carry
            picked = score_chunk(anchors, following, 1 - buffer, chunk, picked)
            return picked, rank_chunk(pos, buffer, chunk, sums)

        picked, sums = lax.fori_loop(0, chunks, both, (nothing, zero))
        finish(start, buffer, pos, sums)
        return split(following, 1 - buffer, picked)

    last = total // lane_block - 1
    pos = lax.fori_loop(0, last, block_step, split(0, 0, picked))
    sums = lax.fori_loop(
        0, chunks, lambda chunk, have: rank_chunk(pos, last % 2, chunk, have), zero
    )
    finish(last * lane_block, last % 2, pos, sums)

    scores = own_ref[...]
    lane = lax.broadcasted_iota(jnp.int32, (shard, total), 1)
    line = lax.broadcasted_iota(jnp.int32, (shard, total), 0)
    columns = jnp.transpose(
        jnp.concatenate(
            [stat_ref[:, 0:128], target_ref[:, 0:128].astype(jnp.float32)], axis=0
        )
    )[0:shard, :]
    grads = [jnp.zeros((shard, total), jnp.float32) for _ in range(2)]
    for m in range(pos_count):
        bent = jnp.tanh(scores - stat_ref[m : m + 1, :])
        grads[0] = grads[0] + stat_ref[8 + m : 9 + m, :] * (1.0 - bent * bent)
        bent = jnp.tanh(scores - columns[:, m : m + 1])
        grads[1] = grads[1] + columns[:, 8 + m : 9 + m] * (1.0 - bent * bent)
    for m in range(pos_count):
        found = line == target_ref[m : m + 1, :]
        grads[0] = grads[0] + jnp.where(found, stat_ref[16 + m : 17 + m, :], 0.0)
        found = lane == columns[:, 24 + m : 25 + m].astype(jnp.int32)
        grads[1] = grads[1] + jnp.where(found, columns[:, 16 + m : 17 + m], 0.0)
    both = jnp.concatenate(grads, axis=0).astype(jnp.bfloat16)
    product = jnp.dot(both, embed_ref[...], preferred_element_type=jnp.float32)
    out_ref[...] = product[:shard, :] + product[shard:, :]


def body(embed, positives, placement):
    shard, width = embed.shape
    axes = ("row", "col")
    rows = lax.axis_size("row")
    cols = lax.axis_size("col")
    levels = rows // 2
    total = shard * rows * cols
    pos_count = positives.shape[1]
    lane_block = 256 if total <= 4096 else 128

    def swap(array, axis, mask):
        size = lax.axis_size(axis)
        return lax.ppermute(array, axis, [(i, i ^ mask) for i in range(size)])

    def join(parts):
        return parts[0] if len(parts) == 1 else jnp.concatenate(parts, axis=0)

    bits = [1 << b for b in reversed(range(levels.bit_length() - 1))]
    order = [0]
    steps = list(bits)

    def spread(ids):
        if not steps:
            return ids
        bit = steps.pop(0)
        order.extend([d ^ bit for d in order])
        return jnp.concatenate([ids, swap(ids, "row", 2 * bit)], axis=0)

    line = {0: embed}
    for bit in bits:
        line.update({d ^ bit: swap(line[d], "row", 2 * bit) for d in line})
    ids = spread(positives.T)
    line, ids = lax.optimization_barrier((line, ids))
    tall = join([line[d] for d in range(levels)])

    plane = {0: tall}
    plane.update({p: swap(tall, "col", p) for p in range(1, cols)})
    while steps:
        ids = spread(ids)
    plane, ids = lax.optimization_barrier((plane, ids))

    ids = (ids, swap(ids, "row", 1))

    pieces = []
    layout = []
    for p in range(cols):
        for c, part in enumerate((plane[p], swap(plane[p], "row", 1))):
            pieces.append(part)
            layout.append([(d * 2 + c) * cols + p for d in range(levels)])

    place = jnp.stack([lax.axis_index(axes) * shard, lax.axis_index("col") * shard])
    vmem = pl.BlockSpec(memory_space=pltpu.VMEM)
    return pl.pallas_call(
        functools.partial(kernel, cols, order, shard, pos_count, lane_block, layout),
        out_shape=jax.ShapeDtypeStruct((shard, width), jnp.float32),
        in_specs=[pl.BlockSpec(memory_space=pltpu.SMEM)] + [vmem] * (3 + len(pieces)),
        out_specs=vmem,
        scratch_shapes=[
            pltpu.VMEM((total, width), jnp.bfloat16),
            pltpu.VMEM((2, total, lane_block), jnp.float32),
            pltpu.VMEM((shard, total), jnp.float32),
            pltpu.VMEM((8, total), jnp.int32),
            pltpu.VMEM((24, total), jnp.float32),
        ],
        compiler_params=pltpu.CompilerParams(vmem_limit_bytes=4 * total * width + 8 * total * lane_block + (16 << 20)),
        cost_estimate=pl.CostEstimate(
            flops=2 * total * total * width,
            bytes_accessed=2 * total * width,
            transcendentals=4 * total * total,
        ),
    )(
        place.astype(jnp.int32),
        placement.reshape(-1, 128),
        *ids,
        *pieces,
    )


def solution(mesh):
    return jax.shard_map(
        body,
        mesh=mesh,
        in_specs=(P(("row", "col"), None), P("row", None), P()),
        out_specs=P(("row", "col"), None),
        check_vma=False,
    )
```

```python
import functools

import jax
import jax.numpy as jnp
from jax import lax
from jax.experimental import pallas as pl
from jax.experimental.pallas import tpu as pltpu
from jax.sharding import PartitionSpec as P

logistic_sharpness = 0.02
half_scale = 0.5 / logistic_sharpness
masked = -1e30


def fold_rows(values):
    return jnp.sum(values.reshape(values.shape[0] // 8, 8, values.shape[1]), axis=0)


def lookup(table_ref, ids):
    low = ids % 128
    high = ids // 128
    found = jnp.zeros(ids.shape, jnp.int32)
    for line in range(table_ref.shape[0]):
        entries = jnp.broadcast_to(table_ref[line : line + 1, :], ids.shape)
        found = jnp.where(high == line, jnp.take_along_axis(entries, low, axis=1), found)
    return found


def kernel(cols, order, shard, pos_count, lane_block, layout, *refs):
    place_ref, table_ref = refs[:2]
    ids_refs = refs[2:4]
    pieces = refs[4 : 4 + len(layout)]
    out_ref, embed_ref, score_ref, own_ref, target_ref, stat_ref = refs[4 + len(layout) :]
    total = embed_ref.shape[0]
    me = place_ref[0]
    my_col = place_ref[1]
    pair = lane_block // 128
    row_chunk = min(1024, total)

    for piece, slots in zip(pieces, layout):
        for spot, slot in enumerate(slots):
            embed_ref[slot * shard : (slot + 1) * shard, :] = piece[spot * shard : (spot + 1) * shard, :]

    group = cols * shard
    for line in range(2 * len(order)):
        for begin in range(0, group, 128):
            level = order.index(line // 2) * pos_count
            ids = ids_refs[line % 2][level : level + pos_count, begin : begin + 128]
            ids = jnp.concatenate([ids, ids], axis=0)
            found = lookup(table_ref, ids) ^ me
            lane = lax.broadcasted_iota(jnp.int32, found.shape, 1)
            found = jnp.take_along_axis(found, lane ^ (my_col % 128), axis=1)
            start = line * group + (begin ^ (my_col - my_col % 128))
            target_ref[:, pl.ds(pl.multiple_of(start, 128), 128)] = found

    def score_chunk(anchors, start, buffer, chunk, picked):
        row = pl.multiple_of(chunk * row_chunk, row_chunk)
        scores = half_scale * lax.dot_general(
            embed_ref[pl.ds(row, row_chunk), :],
            anchors,
            (((1,), (1,)), ((), ())),
            preferred_element_type=jnp.float32,
        )
        score_ref[buffer, pl.ds(row, row_chunk), :] = scores
        picked = list(picked)
        for half in range(pair):
            lanes = slice(half * 128, (half + 1) * 128)
            for m in range(pos_count):
                target = jnp.broadcast_to(
                    target_ref[m : m + 1, pl.ds(pl.multiple_of(start + half * 128, 128), 128)],
                    (8, 128),
                )
                odd = [(target & (8 << b)) != 0 for b in range(3)]
                near = (target - row) >> 6
                at = half * pos_count + m
                for step in range(row_chunk // 64):
                    tiles = [
                        scores[step * 64 + k * 8 : step * 64 + (k + 1) * 8, lanes] for k in range(8)
                    ]
                    for b in range(3):
                        tiles = [
                            jnp.where(odd[b], tiles[2 * k + 1], tiles[2 * k])
                            for k in range(len(tiles) // 2)
                        ]
                    picked[at] = jnp.where(near == step, tiles[0], picked[at])
        return tuple(picked)

    def rank_chunk(pos, buffer, chunk, sums):
        row = pl.multiple_of(chunk * row_chunk, row_chunk)
        sums = list(sums)
        for half in range(pair):
            for part in range(row_chunk // 32):
                scores = score_ref[buffer, pl.ds(row + part * 32, 32), half * 128 : (half + 1) * 128]
                for m in range(pos_count):
                    at = (half * pos_count + m) * 2
                    bent = jnp.tanh(scores - pos[half][m])
                    sums[at] = sums[at] + fold_rows(bent)
                    sums[at + 1] = sums[at + 1] + fold_rows(bent * bent)
        return tuple(sums)

    chunks = total // row_chunk
    nothing = (jnp.zeros((8, 128), jnp.float32),) * (pair * pos_count)
    zero = (jnp.zeros((8, 128), jnp.float32),) * (2 * pos_count * pair)

    def split(start, buffer, picked):
        inside = (buffer, pl.ds(start, lane_block), slice(None))
        index = lax.broadcasted_iota(jnp.int32, (lane_block, lane_block), 0)
        lane = lax.broadcasted_iota(jnp.int32, (lane_block, lane_block), 1)
        score_ref[inside] = jnp.where(index == lane, masked, score_ref[inside])
        sub = lax.broadcasted_iota(jnp.int32, (8, 128), 0)
        pos = []
        for half in range(pair):
            targets = target_ref[:, pl.ds(pl.multiple_of(start + half * 128, 128), 128)]
            parts = picked[half * pos_count : (half + 1) * pos_count]
            pos.append(
                tuple(
                    jnp.sum(
                        jnp.where(sub == (targets[m : m + 1, :] & 7), parts[m], 0.0),
                        axis=0,
                        keepdims=True,
                    )
                    for m in range(pos_count)
                )
            )
        return tuple(pos)

    def finish(start, buffer, pos, sums):
        factor = 1.0 / (pos_count * total)
        for half in range(pair):
            lanes = pl.ds(pl.multiple_of(start + half * 128, 128), 128)
            spot = pos[half]
            ranks = []
            slopes = []
            for m in range(pos_count):
                at = (half * pos_count + m) * 2
                ranks.append(0.5 + 0.5 * (total + jnp.sum(sums[at], axis=0, keepdims=True)))
                slopes.append(0.25 * (total - jnp.sum(sums[at + 1], axis=0, keepdims=True)))
            own_ref[:, lanes] = score_ref[buffer, 0:shard, half * 128 : (half + 1) * 128]
            pulls = [-factor / ranks[m] for m in range(pos_count)]
            for m in range(pos_count):
                prank = 1.0
                pulled = 0.0
                for q in range(pos_count):
                    if q != m:
                        bent = jnp.tanh(spot[q] - spot[m])
                        prank = prank + 0.5 * (1.0 + bent)
                        pulled = pulled + (pulls[q] - pulls[m]) * (0.25 * (1.0 - bent * bent))
                weight = prank / (ranks[m] * ranks[m]) * (factor / logistic_sharpness)
                extra = pulled / logistic_sharpness - weight * slopes[m]
                stat_ref[m : m + 1, lanes] = spot[m]
                stat_ref[8 + m : 9 + m, lanes] = 0.25 * weight
                stat_ref[16 + m : 17 + m, lanes] = extra

    first = embed_ref[0:lane_block, :]
    picked = lax.fori_loop(
        0, chunks, lambda chunk, have: score_chunk(first, 0, 0, chunk, have), nothing
    )

    def block_step(block, pos):
        start = pl.multiple_of(block * lane_block, lane_block)
        buffer = lax.rem(block, 2)
        following = pl.multiple_of(start + lane_block, lane_block)
        anchors = embed_ref[pl.ds(following, lane_block), :]

        def both(chunk, carry):
            picked, sums = carry
            picked = score_chunk(anchors, following, 1 - buffer, chunk, picked)
            return picked, rank_chunk(pos, buffer, chunk, sums)

        picked, sums = lax.fori_loop(0, chunks, both, (nothing, zero))
        finish(start, buffer, pos, sums)
        return split(following, 1 - buffer, picked)

    last = total // lane_block - 1
    pos = lax.fori_loop(0, last, block_step, split(0, 0, picked))
    sums = lax.fori_loop(
        0, chunks, lambda chunk, have: rank_chunk(pos, last % 2, chunk, have), zero
    )
    finish(last * lane_block, last % 2, pos, sums)

    scores = own_ref[...]
    lane = lax.broadcasted_iota(jnp.int32, (shard, total), 1)
    line = lax.broadcasted_iota(jnp.int32, (shard, total), 0)
    columns = jnp.transpose(
        jnp.concatenate(
            [stat_ref[:, 0:128], target_ref[:, 0:128].astype(jnp.float32)], axis=0
        )
    )[0:shard, :]
    grads = [jnp.zeros((shard, total), jnp.float32) for _ in range(2)]
    for m in range(pos_count):
        bent = jnp.tanh(scores - stat_ref[m : m + 1, :])
        grads[0] = grads[0] + stat_ref[8 + m : 9 + m, :] * (1.0 - bent * bent)
        bent = jnp.tanh(scores - columns[:, m : m + 1])
        grads[1] = grads[1] + columns[:, 8 + m : 9 + m] * (1.0 - bent * bent)
    for m in range(pos_count):
        found = line == target_ref[m : m + 1, :]
        grads[0] = grads[0] + jnp.where(found, stat_ref[16 + m : 17 + m, :], 0.0)
        found = lane == columns[:, 24 + m : 25 + m].astype(jnp.int32)
        grads[1] = grads[1] + jnp.where(found, columns[:, 16 + m : 17 + m], 0.0)
    both = jnp.concatenate(grads, axis=0).astype(jnp.bfloat16)
    product = jnp.dot(both, embed_ref[...], preferred_element_type=jnp.float32)
    out_ref[...] = product[:shard, :] + product[shard:, :]


def body(embed, positives, placement):
    shard, width = embed.shape
    axes = ("row", "col")
    rows = lax.axis_size("row")
    cols = lax.axis_size("col")
    levels = rows // 2
    total = shard * rows * cols
    pos_count = positives.shape[1]
    lane_block = 256 if total <= 4096 else 128

    def swap(array, axis, mask):
        size = lax.axis_size(axis)
        return lax.ppermute(array, axis, [(i, i ^ mask) for i in range(size)])

    def join(parts):
        return parts[0] if len(parts) == 1 else jnp.concatenate(parts, axis=0)

    bits = [1 << b for b in reversed(range(levels.bit_length() - 1))]
    order = [0]
    steps = list(bits)

    def spread(ids):
        if not steps:
            return ids
        bit = steps.pop(0)
        order.extend([d ^ bit for d in order])
        return jnp.concatenate([ids, swap(ids, "row", 2 * bit)], axis=0)

    line = [swap(embed, "row", 2 * d) for d in range(1, levels)]
    mine = {0: embed}
    mine.update({p: swap(embed, "col", p) for p in range(1, cols)})
    ids = spread(positives.T)
    line, mine, ids = lax.optimization_barrier((line, mine, ids))
    tall = join(line)

    plane = {0: tall}
    plane.update({p: swap(tall, "col", p) for p in range(1, cols)})
    while steps:
        ids = spread(ids)
    plane, ids = lax.optimization_barrier((plane, ids))

    ids = (ids, swap(ids, "row", 1))
    near = join([mine[p] for p in range(cols)])
    pieces = [near, swap(near, "row", 1)]
    layout = [[c * cols + p for p in range(cols)] for c in range(2)]
    for p in range(cols):
        for c, part in enumerate((plane[p], swap(plane[p], "row", 1))):
            pieces.append(part)
            layout.append([(d * 2 + c) * cols + p for d in range(1, levels)])

    place = jnp.stack([lax.axis_index(axes) * shard, lax.axis_index("col") * shard])
    vmem = pl.BlockSpec(memory_space=pltpu.VMEM)
    return pl.pallas_call(
        functools.partial(kernel, cols, order, shard, pos_count, lane_block, layout),
        out_shape=jax.ShapeDtypeStruct((shard, width), jnp.float32),
        in_specs=[pl.BlockSpec(memory_space=pltpu.SMEM)] + [vmem] * (3 + len(pieces)),
        out_specs=vmem,
        scratch_shapes=[
            pltpu.VMEM((total, width), jnp.bfloat16),
            pltpu.VMEM((2, total, lane_block), jnp.float32),
            pltpu.VMEM((shard, total), jnp.float32),
            pltpu.VMEM((8, total), jnp.int32),
            pltpu.VMEM((24, total), jnp.float32),
        ],
        compiler_params=pltpu.CompilerParams(vmem_limit_bytes=4 * total * width + 8 * total * lane_block + (16 << 20)),
        cost_estimate=pl.CostEstimate(
            flops=2 * total * total * width,
            bytes_accessed=2 * total * width,
            transcendentals=4 * total * total,
        ),
    )(
        place.astype(jnp.int32),
        placement.reshape(-1, 128),
        *ids,
        *pieces,
    )


def solution(mesh):
    return jax.shard_map(
        body,
        mesh=mesh,
        in_specs=(P(("row", "col"), None), P("row", None), P()),
        out_specs=P(("row", "col"), None),
        check_vma=False,
    )
```

```python
import functools

import jax
import jax.numpy as jnp
from jax import lax
from jax.experimental import pallas as pl
from jax.experimental.pallas import tpu as pltpu
from jax.sharding import PartitionSpec as P

logistic_sharpness = 0.02
half_scale = 0.5 / logistic_sharpness
masked = -1e30


def lookup(table_ref, ids):
    low = ids % 128
    high = ids // 128
    found = jnp.zeros(ids.shape, jnp.int32)
    for line in range(table_ref.shape[0]):
        entries = jnp.broadcast_to(table_ref[line : line + 1, :], ids.shape)
        found = jnp.where(high == line, jnp.take_along_axis(entries, low, axis=1), found)
    return found


def kernel(cols, order, shard, pos_count, lane_block, layout, *refs):
    levels = len(order)
    place_ref, table_ref = refs[:2]
    ids_refs = refs[2:4]
    pieces = refs[4 : 4 + len(layout)]
    out_ref, embed_ref, score_ref, own_ref, target_ref, stat_ref = refs[4 + len(layout) :]
    total = embed_ref.shape[0]
    me = place_ref[0]
    my_col = place_ref[1]
    pair = lane_block // 128
    row_chunk = min(1024, total)

    for piece, slots in zip(pieces, layout):
        for spot, slot in enumerate(slots):
            embed_ref[slot * shard : (slot + 1) * shard, :] = piece[spot * shard : (spot + 1) * shard, :]

    group = cols * shard
    for line in range(2 * levels):
        for begin in range(0, group, 128):
            ids_ref = ids_refs[line % 2]
            size = ids_ref.shape[0] // levels
            at = order.index(line // 2) * size
            ids = ids_ref[at : at + size, begin : begin + 128]
            ids = jnp.concatenate([ids] * (8 // size), axis=0)
            found = lookup(table_ref, ids) ^ me
            lane = lax.broadcasted_iota(jnp.int32, found.shape, 1)
            found = jnp.take_along_axis(found, lane ^ (my_col % 128), axis=1)
            start = line * group + (begin ^ (my_col - my_col % 128))
            target_ref[:, pl.ds(pl.multiple_of(start, 128), 128)] = found

    def score_chunk(anchors, start, buffer, chunk, picked):
        row = pl.multiple_of(chunk * row_chunk, row_chunk)
        scores = half_scale * lax.dot_general(
            embed_ref[pl.ds(row, row_chunk), :],
            anchors,
            (((1,), (1,)), ((), ())),
            preferred_element_type=jnp.float32,
        )
        score_ref[buffer, pl.ds(row, row_chunk), :] = scores
        picked = list(picked)
        for half in range(pair):
            lanes = slice(half * 128, (half + 1) * 128)
            for m in range(pos_count):
                target = jnp.broadcast_to(
                    target_ref[m : m + 1, pl.ds(pl.multiple_of(start + half * 128, 128), 128)],
                    (8, 128),
                )
                odd = [(target & (8 << b)) != 0 for b in range(3)]
                near = (target - row) >> 6
                at = half * pos_count + m
                for step in range(row_chunk // 64):
                    tiles = [
                        scores[step * 64 + k * 8 : step * 64 + (k + 1) * 8, lanes] for k in range(8)
                    ]
                    for b in range(3):
                        tiles = [
                            jnp.where(odd[b], tiles[2 * k + 1], tiles[2 * k])
                            for k in range(len(tiles) // 2)
                        ]
                    picked[at] = jnp.where(near == step, tiles[0], picked[at])
        return tuple(picked)

    def rank_chunk(pos, buffer, chunk, sums):
        row = pl.multiple_of(chunk * row_chunk, row_chunk)
        sums = list(sums)
        for half in range(pair):
            for part in range(row_chunk // 32):
                scores = score_ref[buffer, pl.ds(row + part * 32, 32), half * 128 : (half + 1) * 128]
                scores = scores.reshape(4, 8, 128)
                for m in range(pos_count):
                    at = half * pos_count + m
                    bent = jnp.tanh(scores - pos[at][None])
                    sums[2 * at] = sums[2 * at] + jnp.sum(bent, axis=0)
                    sums[2 * at + 1] = sums[2 * at + 1] + jnp.sum(bent * bent, axis=0)
        return tuple(sums)

    def over_chunks(step, have):
        if chunks == 1:
            return step(0, have)
        return lax.fori_loop(0, chunks, step, have)

    chunks = total // row_chunk
    nothing = (jnp.zeros((8, 128), jnp.float32),) * (pair * pos_count)
    zero = (jnp.zeros((8, 128), jnp.float32),) * (2 * pos_count * pair)

    def split(start, buffer, picked):
        inside = (buffer, pl.ds(start, lane_block), slice(None))
        index = lax.broadcasted_iota(jnp.int32, (lane_block, lane_block), 0)
        lane = lax.broadcasted_iota(jnp.int32, (lane_block, lane_block), 1)
        score_ref[inside] = jnp.where(index == lane, masked, score_ref[inside])
        sub = lax.broadcasted_iota(jnp.int32, (8, 128), 0)
        pos = []
        for half in range(pair):
            lanes = pl.ds(pl.multiple_of(start + half * 128, 128), 128)
            own_ref[:, lanes] = score_ref[buffer, 0:shard, half * 128 : (half + 1) * 128]
            for m in range(pos_count):
                hit = sub == (target_ref[m : m + 1, lanes] & 7)
                spot = jnp.where(hit, picked[half * pos_count + m], 0.0)
                spot = jnp.sum(spot, axis=0, keepdims=True)
                stat_ref[m : m + 1, lanes] = spot
                pos.append(jnp.broadcast_to(spot, (8, 128)))
        return tuple(pos)

    def finish(start, sums):
        for half in range(pair):
            lanes = pl.ds(pl.multiple_of(start + half * 128, 128), 128)
            for m in range(pos_count):
                at = (half * pos_count + m) * 2
                stat_ref[8 + m : 9 + m, lanes] = jnp.sum(sums[at], axis=0, keepdims=True)
                stat_ref[16 + m : 17 + m, lanes] = jnp.sum(sums[at + 1], axis=0, keepdims=True)

    first = embed_ref[0:lane_block, :]
    picked = over_chunks(lambda chunk, have: score_chunk(first, 0, 0, chunk, have), nothing)

    def block_step(block, pos):
        start = pl.multiple_of(block * lane_block, lane_block)
        buffer = lax.rem(block, 2)
        following = pl.multiple_of(start + lane_block, lane_block)
        anchors = embed_ref[pl.ds(following, lane_block), :]

        def both(chunk, carry):
            picked, sums = carry
            picked = score_chunk(anchors, following, 1 - buffer, chunk, picked)
            return picked, rank_chunk(pos, buffer, chunk, sums)

        picked, sums = over_chunks(both, (nothing, zero))
        finish(start, sums)
        return split(following, 1 - buffer, picked)

    last = total // lane_block - 1
    pos = lax.fori_loop(0, last, block_step, split(0, 0, picked))
    sums = over_chunks(lambda chunk, have: rank_chunk(pos, last % 2, chunk, have), zero)
    finish(last * lane_block, sums)

    def turned(values, steps):
        return jnp.concatenate([values[steps:], values[:steps]], axis=0)

    spot = stat_ref[0:pos_count, :]
    ranks = 0.5 + 0.5 * (total + stat_ref[8 : 8 + pos_count, :])
    slopes = 0.25 * (total - stat_ref[16 : 16 + pos_count, :])
    factor = 1.0 / (pos_count * total)
    pulls = -factor / ranks
    prank = 1.0
    pulled = 0.0
    for steps in range(1, pos_count):
        bent = jnp.tanh(turned(spot, steps) - spot)
        prank = prank + 0.5 * (1.0 + bent)
        pulled = pulled + (turned(pulls, steps) - pulls) * (0.25 * (1.0 - bent * bent))
    weight = prank / (ranks * ranks) * (factor / logistic_sharpness)
    stat_ref[8 : 8 + pos_count, :] = 0.25 * weight
    stat_ref[16 : 16 + pos_count, :] = pulled / logistic_sharpness - weight * slopes

    scores = own_ref[...]
    lane = lax.broadcasted_iota(jnp.int32, (shard, total), 1)
    line = lax.broadcasted_iota(jnp.int32, (shard, total), 0)
    columns = jnp.transpose(
        jnp.concatenate(
            [stat_ref[:, 0:128], target_ref[:, 0:128].astype(jnp.float32)], axis=0
        )
    )[0:shard, :]
    grads = [jnp.zeros((shard, total), jnp.float32) for _ in range(2)]
    for m in range(pos_count):
        bent = jnp.tanh(scores - stat_ref[m : m + 1, :])
        grads[0] = grads[0] + stat_ref[8 + m : 9 + m, :] * (1.0 - bent * bent)
        bent = jnp.tanh(scores - columns[:, m : m + 1])
        grads[1] = grads[1] + columns[:, 8 + m : 9 + m] * (1.0 - bent * bent)
    for m in range(pos_count):
        found = line == target_ref[m : m + 1, :]
        grads[0] = grads[0] + jnp.where(found, stat_ref[16 + m : 17 + m, :], 0.0)
        found = lane == columns[:, 24 + m : 25 + m].astype(jnp.int32)
        grads[1] = grads[1] + jnp.where(found, columns[:, 16 + m : 17 + m], 0.0)
    both = jnp.concatenate(grads, axis=0).astype(jnp.bfloat16)
    product = jnp.dot(both, embed_ref[...], preferred_element_type=jnp.float32)
    out_ref[...] = product[:shard, :] + product[shard:, :]


def body(embed, positives, placement):
    shard, width = embed.shape
    axes = ("row", "col")
    rows = lax.axis_size("row")
    cols = lax.axis_size("col")
    levels = rows // 2
    total = shard * rows * cols
    pos_count = positives.shape[1]
    lane_block = 256 if total <= 4096 else 128

    def swap(array, axis, mask):
        size = lax.axis_size(axis)
        return lax.ppermute(array, axis, [(i, i ^ mask) for i in range(size)])

    def join(parts):
        return parts[0] if len(parts) == 1 else jnp.concatenate(parts, axis=0)

    order = [0]
    steps = [1 << b for b in reversed(range(levels.bit_length() - 1))]

    def spread(ids):
        if not steps:
            return ids
        bit = steps.pop(0)
        order.extend([d ^ bit for d in order])
        return jnp.concatenate([ids, swap(ids, "row", 2 * bit)], axis=0)

    line = [swap(embed, "row", 2 * d) for d in range(1, levels)]
    near = jnp.concatenate([embed, jnp.zeros(((cols - 1) * shard, width), embed.dtype)], axis=0)
    near = lax.optimization_barrier(near)
    mine = [swap(near[:shard], "col", p) for p in range(1, cols)]
    ids = positives.T
    line, mine, near, ids = lax.optimization_barrier((line, mine, near, ids))
    tall = join(line)

    plane = {0: tall}
    plane.update({p: swap(tall, "col", p) for p in range(1, cols)})
    for p in range(1, cols):
        near = lax.dynamic_update_slice(near, mine[p - 1], (p * shard, 0))
    while steps:
        ids = spread(ids)
    near, tall, ids = lax.optimization_barrier((near, tall, ids))
    other = [swap(near, "row", 1), swap(tall, "row", 1)]

    ids = (ids, swap(ids, "row", 1))
    pieces = [near, other[0]]
    layout = [[c * cols + p for p in range(cols)] for c in range(2)]
    for p in range(cols):
        for c, part in enumerate((plane[p], swap(plane[p], "row", 1) if p else other[1])):
            pieces.append(part)
            layout.append([(d * 2 + c) * cols + p for d in range(1, levels)])

    place = jnp.stack([lax.axis_index(axes) * shard, lax.axis_index("col") * shard])
    vmem = pl.BlockSpec(memory_space=pltpu.VMEM)
    return pl.pallas_call(
        functools.partial(kernel, cols, order, shard, pos_count, lane_block, layout),
        out_shape=jax.ShapeDtypeStruct((shard, width), jnp.float32),
        in_specs=[pl.BlockSpec(memory_space=pltpu.SMEM)] + [vmem] * (3 + len(pieces)),
        out_specs=vmem,
        scratch_shapes=[
            pltpu.VMEM((total, width), jnp.bfloat16),
            pltpu.VMEM((2, total, lane_block), jnp.float32),
            pltpu.VMEM((shard, total), jnp.float32),
            pltpu.VMEM((8, total), jnp.int32),
            pltpu.VMEM((24, total), jnp.float32),
        ],
        compiler_params=pltpu.CompilerParams(vmem_limit_bytes=4 * total * width + 8 * total * lane_block + (16 << 20)),
        cost_estimate=pl.CostEstimate(
            flops=2 * total * total * width,
            bytes_accessed=2 * total * width,
            transcendentals=4 * total * total,
        ),
    )(
        place.astype(jnp.int32),
        placement.reshape(-1, 128),
        *ids,
        *pieces,
    )


def solution(mesh):
    return jax.shard_map(
        body,
        mesh=mesh,
        in_specs=(P(("row", "col"), None), P("row", None), P()),
        out_specs=P(("row", "col"), None),
        check_vma=False,
    )
```

```python
import functools

import jax
import jax.numpy as jnp
from jax import lax
from jax.experimental import pallas as pl
from jax.experimental.pallas import tpu as pltpu
from jax.sharding import PartitionSpec as P

logistic_sharpness = 0.02
half_scale = 0.5 / logistic_sharpness
masked = -1e30


def lookup(table_ref, ids):
    low = ids % 128
    high = ids // 128
    found = jnp.zeros(ids.shape, jnp.int32)
    for line in range(table_ref.shape[0]):
        entries = jnp.broadcast_to(table_ref[line : line + 1, :], ids.shape)
        found = jnp.where(high == line, jnp.take_along_axis(entries, low, axis=1), found)
    return found


def kernel(cols, order, shard, pos_count, lane_block, layout, *refs):
    levels = len(order)
    place_ref, table_ref = refs[:2]
    ids_refs = refs[2:4]
    pieces = refs[4 : 4 + len(layout)]
    out_ref, embed_ref, score_ref, own_ref, target_ref, stat_ref = refs[4 + len(layout) :]
    total = embed_ref.shape[0]
    me = place_ref[0]
    my_col = place_ref[1]
    pair = lane_block // 128
    row_chunk = min(1024, total)

    for piece, slots in zip(pieces, layout):
        for spot, slot in enumerate(slots):
            embed_ref[slot * shard : (slot + 1) * shard, :] = piece[spot * shard : (spot + 1) * shard, :]

    group = cols * shard
    for line in range(2 * levels):
        for begin in range(0, group, 128):
            ids_ref = ids_refs[line % 2]
            size = ids_ref.shape[0] // levels
            at = order.index(line // 2) * size
            ids = ids_ref[at : at + size, begin : begin + 128]
            ids = jnp.concatenate([ids] * (8 // size), axis=0)
            found = lookup(table_ref, ids) ^ me
            lane = lax.broadcasted_iota(jnp.int32, found.shape, 1)
            found = jnp.take_along_axis(found, lane ^ (my_col % 128), axis=1)
            start = line * group + (begin ^ (my_col - my_col % 128))
            target_ref[:, pl.ds(pl.multiple_of(start, 128), 128)] = found

    def score_chunk(anchors, start, buffer, chunk, picked):
        row = pl.multiple_of(chunk * row_chunk, row_chunk)
        scores = half_scale * lax.dot_general(
            embed_ref[pl.ds(row, row_chunk), :],
            anchors,
            (((1,), (1,)), ((), ())),
            preferred_element_type=jnp.float32,
        )
        score_ref[buffer, pl.ds(row, row_chunk), :] = scores
        picked = list(picked)
        for half in range(pair):
            targets = target_ref[:, pl.ds(pl.multiple_of(start + half * 128, 128), 128)]
            near = (targets - row) >> 3
            sub = targets & 7
            for step in range(row_chunk // 8):
                tile = scores[step * 8 : (step + 1) * 8, half * 128 : (half + 1) * 128]
                tile = jnp.take_along_axis(tile, sub, axis=0)
                picked[half] = jnp.where(near == step, tile, picked[half])
        return tuple(picked)

    def rank_chunk(pos, buffer, chunk, sums):
        row = pl.multiple_of(chunk * row_chunk, row_chunk)
        sums = list(sums)
        for half in range(pair):
            for part in range(row_chunk // 32):
                scores = score_ref[buffer, pl.ds(row + part * 32, 32), half * 128 : (half + 1) * 128]
                scores = scores.reshape(4, 8, 128)
                for m in range(pos_count):
                    at = half * pos_count + m
                    bent = jnp.tanh(scores - pos[at][None])
                    sums[2 * at] = sums[2 * at] + jnp.sum(bent, axis=0)
                    sums[2 * at + 1] = sums[2 * at + 1] + jnp.sum(bent * bent, axis=0)
        return tuple(sums)

    def over_chunks(step, have):
        if chunks == 1:
            return step(0, have)
        return lax.fori_loop(0, chunks, step, have)

    chunks = total // row_chunk
    nothing = (jnp.zeros((8, 128), jnp.float32),) * pair
    zero = (jnp.zeros((8, 128), jnp.float32),) * (2 * pos_count * pair)

    def split(start, buffer, picked):
        inside = (buffer, pl.ds(start, lane_block), slice(None))
        index = lax.broadcasted_iota(jnp.int32, (lane_block, lane_block), 0)
        lane = lax.broadcasted_iota(jnp.int32, (lane_block, lane_block), 1)
        score_ref[inside] = jnp.where(index == lane, masked, score_ref[inside])
        pos = []
        for half in range(pair):
            lanes = pl.ds(pl.multiple_of(start + half * 128, 128), 128)
            own_ref[:, lanes] = score_ref[buffer, 0:shard, half * 128 : (half + 1) * 128]
            stat_ref[0:8, lanes] = picked[half]
            for m in range(pos_count):
                pos.append(jnp.broadcast_to(picked[half][m : m + 1, :], (8, 128)))
        return tuple(pos)

    def finish(start, sums):
        for half in range(pair):
            lanes = pl.ds(pl.multiple_of(start + half * 128, 128), 128)
            for m in range(pos_count):
                at = (half * pos_count + m) * 2
                stat_ref[8 + m : 9 + m, lanes] = jnp.sum(sums[at], axis=0, keepdims=True)
                stat_ref[16 + m : 17 + m, lanes] = jnp.sum(sums[at + 1], axis=0, keepdims=True)

    first = embed_ref[0:lane_block, :]
    picked = over_chunks(lambda chunk, have: score_chunk(first, 0, 0, chunk, have), nothing)

    def block_step(block, pos):
        start = pl.multiple_of(block * lane_block, lane_block)
        buffer = lax.rem(block, 2)
        following = pl.multiple_of(start + lane_block, lane_block)
        anchors = embed_ref[pl.ds(following, lane_block), :]

        def both(chunk, carry):
            picked, sums = carry
            picked = score_chunk(anchors, following, 1 - buffer, chunk, picked)
            return picked, rank_chunk(pos, buffer, chunk, sums)

        picked, sums = over_chunks(both, (nothing, zero))
        finish(start, sums)
        return split(following, 1 - buffer, picked)

    last = total // lane_block - 1
    pos = lax.fori_loop(0, last, block_step, split(0, 0, picked))
    sums = over_chunks(lambda chunk, have: rank_chunk(pos, last % 2, chunk, have), zero)
    finish(last * lane_block, sums)

    def turned(values, steps):
        return jnp.concatenate([values[steps:], values[:steps]], axis=0)

    spot = stat_ref[0:pos_count, :]
    ranks = 0.5 + 0.5 * (total + stat_ref[8 : 8 + pos_count, :])
    slopes = 0.25 * (total - stat_ref[16 : 16 + pos_count, :])
    factor = 1.0 / (pos_count * total)
    pulls = -factor / ranks
    prank = 1.0
    pulled = 0.0
    for steps in range(1, pos_count):
        bent = jnp.tanh(turned(spot, steps) - spot)
        prank = prank + 0.5 * (1.0 + bent)
        pulled = pulled + (turned(pulls, steps) - pulls) * (0.25 * (1.0 - bent * bent))
    weight = prank / (ranks * ranks) * (factor / logistic_sharpness)
    stat_ref[8 : 8 + pos_count, :] = 0.25 * weight
    stat_ref[16 : 16 + pos_count, :] = pulled / logistic_sharpness - weight * slopes

    scores = own_ref[...]
    lane = lax.broadcasted_iota(jnp.int32, (shard, total), 1)
    line = lax.broadcasted_iota(jnp.int32, (shard, total), 0)
    columns = jnp.transpose(
        jnp.concatenate(
            [stat_ref[:, 0:128], target_ref[:, 0:128].astype(jnp.float32)], axis=0
        )
    )[0:shard, :]
    grads = [jnp.zeros((shard, total), jnp.float32) for _ in range(2)]
    for m in range(pos_count):
        bent = jnp.tanh(scores - stat_ref[m : m + 1, :])
        grads[0] = grads[0] + stat_ref[8 + m : 9 + m, :] * (1.0 - bent * bent)
        bent = jnp.tanh(scores - columns[:, m : m + 1])
        grads[1] = grads[1] + columns[:, 8 + m : 9 + m] * (1.0 - bent * bent)
    for m in range(pos_count):
        found = line == target_ref[m : m + 1, :]
        grads[0] = grads[0] + jnp.where(found, stat_ref[16 + m : 17 + m, :], 0.0)
        found = lane == columns[:, 24 + m : 25 + m].astype(jnp.int32)
        grads[1] = grads[1] + jnp.where(found, columns[:, 16 + m : 17 + m], 0.0)
    both = jnp.concatenate(grads, axis=0).astype(jnp.bfloat16)
    product = jnp.dot(both, embed_ref[...], preferred_element_type=jnp.float32)
    out_ref[...] = product[:shard, :] + product[shard:, :]


def body(embed, positives, placement):
    shard, width = embed.shape
    axes = ("row", "col")
    rows = lax.axis_size("row")
    cols = lax.axis_size("col")
    levels = rows // 2
    total = shard * rows * cols
    pos_count = positives.shape[1]
    lane_block = 256 if total <= 4096 else 128

    def swap(array, axis, mask):
        size = lax.axis_size(axis)
        return lax.ppermute(array, axis, [(i, i ^ mask) for i in range(size)])

    def join(parts):
        return parts[0] if len(parts) == 1 else jnp.concatenate(parts, axis=0)

    order = [0]
    steps = [1 << b for b in reversed(range(levels.bit_length() - 1))]

    def spread(ids):
        if not steps:
            return ids
        bit = steps.pop(0)
        order.extend([d ^ bit for d in order])
        return jnp.concatenate([ids, swap(ids, "row", 2 * bit)], axis=0)

    line = [swap(embed, "row", 2 * d) for d in range(1, levels)]
    ids = spread(positives.T)
    line, ids = lax.optimization_barrier((line, ids))
    tall = join([embed] + line)

    plane = {p: swap(tall, "col", p) for p in range(1, cols)}
    while steps:
        ids = spread(ids)
    other = {0: swap(tall, "row", 1)}
    ids = (ids, swap(ids, "row", 1))
    ids, plane[cols - 1] = lax.optimization_barrier((ids, plane[cols - 1]))

    plane[0] = tall
    other.update({p: swap(plane[p], "row", 1) for p in range(1, cols)})
    pieces = []
    layout = []
    for p in range(cols):
        for c, part in enumerate((plane[p], other[p])):
            pieces.append(part)
            layout.append([(d * 2 + c) * cols + p for d in range(levels)])

    place = jnp.stack([lax.axis_index(axes) * shard, lax.axis_index("col") * shard])
    vmem = pl.BlockSpec(memory_space=pltpu.VMEM)
    return pl.pallas_call(
        functools.partial(kernel, cols, order, shard, pos_count, lane_block, layout),
        out_shape=jax.ShapeDtypeStruct((shard, width), jnp.float32),
        in_specs=[pl.BlockSpec(memory_space=pltpu.SMEM)] + [vmem] * (3 + len(pieces)),
        out_specs=vmem,
        scratch_shapes=[
            pltpu.VMEM((total, width), jnp.bfloat16),
            pltpu.VMEM((2, total, lane_block), jnp.float32),
            pltpu.VMEM((shard, total), jnp.float32),
            pltpu.VMEM((8, total), jnp.int32),
            pltpu.VMEM((24, total), jnp.float32),
        ],
        compiler_params=pltpu.CompilerParams(vmem_limit_bytes=4 * total * width + 8 * total * lane_block + (16 << 20)),
        cost_estimate=pl.CostEstimate(
            flops=2 * total * total * width,
            bytes_accessed=2 * total * width,
            transcendentals=4 * total * total,
        ),
    )(
        place.astype(jnp.int32),
        placement.reshape(-1, 128),
        *ids,
        *pieces,
    )


def solution(mesh):
    return jax.shard_map(
        body,
        mesh=mesh,
        in_specs=(P(("row", "col"), None), P("row", None), P()),
        out_specs=P(("row", "col"), None),
        check_vma=False,
    )
```

```python
import functools

import jax
import jax.numpy as jnp
from jax import lax
from jax.experimental import pallas as pl
from jax.experimental.pallas import tpu as pltpu
from jax.sharding import PartitionSpec as P

logistic_sharpness = 0.02
half_scale = 0.5 / logistic_sharpness
masked = -1e30


def aligned(start, size):
    if isinstance(start, int):
        return slice(start, start + size)
    return pl.ds(pl.multiple_of(start, size), size)


def lookup(table_ref, ids):
    low = ids % 128
    high = ids // 128
    found = jnp.zeros(ids.shape, jnp.int32)
    for line in range(table_ref.shape[0]):
        entries = jnp.broadcast_to(table_ref[line : line + 1, :], ids.shape)
        found = jnp.where(high == line, jnp.take_along_axis(entries, low, axis=1), found)
    return found


def kernel(cols, order, shard, pos_count, lane_block, layout, *refs):
    levels = len(order)
    place_ref, table_ref = refs[:2]
    ids_refs = refs[2:4]
    pieces = refs[4 : 4 + len(layout)]
    out_ref, embed_ref, score_ref, own_ref, target_ref, stat_ref = refs[4 + len(layout) :]
    total = embed_ref.shape[0]
    me = place_ref[0]
    my_col = place_ref[1]
    pair = lane_block // 128
    row_chunk = min(1024, total)

    for piece, slots in zip(pieces, layout):
        for spot, slot in enumerate(slots):
            embed_ref[slot * shard : (slot + 1) * shard, :] = piece[spot * shard : (spot + 1) * shard, :]

    group = cols * shard
    for line in range(2 * levels):
        for begin in range(0, group, 128):
            ids_ref = ids_refs[line % 2]
            size = ids_ref.shape[0] // levels
            at = order.index(line // 2) * size
            ids = ids_ref[at : at + size, begin : begin + 128]
            ids = jnp.concatenate([ids] * (8 // size), axis=0)
            found = lookup(table_ref, ids) ^ me
            lane = lax.broadcasted_iota(jnp.int32, found.shape, 1)
            found = jnp.take_along_axis(found, lane ^ (my_col % 128), axis=1)
            start = line * group + (begin ^ (my_col - my_col % 128))
            target_ref[:, pl.ds(pl.multiple_of(start, 128), 128)] = found

    def score_chunk(anchors, start, buffer, chunk, picked):
        row = chunk * row_chunk
        scores = half_scale * lax.dot_general(
            embed_ref[aligned(row, row_chunk), :],
            anchors,
            (((1,), (1,)), ((), ())),
            preferred_element_type=jnp.float32,
        )
        score_ref[buffer, aligned(row, row_chunk), :] = scores
        picked = list(picked)
        for half in range(pair):
            targets = target_ref[:, aligned(start + half * 128, 128)]
            near = (targets - row) >> 3
            sub = targets & 7
            for step in range(row_chunk // 8):
                tile = scores[step * 8 : (step + 1) * 8, half * 128 : (half + 1) * 128]
                tile = jnp.take_along_axis(tile, sub, axis=0)
                picked[half] = jnp.where(near == step, tile, picked[half])
        return tuple(picked)

    def rank_chunk(pos, buffer, chunk, sums):
        row = chunk * row_chunk
        sums = list(sums)
        for half in range(pair):
            for part in range(row_chunk // 32):
                scores = score_ref[buffer, aligned(row + part * 32, 32), half * 128 : (half + 1) * 128]
                scores = scores.reshape(4, 8, 128)
                for m in range(pos_count):
                    at = half * pos_count + m
                    bent = jnp.tanh(scores - pos[at][None])
                    sums[2 * at] = sums[2 * at] + jnp.sum(bent, axis=0)
                    sums[2 * at + 1] = sums[2 * at + 1] + jnp.sum(bent * bent, axis=0)
        return tuple(sums)

    def over_chunks(step, have):
        if chunks == 1:
            return step(0, have)
        return lax.fori_loop(0, chunks, step, have)

    chunks = total // row_chunk
    nothing = (jnp.zeros((8, 128), jnp.float32),) * pair
    zero = (jnp.zeros((8, 128), jnp.float32),) * (2 * pos_count * pair)

    def split(start, buffer, picked):
        inside = (buffer, aligned(start, lane_block), slice(None))
        index = lax.broadcasted_iota(jnp.int32, (lane_block, lane_block), 0)
        lane = lax.broadcasted_iota(jnp.int32, (lane_block, lane_block), 1)
        score_ref[inside] = jnp.where(index == lane, masked, score_ref[inside])
        pos = []
        for half in range(pair):
            lanes = aligned(start + half * 128, 128)
            own_ref[:, lanes] = score_ref[buffer, 0:shard, half * 128 : (half + 1) * 128]
            stat_ref[0:8, lanes] = picked[half]
            for m in range(pos_count):
                pos.append(jnp.broadcast_to(picked[half][m : m + 1, :], (8, 128)))
        return tuple(pos)

    def finish(start, sums):
        for half in range(pair):
            lanes = aligned(start + half * 128, 128)
            for m in range(pos_count):
                at = (half * pos_count + m) * 2
                stat_ref[8 + m : 9 + m, lanes] = jnp.sum(sums[at], axis=0, keepdims=True)
                stat_ref[16 + m : 17 + m, lanes] = jnp.sum(sums[at + 1], axis=0, keepdims=True)

    first = embed_ref[0:lane_block, :]
    picked = over_chunks(lambda chunk, have: score_chunk(first, 0, 0, chunk, have), nothing)

    def block_step(block, pos):
        start = block * lane_block
        following = start + lane_block
        buffer = block % 2
        anchors = embed_ref[aligned(following, lane_block), :]

        def both(chunk, carry):
            picked, sums = carry
            picked = score_chunk(anchors, following, 1 - buffer, chunk, picked)
            return picked, rank_chunk(pos, buffer, chunk, sums)

        picked, sums = over_chunks(both, (nothing, zero))
        finish(start, sums)
        return split(following, 1 - buffer, picked)

    last = total // lane_block - 1
    pos = split(0, 0, picked)
    if chunks == 1:
        for block in range(last):
            pos = block_step(block, pos)
    else:
        pos = lax.fori_loop(0, last, block_step, pos)
    sums = over_chunks(lambda chunk, have: rank_chunk(pos, last % 2, chunk, have), zero)
    finish(last * lane_block, sums)

    def turned(values, steps):
        return jnp.concatenate([values[steps:], values[:steps]], axis=0)

    spot = stat_ref[0:pos_count, :]
    ranks = 0.5 + 0.5 * (total + stat_ref[8 : 8 + pos_count, :])
    slopes = 0.25 * (total - stat_ref[16 : 16 + pos_count, :])
    factor = 1.0 / (pos_count * total)
    pulls = -factor / ranks
    prank = 1.0
    pulled = 0.0
    for steps in range(1, pos_count):
        bent = jnp.tanh(turned(spot, steps) - spot)
        prank = prank + 0.5 * (1.0 + bent)
        pulled = pulled + (turned(pulls, steps) - pulls) * (0.25 * (1.0 - bent * bent))
    weight = prank / (ranks * ranks) * (factor / logistic_sharpness)
    stat_ref[8 : 8 + pos_count, :] = 0.25 * weight
    stat_ref[16 : 16 + pos_count, :] = pulled / logistic_sharpness - weight * slopes

    scores = own_ref[...]
    lane = lax.broadcasted_iota(jnp.int32, (shard, total), 1)
    line = lax.broadcasted_iota(jnp.int32, (shard, total), 0)
    columns = jnp.transpose(
        jnp.concatenate(
            [stat_ref[:, 0:128], target_ref[:, 0:128].astype(jnp.float32)], axis=0
        )
    )[0:shard, :]
    grads = [jnp.zeros((shard, total), jnp.float32) for _ in range(2)]
    for m in range(pos_count):
        bent = jnp.tanh(scores - stat_ref[m : m + 1, :])
        grads[0] = grads[0] + stat_ref[8 + m : 9 + m, :] * (1.0 - bent * bent)
        bent = jnp.tanh(scores - columns[:, m : m + 1])
        grads[1] = grads[1] + columns[:, 8 + m : 9 + m] * (1.0 - bent * bent)
    for m in range(pos_count):
        found = line == target_ref[m : m + 1, :]
        grads[0] = grads[0] + jnp.where(found, stat_ref[16 + m : 17 + m, :], 0.0)
        found = lane == columns[:, 24 + m : 25 + m].astype(jnp.int32)
        grads[1] = grads[1] + jnp.where(found, columns[:, 16 + m : 17 + m], 0.0)
    both = jnp.concatenate(grads, axis=0).astype(jnp.bfloat16)
    product = jnp.dot(both, embed_ref[...], preferred_element_type=jnp.float32)
    out_ref[...] = product[:shard, :] + product[shard:, :]


def body(embed, positives, placement):
    shard, width = embed.shape
    axes = ("row", "col")
    rows = lax.axis_size("row")
    cols = lax.axis_size("col")
    levels = rows // 2
    total = shard * rows * cols
    pos_count = positives.shape[1]
    lane_block = 256 if total <= 4096 else 128

    def swap(array, axis, mask):
        size = lax.axis_size(axis)
        return lax.ppermute(array, axis, [(i, i ^ mask) for i in range(size)])

    def join(parts):
        return parts[0] if len(parts) == 1 else jnp.concatenate(parts, axis=0)

    order = [0]
    steps = [1 << b for b in reversed(range(levels.bit_length() - 1))]

    def spread(ids):
        if not steps:
            return ids
        bit = steps.pop(0)
        order.extend([d ^ bit for d in order])
        return jnp.concatenate([ids, swap(ids, "row", 2 * bit)], axis=0)

    line = [swap(embed, "row", 2 * d) for d in range(1, levels)]
    far = cols - 1
    ids = spread(positives.T)
    tall = jnp.concatenate([embed, jnp.zeros(((levels - 1) * shard, width), embed.dtype)], axis=0)
    tall = lax.optimization_barrier(tall)
    early = swap(tall[:shard], "col", far)
    line, ids, early, tall = lax.optimization_barrier((line, ids, early, tall))
    for d in range(1, levels):
        tall = lax.dynamic_update_slice(tall, line[d - 1], (d * shard, 0))

    plane = {0: tall}
    plane.update({p: swap(tall, "col", p) for p in range(1, far)})
    plane[far] = swap(tall[shard:], "col", far)
    while steps:
        ids = spread(ids)
    plane, ids, early = lax.optimization_barrier((plane, ids, early))

    plane[far] = join([early, plane[far]])
    ids = (ids, swap(ids, "row", 1))
    other = {p: swap(plane[p], "row", 1) for p in range(cols)}
    pieces = []
    layout = []
    for p in range(cols):
        for c, part in enumerate((plane[p], other[p])):
            pieces.append(part)
            layout.append([(d * 2 + c) * cols + p for d in range(levels)])

    place = jnp.stack([lax.axis_index(axes) * shard, lax.axis_index("col") * shard])
    vmem = pl.BlockSpec(memory_space=pltpu.VMEM)
    return pl.pallas_call(
        functools.partial(kernel, cols, order, shard, pos_count, lane_block, layout),
        out_shape=jax.ShapeDtypeStruct((shard, width), jnp.float32),
        in_specs=[pl.BlockSpec(memory_space=pltpu.SMEM)] + [vmem] * (3 + len(pieces)),
        out_specs=vmem,
        scratch_shapes=[
            pltpu.VMEM((total, width), jnp.bfloat16),
            pltpu.VMEM((2, total, lane_block), jnp.float32),
            pltpu.VMEM((shard, total), jnp.float32),
            pltpu.VMEM((8, total), jnp.int32),
            pltpu.VMEM((24, total), jnp.float32),
        ],
        compiler_params=pltpu.CompilerParams(vmem_limit_bytes=4 * total * width + 8 * total * lane_block + (16 << 20)),
        cost_estimate=pl.CostEstimate(
            flops=2 * total * total * width,
            bytes_accessed=2 * total * width,
            transcendentals=4 * total * total,
        ),
    )(
        place.astype(jnp.int32),
        placement.reshape(-1, 128),
        *ids,
        *pieces,
    )


def solution(mesh):
    return jax.shard_map(
        body,
        mesh=mesh,
        in_specs=(P(("row", "col"), None), P("row", None), P()),
        out_specs=P(("row", "col"), None),
        check_vma=False,
    )
```

```python
import functools

import jax
import jax.numpy as jnp
from jax import lax
from jax.experimental import pallas as pl
from jax.experimental.pallas import tpu as pltpu
from jax.sharding import PartitionSpec as P

logistic_sharpness = 0.02
half_scale = 0.5 / logistic_sharpness
masked = -1e30


def aligned(start, size):
    if isinstance(start, int):
        return slice(start, start + size)
    return pl.ds(pl.multiple_of(start, size), size)


def lookup(table_ref, ids):
    low = ids % 128
    high = ids // 128
    found = jnp.zeros(ids.shape, jnp.int32)
    for line in range(table_ref.shape[0]):
        entries = jnp.broadcast_to(table_ref[line : line + 1, :], ids.shape)
        found = jnp.where(high == line, jnp.take_along_axis(entries, low, axis=1), found)
    return found


def kernel(cols, order, shard, pos_count, lane_block, layout, *refs):
    levels = len(order)
    place_ref, table_ref = refs[:2]
    ids_refs = refs[2:4]
    pieces = refs[4 : 4 + len(layout)]
    out_ref, embed_ref, score_ref, own_ref, target_ref, stat_ref = refs[4 + len(layout) :]
    total = embed_ref.shape[0]
    me = place_ref[0]
    my_col = place_ref[1]
    pair = lane_block // 128
    row_chunk = min(1024, total)

    for piece, (c, p) in zip(pieces, layout):
        for z in range(levels):
            start = (((z ^ place_ref[2]) * 2 + c) * cols + p) * shard
            embed_ref[pl.ds(pl.multiple_of(start, shard), shard), :] = piece[
                z * shard : (z + 1) * shard, :
            ]

    group = cols * shard
    for line in range(2 * levels):
        for begin in range(0, group, 128):
            ids_ref = ids_refs[line % 2]
            size = ids_ref.shape[0] // levels
            at = order.index(line // 2) * size
            ids = ids_ref[at : at + size, begin : begin + 128]
            ids = jnp.concatenate([ids] * (8 // size), axis=0)
            found = lookup(table_ref, ids) ^ me
            lane = lax.broadcasted_iota(jnp.int32, found.shape, 1)
            found = jnp.take_along_axis(found, lane ^ (my_col % 128), axis=1)
            start = line * group + (begin ^ (my_col - my_col % 128))
            target_ref[:, pl.ds(pl.multiple_of(start, 128), 128)] = found

    def score_chunk(anchors, start, buffer, chunk, picked):
        row = chunk * row_chunk
        scores = half_scale * lax.dot_general(
            embed_ref[aligned(row, row_chunk), :],
            anchors,
            (((1,), (1,)), ((), ())),
            preferred_element_type=jnp.float32,
        )
        score_ref[buffer, aligned(row, row_chunk), :] = scores
        picked = list(picked)
        for half in range(pair):
            targets = target_ref[:, aligned(start + half * 128, 128)]
            near = (targets - row) >> 3
            sub = targets & 7
            for step in range(row_chunk // 8):
                tile = scores[step * 8 : (step + 1) * 8, half * 128 : (half + 1) * 128]
                tile = jnp.take_along_axis(tile, sub, axis=0)
                picked[half] = jnp.where(near == step, tile, picked[half])
        return tuple(picked)

    def rank_chunk(pos, buffer, chunk, sums):
        row = chunk * row_chunk
        sums = list(sums)
        for half in range(pair):
            for part in range(row_chunk // 32):
                scores = score_ref[buffer, aligned(row + part * 32, 32), half * 128 : (half + 1) * 128]
                scores = scores.reshape(4, 8, 128)
                for m in range(pos_count):
                    at = half * pos_count + m
                    bent = jnp.tanh(scores - pos[at][None])
                    sums[2 * at] = sums[2 * at] + jnp.sum(bent, axis=0)
                    sums[2 * at + 1] = sums[2 * at + 1] + jnp.sum(bent * bent, axis=0)
        return tuple(sums)

    def over_chunks(step, have):
        if chunks == 1:
            return step(0, have)
        return lax.fori_loop(0, chunks, step, have)

    chunks = total // row_chunk
    nothing = (jnp.zeros((8, 128), jnp.float32),) * pair
    zero = (jnp.zeros((8, 128), jnp.float32),) * (2 * pos_count * pair)

    def split(start, buffer, picked):
        inside = (buffer, aligned(start, lane_block), slice(None))
        index = lax.broadcasted_iota(jnp.int32, (lane_block, lane_block), 0)
        lane = lax.broadcasted_iota(jnp.int32, (lane_block, lane_block), 1)
        score_ref[inside] = jnp.where(index == lane, masked, score_ref[inside])
        pos = []
        for half in range(pair):
            lanes = aligned(start + half * 128, 128)
            own_ref[:, lanes] = score_ref[buffer, 0:shard, half * 128 : (half + 1) * 128]
            stat_ref[0:8, lanes] = picked[half]
            for m in range(pos_count):
                pos.append(jnp.broadcast_to(picked[half][m : m + 1, :], (8, 128)))
        return tuple(pos)

    def finish(start, sums):
        for half in range(pair):
            lanes = aligned(start + half * 128, 128)
            for m in range(pos_count):
                at = (half * pos_count + m) * 2
                stat_ref[8 + m : 9 + m, lanes] = jnp.sum(sums[at], axis=0, keepdims=True)
                stat_ref[16 + m : 17 + m, lanes] = jnp.sum(sums[at + 1], axis=0, keepdims=True)

    first = embed_ref[0:lane_block, :]
    picked = over_chunks(lambda chunk, have: score_chunk(first, 0, 0, chunk, have), nothing)

    def block_step(block, pos):
        start = block * lane_block
        following = start + lane_block
        buffer = block % 2
        anchors = embed_ref[aligned(following, lane_block), :]

        def both(chunk, carry):
            picked, sums = carry
            picked = score_chunk(anchors, following, 1 - buffer, chunk, picked)
            return picked, rank_chunk(pos, buffer, chunk, sums)

        picked, sums = over_chunks(both, (nothing, zero))
        finish(start, sums)
        return split(following, 1 - buffer, picked)

    last = total // lane_block - 1
    pos = split(0, 0, picked)
    if chunks == 1:
        for block in range(last):
            pos = block_step(block, pos)
    else:
        pos = lax.fori_loop(0, last, block_step, pos)
    sums = over_chunks(lambda chunk, have: rank_chunk(pos, last % 2, chunk, have), zero)
    finish(last * lane_block, sums)

    def turned(values, steps):
        return jnp.concatenate([values[steps:], values[:steps]], axis=0)

    spot = stat_ref[0:pos_count, :]
    ranks = 0.5 + 0.5 * (total + stat_ref[8 : 8 + pos_count, :])
    slopes = 0.25 * (total - stat_ref[16 : 16 + pos_count, :])
    factor = 1.0 / (pos_count * total)
    pulls = -factor / ranks
    prank = 1.0
    pulled = 0.0
    for steps in range(1, pos_count):
        bent = jnp.tanh(turned(spot, steps) - spot)
        prank = prank + 0.5 * (1.0 + bent)
        pulled = pulled + (turned(pulls, steps) - pulls) * (0.25 * (1.0 - bent * bent))
    weight = prank / (ranks * ranks) * (factor / logistic_sharpness)
    stat_ref[8 : 8 + pos_count, :] = 0.25 * weight
    stat_ref[16 : 16 + pos_count, :] = pulled / logistic_sharpness - weight * slopes

    scores = own_ref[...]
    lane = lax.broadcasted_iota(jnp.int32, (shard, total), 1)
    line = lax.broadcasted_iota(jnp.int32, (shard, total), 0)
    columns = jnp.transpose(
        jnp.concatenate(
            [stat_ref[:, 0:128], target_ref[:, 0:128].astype(jnp.float32)], axis=0
        )
    )[0:shard, :]
    grads = [jnp.zeros((shard, total), jnp.float32) for _ in range(2)]
    for m in range(pos_count):
        bent = jnp.tanh(scores - stat_ref[m : m + 1, :])
        grads[0] = grads[0] + stat_ref[8 + m : 9 + m, :] * (1.0 - bent * bent)
        bent = jnp.tanh(scores - columns[:, m : m + 1])
        grads[1] = grads[1] + columns[:, 8 + m : 9 + m] * (1.0 - bent * bent)
    for m in range(pos_count):
        found = line == target_ref[m : m + 1, :]
        grads[0] = grads[0] + jnp.where(found, stat_ref[16 + m : 17 + m, :], 0.0)
        found = lane == columns[:, 24 + m : 25 + m].astype(jnp.int32)
        grads[1] = grads[1] + jnp.where(found, columns[:, 16 + m : 17 + m], 0.0)
    both = jnp.concatenate(grads, axis=0).astype(jnp.bfloat16)
    product = jnp.dot(both, embed_ref[...], preferred_element_type=jnp.float32)
    out_ref[...] = product[:shard, :] + product[shard:, :]


def body(embed, positives, placement):
    shard, width = embed.shape
    axes = ("row", "col")
    rows = lax.axis_size("row")
    cols = lax.axis_size("col")
    levels = rows // 2
    total = shard * rows * cols
    pos_count = positives.shape[1]
    lane_block = 256 if total <= 4096 else 128

    def swap(array, axis, mask):
        size = lax.axis_size(axis)
        return lax.ppermute(array, axis, [(i, i ^ mask) for i in range(size)])

    def join(parts):
        return parts[0] if len(parts) == 1 else jnp.concatenate(parts, axis=0)

    order = [0]
    steps = [1 << b for b in reversed(range(levels.bit_length() - 1))]

    def spread(ids):
        if not steps:
            return ids
        bit = steps.pop(0)
        order.extend([d ^ bit for d in order])
        return jnp.concatenate([ids, swap(ids, "row", 2 * bit)], axis=0)

    lines = [[2 * d + c for d in range(levels)] for c in range(2)]
    ids = spread(positives.T)
    tall = lax.all_gather(embed, "row", axis_index_groups=lines, axis=0, tiled=True)
    tall, ids = lax.optimization_barrier((tall, ids))

    plane = {0: tall}
    plane.update({p: swap(tall, "col", p) for p in range(1, cols)})
    while steps:
        ids = spread(ids)
    plane, ids = lax.optimization_barrier((plane, ids))

    ids = (ids, swap(ids, "row", 1))
    pieces = []
    layout = []
    for p in range(cols):
        for c, part in enumerate((plane[p], swap(plane[p], "row", 1))):
            pieces.append(part)
            layout.append((c, p))

    place = jnp.stack(
        [lax.axis_index(axes) * shard, lax.axis_index("col") * shard, lax.axis_index("row") // 2]
    )
    vmem = pl.BlockSpec(memory_space=pltpu.VMEM)
    return pl.pallas_call(
        functools.partial(kernel, cols, order, shard, pos_count, lane_block, layout),
        out_shape=jax.ShapeDtypeStruct((shard, width), jnp.float32),
        in_specs=[pl.BlockSpec(memory_space=pltpu.SMEM)] + [vmem] * (3 + len(pieces)),
        out_specs=vmem,
        scratch_shapes=[
            pltpu.VMEM((total, width), jnp.bfloat16),
            pltpu.VMEM((2, total, lane_block), jnp.float32),
            pltpu.VMEM((shard, total), jnp.float32),
            pltpu.VMEM((8, total), jnp.int32),
            pltpu.VMEM((24, total), jnp.float32),
        ],
        compiler_params=pltpu.CompilerParams(vmem_limit_bytes=4 * total * width + 8 * total * lane_block + (16 << 20)),
        cost_estimate=pl.CostEstimate(
            flops=2 * total * total * width,
            bytes_accessed=2 * total * width,
            transcendentals=4 * total * total,
        ),
    )(
        place.astype(jnp.int32),
        placement.reshape(-1, 128),
        *ids,
        *pieces,
    )


def solution(mesh):
    return jax.shard_map(
        body,
        mesh=mesh,
        in_specs=(P(("row", "col"), None), P("row", None), P()),
        out_specs=P(("row", "col"), None),
        check_vma=False,
    )
```

```python
import functools

import jax
import jax.numpy as jnp
from jax import lax
from jax.experimental import pallas as pl
from jax.experimental.pallas import tpu as pltpu
from jax.sharding import PartitionSpec as P

logistic_sharpness = 0.02
half_scale = 0.5 / logistic_sharpness
masked = -1e30


def aligned(start, size):
    if isinstance(start, int):
        return slice(start, start + size)
    return pl.ds(pl.multiple_of(start, size), size)


def lookup(table_ref, ids):
    low = ids % 128
    high = ids // 128
    found = jnp.zeros(ids.shape, jnp.int32)
    for line in range(table_ref.shape[0]):
        entries = jnp.broadcast_to(table_ref[line : line + 1, :], ids.shape)
        found = jnp.where(high == line, jnp.take_along_axis(entries, low, axis=1), found)
    return found


def kernel(cols, order, shard, pos_count, lane_block, layout, *refs):
    levels = len(order)
    place_ref, table_ref = refs[:2]
    ids_refs = refs[2:4]
    pieces = refs[4 : 4 + len(layout)]
    out_ref, embed_ref, score_ref, own_ref, target_ref, stat_ref, column_ref = refs[4 + len(layout) :]
    total = embed_ref.shape[0]
    me = place_ref[0]
    my_col = place_ref[1]
    pair = lane_block // 128
    row_chunk = min(1024, total)

    for piece, slots in zip(pieces, layout):
        for spot, slot in enumerate(slots):
            embed_ref[slot * shard : (slot + 1) * shard, :] = piece[spot * shard : (spot + 1) * shard, :]

    group = cols * shard
    for line in range(2 * levels):
        for begin in range(0, group, 128):
            ids_ref = ids_refs[line % 2]
            size = ids_ref.shape[0] // levels
            at = order.index(line // 2) * size
            ids = ids_ref[at : at + size, begin : begin + 128]
            ids = jnp.concatenate([ids] * (8 // size), axis=0)
            found = lookup(table_ref, ids) ^ me
            lane = lax.broadcasted_iota(jnp.int32, found.shape, 1)
            found = jnp.take_along_axis(found, lane ^ (my_col % 128), axis=1)
            start = line * group + (begin ^ (my_col - my_col % 128))
            target_ref[:, pl.ds(pl.multiple_of(start, 128), 128)] = found

    def score_chunk(anchors, start, buffer, chunk, picked):
        row = chunk * row_chunk
        scores = half_scale * lax.dot_general(
            embed_ref[aligned(row, row_chunk), :],
            anchors,
            (((1,), (1,)), ((), ())),
            preferred_element_type=jnp.float32,
        )
        score_ref[buffer, aligned(row, row_chunk), :] = scores
        picked = list(picked)
        for half in range(pair):
            targets = target_ref[:, aligned(start + half * 128, 128)]
            near = (targets - row) >> 3
            sub = targets & 7
            for step in range(row_chunk // 8):
                tile = scores[step * 8 : (step + 1) * 8, half * 128 : (half + 1) * 128]
                tile = jnp.take_along_axis(tile, sub, axis=0)
                picked[half] = jnp.where(near == step, tile, picked[half])
        return tuple(picked)

    def rank_chunk(pos, buffer, chunk, sums):
        row = chunk * row_chunk
        sums = list(sums)
        for half in range(pair):
            for part in range(row_chunk // 32):
                scores = score_ref[buffer, aligned(row + part * 32, 32), half * 128 : (half + 1) * 128]
                scores = scores.reshape(4, 8, 128)
                for m in range(pos_count):
                    at = half * pos_count + m
                    bent = jnp.tanh(scores - pos[at][None])
                    sums[2 * at] = sums[2 * at] + jnp.sum(bent, axis=0)
                    sums[2 * at + 1] = sums[2 * at + 1] + jnp.sum(bent * bent, axis=0)
        return tuple(sums)

    def over_chunks(step, have):
        if chunks == 1:
            return step(0, have)
        return lax.fori_loop(0, chunks, step, have)

    chunks = total // row_chunk
    nothing = (jnp.zeros((8, 128), jnp.float32),) * pair
    zero = (jnp.zeros((8, 128), jnp.float32),) * (2 * pos_count * pair)

    def split(start, buffer, picked):
        inside = (buffer, aligned(start, lane_block), slice(None))
        index = lax.broadcasted_iota(jnp.int32, (lane_block, lane_block), 0)
        lane = lax.broadcasted_iota(jnp.int32, (lane_block, lane_block), 1)
        score_ref[inside] = jnp.where(index == lane, masked, score_ref[inside])
        pos = []
        for half in range(pair):
            lanes = aligned(start + half * 128, 128)
            own_ref[:, lanes] = score_ref[buffer, 0:shard, half * 128 : (half + 1) * 128]
            stat_ref[0:8, lanes] = picked[half]
            for m in range(pos_count):
                pos.append(jnp.broadcast_to(picked[half][m : m + 1, :], (8, 128)))
        return tuple(pos)

    factor = 1.0 / (pos_count * total)

    def turned(values, steps):
        return jnp.concatenate([values[steps:], values[:steps]], axis=0)

    def finish(start, sums):
        for half in range(pair):
            lanes = aligned(start + half * 128, 128)
            for m in range(pos_count):
                at = (half * pos_count + m) * 2
                stat_ref[8 + m : 9 + m, lanes] = jnp.sum(sums[at], axis=0, keepdims=True)
                stat_ref[16 + m : 17 + m, lanes] = jnp.sum(sums[at + 1], axis=0, keepdims=True)
        lanes = aligned(start, lane_block)
        spot = stat_ref[0:pos_count, lanes]
        ranks = 0.5 + 0.5 * (total + stat_ref[8 : 8 + pos_count, lanes])
        slopes = 0.25 * (total - stat_ref[16 : 16 + pos_count, lanes])
        pulls = -factor / ranks
        prank = 1.0
        pulled = 0.0
        for steps in range(1, pos_count):
            bent = jnp.tanh(turned(spot, steps) - spot)
            prank = prank + 0.5 * (1.0 + bent)
            pulled = pulled + (turned(pulls, steps) - pulls) * (0.25 * (1.0 - bent * bent))
        weight = prank / (ranks * ranks) * (factor / logistic_sharpness)
        stat_ref[8 : 8 + pos_count, lanes] = 0.25 * weight
        stat_ref[16 : 16 + pos_count, lanes] = pulled / logistic_sharpness - weight * slopes

    def keep_own():
        rows = [stat_ref[:, 0:128], target_ref[:, 0:128].astype(jnp.float32)]
        column_ref[:, 0:32] = jnp.transpose(jnp.concatenate(rows, axis=0))[0:shard, :]

    def contribute(start, fresh):
        lanes = aligned(start, lane_block)
        scores = own_ref[:, lanes]
        lane = lax.broadcasted_iota(jnp.int32, (shard, lane_block), 1) + start
        line = lax.broadcasted_iota(jnp.int32, (shard, lane_block), 0)
        grads = [jnp.zeros((shard, lane_block), jnp.float32) for _ in range(2)]

        def column(k):
            return column_ref[:, k : k + 1]

        for m in range(pos_count):
            bent = jnp.tanh(scores - stat_ref[m : m + 1, lanes])
            grads[0] = grads[0] + stat_ref[8 + m : 9 + m, lanes] * (1.0 - bent * bent)
            bent = jnp.tanh(scores - column(m))
            grads[1] = grads[1] + column(8 + m) * (1.0 - bent * bent)
        for m in range(pos_count):
            found = line == target_ref[m : m + 1, lanes]
            grads[0] = grads[0] + jnp.where(found, stat_ref[16 + m : 17 + m, lanes], 0.0)
            found = lane == column(24 + m).astype(jnp.int32)
            grads[1] = grads[1] + jnp.where(found, column(16 + m), 0.0)
        both = jnp.concatenate(grads, axis=0).astype(jnp.bfloat16)
        part = jnp.dot(both, embed_ref[lanes, :], preferred_element_type=jnp.float32)
        part = part[:shard, :] + part[shard:, :]
        out_ref[...] = part if fresh else out_ref[...] + part

    first = embed_ref[0:lane_block, :]
    picked = over_chunks(lambda chunk, have: score_chunk(first, 0, 0, chunk, have), nothing)
    last = total // lane_block - 1

    def block_step(block, pos):
        start = block * lane_block
        following = start + lane_block
        buffer = block % 2
        anchors = embed_ref[aligned(following, lane_block), :]

        def both(chunk, carry):
            picked, sums = carry
            picked = score_chunk(anchors, following, 1 - buffer, chunk, picked)
            return picked, rank_chunk(pos, buffer, chunk, sums)

        picked, sums = over_chunks(both, (nothing, zero))
        finish(start, sums)
        pos = split(following, 1 - buffer, picked)
        if isinstance(block, int) and block == 0:
            keep_own()
        contribute(start, isinstance(block, int) and block == 0)
        return pos

    pos = block_step(0, split(0, 0, picked))
    if chunks == 1:
        for block in range(1, last):
            pos = block_step(block, pos)
    else:
        pos = lax.fori_loop(1, last, block_step, pos)
    sums = over_chunks(lambda chunk, have: rank_chunk(pos, last % 2, chunk, have), zero)
    finish(last * lane_block, sums)
    contribute(last * lane_block, False)


def body(embed, positives, placement):
    shard, width = embed.shape
    axes = ("row", "col")
    rows = lax.axis_size("row")
    cols = lax.axis_size("col")
    levels = rows // 2
    total = shard * rows * cols
    pos_count = positives.shape[1]
    lane_block = 256 if total <= 4096 else 128

    def swap(array, axis, mask):
        size = lax.axis_size(axis)
        return lax.ppermute(array, axis, [(i, i ^ mask) for i in range(size)])

    def join(parts):
        return parts[0] if len(parts) == 1 else jnp.concatenate(parts, axis=0)

    order = [0]
    steps = [1 << b for b in reversed(range(levels.bit_length() - 1))]

    def spread(ids):
        if not steps:
            return ids
        bit = steps.pop(0)
        order.extend([d ^ bit for d in order])
        return jnp.concatenate([ids, swap(ids, "row", 2 * bit)], axis=0)

    line = [swap(embed, "row", 2 * d) for d in range(1, levels)]
    ids = spread(positives.T)
    line, ids = lax.optimization_barrier((line, ids))
    tall = join([embed] + line)

    plane = {0: tall}
    plane.update({p: swap(tall, "col", p) for p in range(1, cols)})
    while steps:
        ids = spread(ids)
    plane, ids = lax.optimization_barrier((plane, ids))

    ids = (ids, swap(ids, "row", 1))
    pieces = []
    layout = []
    for p in range(cols):
        for c, part in enumerate((plane[p], swap(plane[p], "row", 1))):
            pieces.append(part)
            layout.append([(d * 2 + c) * cols + p for d in range(levels)])

    place = jnp.stack([lax.axis_index(axes) * shard, lax.axis_index("col") * shard])
    vmem = pl.BlockSpec(memory_space=pltpu.VMEM)
    return pl.pallas_call(
        functools.partial(kernel, cols, order, shard, pos_count, lane_block, layout),
        out_shape=jax.ShapeDtypeStruct((shard, width), jnp.float32),
        in_specs=[pl.BlockSpec(memory_space=pltpu.SMEM)] + [vmem] * (3 + len(pieces)),
        out_specs=vmem,
        scratch_shapes=[
            pltpu.VMEM((total, width), jnp.bfloat16),
            pltpu.VMEM((2, total, lane_block), jnp.float32),
            pltpu.VMEM((shard, total), jnp.float32),
            pltpu.VMEM((8, total), jnp.int32),
            pltpu.VMEM((24, total), jnp.float32),
            pltpu.VMEM((shard, 128), jnp.float32),
        ],
        compiler_params=pltpu.CompilerParams(vmem_limit_bytes=4 * total * width + 8 * total * lane_block + (16 << 20)),
        cost_estimate=pl.CostEstimate(
            flops=2 * total * total * width,
            bytes_accessed=2 * total * width,
            transcendentals=4 * total * total,
        ),
    )(
        place.astype(jnp.int32),
        placement.reshape(-1, 128),
        *ids,
        *pieces,
    )


def solution(mesh):
    return jax.shard_map(
        body,
        mesh=mesh,
        in_specs=(P(("row", "col"), None), P("row", None), P()),
        out_specs=P(("row", "col"), None),
        check_vma=False,
    )
```

```python
import functools

import jax
import jax.numpy as jnp
from jax import lax
from jax.experimental import pallas as pl
from jax.experimental.pallas import tpu as pltpu
from jax.sharding import PartitionSpec as P

logistic_sharpness = 0.02
half_scale = 0.5 / logistic_sharpness
masked = -1e30


def aligned(start, size):
    if isinstance(start, int):
        return slice(start, start + size)
    return pl.ds(pl.multiple_of(start, size), size)


def lookup(table_ref, ids):
    low = ids % 128
    high = ids // 128
    found = jnp.zeros(ids.shape, jnp.int32)
    for line in range(table_ref.shape[0]):
        entries = jnp.broadcast_to(table_ref[line : line + 1, :], ids.shape)
        found = jnp.where(high == line, jnp.take_along_axis(entries, low, axis=1), found)
    return found


def kernel(cols, order, shard, pos_count, lane_block, layout, *refs):
    levels = len(order)
    place_ref, table_ref = refs[:2]
    ids_refs = refs[2:4]
    pieces = refs[4 : 4 + len(layout)]
    out_ref, embed_ref, score_ref, own_ref, target_ref, stat_ref = refs[4 + len(layout) :]
    total = embed_ref.shape[0]
    me = place_ref[0]
    my_col = place_ref[1]
    pair = lane_block // 128
    small = total <= 1024
    row_chunk = min(512, total)

    for piece, slots in zip(pieces, layout):
        for spot, slot in enumerate(slots):
            embed_ref[slot * shard : (slot + 1) * shard, :] = piece[spot * shard : (spot + 1) * shard, :]

    group = cols * shard
    for line in range(2 * levels):
        for begin in range(0, group, 128):
            ids_ref = ids_refs[line % 2]
            size = ids_ref.shape[0] // levels
            at = order.index(line // 2) * size
            ids = ids_ref[at : at + size, begin : begin + 128]
            ids = jnp.concatenate([ids] * (8 // size), axis=0)
            found = lookup(table_ref, ids) ^ me
            lane = lax.broadcasted_iota(jnp.int32, found.shape, 1)
            found = jnp.take_along_axis(found, lane ^ (my_col % 128), axis=1)
            start = line * group + (begin ^ (my_col - my_col % 128))
            target_ref[:, pl.ds(pl.multiple_of(start, 128), 128)] = found

    def score_chunk(anchors, start, buffer, chunk, picked):
        row = chunk * row_chunk
        scores = half_scale * lax.dot_general(
            embed_ref[aligned(row, row_chunk), :],
            anchors,
            (((1,), (1,)), ((), ())),
            preferred_element_type=jnp.float32,
        )
        score_ref[buffer, aligned(row, row_chunk), :] = scores
        picked = list(picked)
        for half in range(pair):
            targets = target_ref[:, aligned(start + half * 128, 128)]
            near = (targets - row) >> 3
            sub = targets & 7
            for step in range(row_chunk // 8):
                tile = scores[step * 8 : (step + 1) * 8, half * 128 : (half + 1) * 128]
                tile = jnp.take_along_axis(tile, sub, axis=0)
                picked[half] = jnp.where(near == step, tile, picked[half])
        return tuple(picked)

    def rank_chunk(pos, buffer, chunk, sums):
        row = chunk * row_chunk
        sums = list(sums)
        for half in range(pair):
            for part in range(row_chunk // 32):
                scores = score_ref[buffer, aligned(row + part * 32, 32), half * 128 : (half + 1) * 128]
                scores = scores.reshape(4, 8, 128)
                for m in range(pos_count):
                    at = half * pos_count + m
                    bent = jnp.tanh(scores - pos[at][None])
                    sums[2 * at] = sums[2 * at] + jnp.sum(bent, axis=0)
                    sums[2 * at + 1] = sums[2 * at + 1] + jnp.sum(bent * bent, axis=0)
        return tuple(sums)

    def over_chunks(step, have):
        if not small:
            return lax.fori_loop(0, chunks, step, have)
        for chunk in range(chunks):
            have = step(chunk, have)
        return have

    chunks = total // row_chunk
    nothing = (jnp.zeros((8, 128), jnp.float32),) * pair
    zero = (jnp.zeros((8, 128), jnp.float32),) * (2 * pos_count * pair)

    def split(start, buffer, picked):
        inside = (buffer, aligned(start, lane_block), slice(None))
        index = lax.broadcasted_iota(jnp.int32, (lane_block, lane_block), 0)
        lane = lax.broadcasted_iota(jnp.int32, (lane_block, lane_block), 1)
        score_ref[inside] = jnp.where(index == lane, masked, score_ref[inside])
        pos = []
        for half in range(pair):
            lanes = aligned(start + half * 128, 128)
            own_ref[:, lanes] = score_ref[buffer, 0:shard, half * 128 : (half + 1) * 128]
            stat_ref[0:8, lanes] = picked[half]
            for m in range(pos_count):
                pos.append(jnp.broadcast_to(picked[half][m : m + 1, :], (8, 128)))
        return tuple(pos)

    def finish(start, sums):
        for half in range(pair):
            lanes = aligned(start + half * 128, 128)
            for m in range(pos_count):
                at = (half * pos_count + m) * 2
                stat_ref[8 + m : 9 + m, lanes] = jnp.sum(sums[at], axis=0, keepdims=True)
                stat_ref[16 + m : 17 + m, lanes] = jnp.sum(sums[at + 1], axis=0, keepdims=True)

    first = embed_ref[0:lane_block, :]
    picked = over_chunks(lambda chunk, have: score_chunk(first, 0, 0, chunk, have), nothing)

    def block_step(block, pos):
        start = block * lane_block
        following = start + lane_block
        buffer = block % 2
        anchors = embed_ref[aligned(following, lane_block), :]

        def both(chunk, carry):
            picked, sums = carry
            picked = score_chunk(anchors, following, 1 - buffer, chunk, picked)
            return picked, rank_chunk(pos, buffer, chunk, sums)

        picked, sums = over_chunks(both, (nothing, zero))
        finish(start, sums)
        return split(following, 1 - buffer, picked)

    last = total // lane_block - 1
    pos = split(0, 0, picked)
    if small:
        for block in range(last):
            pos = block_step(block, pos)
    else:
        pos = lax.fori_loop(0, last, block_step, pos)
    sums = over_chunks(lambda chunk, have: rank_chunk(pos, last % 2, chunk, have), zero)
    finish(last * lane_block, sums)

    def turned(values, steps):
        return jnp.concatenate([values[steps:], values[:steps]], axis=0)

    spot = stat_ref[0:pos_count, :]
    ranks = 0.5 + 0.5 * (total + stat_ref[8 : 8 + pos_count, :])
    slopes = 0.25 * (total - stat_ref[16 : 16 + pos_count, :])
    factor = 1.0 / (pos_count * total)
    pulls = -factor / ranks
    prank = 1.0
    pulled = 0.0
    for steps in range(1, pos_count):
        bent = jnp.tanh(turned(spot, steps) - spot)
        prank = prank + 0.5 * (1.0 + bent)
        pulled = pulled + (turned(pulls, steps) - pulls) * (0.25 * (1.0 - bent * bent))
    weight = prank / (ranks * ranks) * (factor / logistic_sharpness)
    stat_ref[8 : 8 + pos_count, :] = 0.25 * weight
    stat_ref[16 : 16 + pos_count, :] = pulled / logistic_sharpness - weight * slopes

    scores = own_ref[...]
    lane = lax.broadcasted_iota(jnp.int32, (shard, total), 1)
    line = lax.broadcasted_iota(jnp.int32, (shard, total), 0)
    columns = jnp.transpose(
        jnp.concatenate(
            [stat_ref[:, 0:128], target_ref[:, 0:128].astype(jnp.float32)], axis=0
        )
    )[0:shard, :]
    grads = [jnp.zeros((shard, total), jnp.float32) for _ in range(2)]
    for m in range(pos_count):
        bent = jnp.tanh(scores - stat_ref[m : m + 1, :])
        grads[0] = grads[0] + stat_ref[8 + m : 9 + m, :] * (1.0 - bent * bent)
        bent = jnp.tanh(scores - columns[:, m : m + 1])
        grads[1] = grads[1] + columns[:, 8 + m : 9 + m] * (1.0 - bent * bent)
    for m in range(pos_count):
        found = line == target_ref[m : m + 1, :]
        grads[0] = grads[0] + jnp.where(found, stat_ref[16 + m : 17 + m, :], 0.0)
        found = lane == columns[:, 24 + m : 25 + m].astype(jnp.int32)
        grads[1] = grads[1] + jnp.where(found, columns[:, 16 + m : 17 + m], 0.0)
    both = jnp.concatenate(grads, axis=0).astype(jnp.bfloat16)
    product = jnp.dot(both, embed_ref[...], preferred_element_type=jnp.float32)
    out_ref[...] = product[:shard, :] + product[shard:, :]


def body(embed, positives, placement):
    shard, width = embed.shape
    axes = ("row", "col")
    rows = lax.axis_size("row")
    cols = lax.axis_size("col")
    levels = rows // 2
    total = shard * rows * cols
    pos_count = positives.shape[1]
    lane_block = 256 if total <= 4096 else 128

    def swap(array, axis, mask):
        size = lax.axis_size(axis)
        return lax.ppermute(array, axis, [(i, i ^ mask) for i in range(size)])

    def join(parts):
        return parts[0] if len(parts) == 1 else jnp.concatenate(parts, axis=0)

    order = [0]
    steps = [1 << b for b in reversed(range(levels.bit_length() - 1))]

    def spread(ids):
        if not steps:
            return ids
        bit = steps.pop(0)
        order.extend([d ^ bit for d in order])
        return jnp.concatenate([ids, swap(ids, "row", 2 * bit)], axis=0)

    line = [swap(embed, "row", 2 * d) for d in range(1, levels)]
    ids = spread(positives.T)
    line, ids = lax.optimization_barrier((line, ids))
    tall = join([embed] + line)

    plane = {p: swap(tall, "col", p) for p in range(1, cols)}
    while steps:
        ids = spread(ids)
    here, ids = lax.optimization_barrier((tall, ids))
    other = {0: swap(here, "row", 1)}
    ids = (ids, swap(ids, "row", 1))

    plane[0] = tall
    other.update({p: swap(plane[p], "row", 1) for p in range(1, cols)})
    pieces = []
    layout = []
    for p in range(cols):
        for c, part in enumerate((plane[p], other[p])):
            pieces.append(part)
            layout.append([(d * 2 + c) * cols + p for d in range(levels)])

    place = jnp.stack([lax.axis_index(axes) * shard, lax.axis_index("col") * shard])
    vmem = pl.BlockSpec(memory_space=pltpu.VMEM)
    return pl.pallas_call(
        functools.partial(kernel, cols, order, shard, pos_count, lane_block, layout),
        out_shape=jax.ShapeDtypeStruct((shard, width), jnp.float32),
        in_specs=[pl.BlockSpec(memory_space=pltpu.SMEM)] + [vmem] * (3 + len(pieces)),
        out_specs=vmem,
        scratch_shapes=[
            pltpu.VMEM((total, width), jnp.bfloat16),
            pltpu.VMEM((2, total, lane_block), jnp.float32),
            pltpu.VMEM((shard, total), jnp.float32),
            pltpu.VMEM((8, total), jnp.int32),
            pltpu.VMEM((24, total), jnp.float32),
        ],
        compiler_params=pltpu.CompilerParams(vmem_limit_bytes=4 * total * width + 8 * total * lane_block + (16 << 20)),
        cost_estimate=pl.CostEstimate(
            flops=2 * total * total * width,
            bytes_accessed=2 * total * width,
            transcendentals=4 * total * total,
        ),
    )(
        place.astype(jnp.int32),
        placement.reshape(-1, 128),
        *ids,
        *pieces,
    )


def solution(mesh):
    return jax.shard_map(
        body,
        mesh=mesh,
        in_specs=(P(("row", "col"), None), P("row", None), P()),
        out_specs=P(("row", "col"), None),
        check_vma=False,
    )
```

```python
import functools

import jax
import jax.numpy as jnp
from jax import lax
from jax.experimental import pallas as pl
from jax.experimental.pallas import tpu as pltpu
from jax.sharding import PartitionSpec as P

logistic_sharpness = 0.02
half_scale = 0.5 / logistic_sharpness
masked = -1e30


def aligned(start, size):
    if isinstance(start, int):
        return slice(start, start + size)
    return pl.ds(pl.multiple_of(start, size), size)


def lookup(table_ref, ids):
    low = ids % 128
    high = ids // 128
    found = jnp.zeros(ids.shape, jnp.int32)
    for line in range(table_ref.shape[0]):
        entries = jnp.broadcast_to(table_ref[line : line + 1, :], ids.shape)
        found = jnp.where(high == line, jnp.take_along_axis(entries, low, axis=1), found)
    return found


def kernel(cols, order, shard, pos_count, lane_block, layout, *refs):
    levels = len(order)
    place_ref, table_ref = refs[:2]
    ids_refs = refs[2:4]
    pieces = refs[4 : 4 + len(layout)]
    out_ref, embed_ref, score_ref, own_ref, target_ref, stat_ref = refs[4 + len(layout) :]
    total = embed_ref.shape[0]
    me = place_ref[0]
    my_col = place_ref[1]
    pair = lane_block // 128
    small = total <= 1024
    row_chunk = min(512, total)

    for piece, slots in zip(pieces, layout):
        for spot, slot in enumerate(slots):
            embed_ref[slot * shard : (slot + 1) * shard, :] = piece[spot * shard : (spot + 1) * shard, :]

    group = cols * shard
    for line in range(2 * levels):
        for begin in range(0, group, 128):
            ids_ref = ids_refs[line % 2]
            size = ids_ref.shape[0] // levels
            at = order.index(line // 2) * size
            ids = ids_ref[at : at + size, begin : begin + 128]
            ids = jnp.concatenate([ids] * (8 // size), axis=0)
            found = lookup(table_ref, ids) ^ me
            lane = lax.broadcasted_iota(jnp.int32, found.shape, 1)
            found = jnp.take_along_axis(found, lane ^ (my_col % 128), axis=1)
            start = line * group + (begin ^ (my_col - my_col % 128))
            target_ref[:, pl.ds(pl.multiple_of(start, 128), 128)] = found

    def score_chunk(anchors, start, buffer, chunk, picked):
        row = chunk * row_chunk
        scores = half_scale * lax.dot_general(
            embed_ref[aligned(row, row_chunk), :],
            anchors,
            (((1,), (0,)), ((), ())),
            preferred_element_type=jnp.float32,
        )
        score_ref[buffer, aligned(row, row_chunk), :] = scores
        picked = list(picked)
        for half in range(pair):
            targets = target_ref[:, aligned(start + half * 128, 128)]
            near = (targets - row) >> 3
            sub = targets & 7
            for step in range(row_chunk // 8):
                tile = scores[step * 8 : (step + 1) * 8, half * 128 : (half + 1) * 128]
                tile = jnp.take_along_axis(tile, sub, axis=0)
                picked[half] = jnp.where(near == step, tile, picked[half])
        return tuple(picked)

    def rank_chunk(pos, buffer, chunk, sums):
        row = chunk * row_chunk
        sums = list(sums)
        for half in range(pair):
            for part in range(row_chunk // 32):
                scores = score_ref[buffer, aligned(row + part * 32, 32), half * 128 : (half + 1) * 128]
                scores = scores.reshape(4, 8, 128)
                for m in range(pos_count):
                    at = half * pos_count + m
                    bent = jnp.tanh(scores - pos[at][None])
                    sums[2 * at] = sums[2 * at] + jnp.sum(bent, axis=0)
                    sums[2 * at + 1] = sums[2 * at + 1] + jnp.sum(bent * bent, axis=0)
        return tuple(sums)

    def over_chunks(step, have):
        if not small:
            return lax.fori_loop(0, chunks, step, have)
        for chunk in range(chunks):
            have = step(chunk, have)
        return have

    chunks = total // row_chunk
    nothing = (jnp.zeros((8, 128), jnp.float32),) * pair
    zero = (jnp.zeros((8, 128), jnp.float32),) * (2 * pos_count * pair)

    def split(start, buffer, picked):
        inside = (buffer, aligned(start, lane_block), slice(None))
        index = lax.broadcasted_iota(jnp.int32, (lane_block, lane_block), 0)
        lane = lax.broadcasted_iota(jnp.int32, (lane_block, lane_block), 1)
        score_ref[inside] = jnp.where(index == lane, masked, score_ref[inside])
        pos = []
        for half in range(pair):
            lanes = aligned(start + half * 128, 128)
            own_ref[:, lanes] = score_ref[buffer, 0:shard, half * 128 : (half + 1) * 128]
            stat_ref[0:8, lanes] = picked[half]
            for m in range(pos_count):
                pos.append(jnp.broadcast_to(picked[half][m : m + 1, :], (8, 128)))
        return tuple(pos)

    def finish(start, sums):
        for half in range(pair):
            lanes = aligned(start + half * 128, 128)
            for m in range(pos_count):
                at = (half * pos_count + m) * 2
                stat_ref[8 + m : 9 + m, lanes] = jnp.sum(sums[at], axis=0, keepdims=True)
                stat_ref[16 + m : 17 + m, lanes] = jnp.sum(sums[at + 1], axis=0, keepdims=True)

    first = jnp.transpose(embed_ref[0:lane_block, :])
    picked = over_chunks(lambda chunk, have: score_chunk(first, 0, 0, chunk, have), nothing)

    def block_step(block, pos):
        start = block * lane_block
        following = start + lane_block
        buffer = block % 2
        anchors = jnp.transpose(embed_ref[aligned(following, lane_block), :])

        def both(chunk, carry):
            picked, sums = carry
            picked = score_chunk(anchors, following, 1 - buffer, chunk, picked)
            return picked, rank_chunk(pos, buffer, chunk, sums)

        picked, sums = over_chunks(both, (nothing, zero))
        finish(start, sums)
        return split(following, 1 - buffer, picked)

    last = total // lane_block - 1
    pos = split(0, 0, picked)
    if small:
        for block in range(last):
            pos = block_step(block, pos)
    else:
        pos = lax.fori_loop(0, last, block_step, pos)
    sums = over_chunks(lambda chunk, have: rank_chunk(pos, last % 2, chunk, have), zero)
    finish(last * lane_block, sums)

    def turned(values, steps):
        return jnp.concatenate([values[steps:], values[:steps]], axis=0)

    spot = stat_ref[0:pos_count, :]
    ranks = 0.5 + 0.5 * (total + stat_ref[8 : 8 + pos_count, :])
    slopes = 0.25 * (total - stat_ref[16 : 16 + pos_count, :])
    factor = 1.0 / (pos_count * total)
    pulls = -factor / ranks
    prank = 1.0
    pulled = 0.0
    for steps in range(1, pos_count):
        bent = jnp.tanh(turned(spot, steps) - spot)
        prank = prank + 0.5 * (1.0 + bent)
        pulled = pulled + (turned(pulls, steps) - pulls) * (0.25 * (1.0 - bent * bent))
    weight = prank / (ranks * ranks) * (factor / logistic_sharpness)
    stat_ref[8 : 8 + pos_count, :] = 0.25 * weight
    stat_ref[16 : 16 + pos_count, :] = pulled / logistic_sharpness - weight * slopes

    scores = own_ref[...]
    lane = lax.broadcasted_iota(jnp.int32, (shard, total), 1)
    line = lax.broadcasted_iota(jnp.int32, (shard, total), 0)
    columns = jnp.transpose(
        jnp.concatenate(
            [stat_ref[:, 0:128], target_ref[:, 0:128].astype(jnp.float32)], axis=0
        )
    )[0:shard, :]
    grads = [jnp.zeros((shard, total), jnp.float32) for _ in range(2)]
    for m in range(pos_count):
        bent = jnp.tanh(scores - stat_ref[m : m + 1, :])
        grads[0] = grads[0] + stat_ref[8 + m : 9 + m, :] * (1.0 - bent * bent)
        bent = jnp.tanh(scores - columns[:, m : m + 1])
        grads[1] = grads[1] + columns[:, 8 + m : 9 + m] * (1.0 - bent * bent)
    for m in range(pos_count):
        found = line == target_ref[m : m + 1, :]
        grads[0] = grads[0] + jnp.where(found, stat_ref[16 + m : 17 + m, :], 0.0)
        found = lane == columns[:, 24 + m : 25 + m].astype(jnp.int32)
        grads[1] = grads[1] + jnp.where(found, columns[:, 16 + m : 17 + m], 0.0)
    both = jnp.concatenate(grads, axis=0).astype(jnp.bfloat16)
    product = jnp.dot(both, embed_ref[...], preferred_element_type=jnp.float32)
    out_ref[...] = product[:shard, :] + product[shard:, :]


def body(embed, positives, placement):
    shard, width = embed.shape
    axes = ("row", "col")
    rows = lax.axis_size("row")
    cols = lax.axis_size("col")
    levels = rows // 2
    total = shard * rows * cols
    pos_count = positives.shape[1]
    lane_block = 256 if total <= 4096 else 128

    def swap(array, axis, mask):
        size = lax.axis_size(axis)
        return lax.ppermute(array, axis, [(i, i ^ mask) for i in range(size)])

    def join(parts):
        return parts[0] if len(parts) == 1 else jnp.concatenate(parts, axis=0)

    order = [0]
    steps = [1 << b for b in reversed(range(levels.bit_length() - 1))]

    def spread(ids):
        if not steps:
            return ids
        bit = steps.pop(0)
        order.extend([d ^ bit for d in order])
        return jnp.concatenate([ids, swap(ids, "row", 2 * bit)], axis=0)

    line = {d: swap(embed, "row", 2 * d) for d in range(1, levels)}
    far = levels - 1
    ranking = [far // 2 + 1, far] + [d for d in range(1, far) if d != far // 2 + 1]
    ids = spread(positives.T)
    parts, ids = lax.optimization_barrier(([line[d] for d in ranking], ids))
    line = dict(zip(ranking, parts))
    tall = join([embed] + [line[d] for d in range(1, levels)])

    plane = {p: swap(tall, "col", p) for p in range(1, cols)}
    while steps:
        ids = spread(ids)
    here, ids = lax.optimization_barrier((tall, ids))
    other = {0: swap(here, "row", 1)}
    ids = (ids, swap(ids, "row", 1))

    plane[0] = tall
    other.update({p: swap(plane[p], "row", 1) for p in range(1, cols)})
    pieces = []
    layout = []
    for p in range(cols):
        for c, part in enumerate((plane[p], other[p])):
            pieces.append(part)
            layout.append([(d * 2 + c) * cols + p for d in range(levels)])

    place = jnp.stack([lax.axis_index(axes) * shard, lax.axis_index("col") * shard])
    vmem = pl.BlockSpec(memory_space=pltpu.VMEM)
    return pl.pallas_call(
        functools.partial(kernel, cols, order, shard, pos_count, lane_block, layout),
        out_shape=jax.ShapeDtypeStruct((shard, width), jnp.float32),
        in_specs=[pl.BlockSpec(memory_space=pltpu.SMEM)] + [vmem] * (3 + len(pieces)),
        out_specs=vmem,
        scratch_shapes=[
            pltpu.VMEM((total, width), jnp.bfloat16),
            pltpu.VMEM((2, total, lane_block), jnp.float32),
            pltpu.VMEM((shard, total), jnp.float32),
            pltpu.VMEM((8, total), jnp.int32),
            pltpu.VMEM((24, total), jnp.float32),
        ],
        compiler_params=pltpu.CompilerParams(vmem_limit_bytes=4 * total * width + 8 * total * lane_block + (16 << 20)),
        cost_estimate=pl.CostEstimate(
            flops=2 * total * total * width,
            bytes_accessed=2 * total * width,
            transcendentals=4 * total * total,
        ),
    )(
        place.astype(jnp.int32),
        placement.reshape(-1, 128),
        *ids,
        *pieces,
    )


def solution(mesh):
    return jax.shard_map(
        body,
        mesh=mesh,
        in_specs=(P(("row", "col"), None), P("row", None), P()),
        out_specs=P(("row", "col"), None),
        check_vma=False,
    )
```

```python
import functools

import jax
import jax.numpy as jnp
from jax import lax
from jax.experimental import pallas as pl
from jax.experimental.pallas import tpu as pltpu
from jax.sharding import PartitionSpec as P

logistic_sharpness = 0.02
half_scale = 0.5 / logistic_sharpness
masked = -1e30


def aligned(start, size):
    if isinstance(start, int):
        return slice(start, start + size)
    return pl.ds(pl.multiple_of(start, size), size)


def lookup(table_ref, ids):
    low = ids % 128
    high = ids // 128
    found = jnp.zeros(ids.shape, jnp.int32)
    for line in range(table_ref.shape[0]):
        entries = jnp.broadcast_to(table_ref[line : line + 1, :], ids.shape)
        found = jnp.where(high == line, jnp.take_along_axis(entries, low, axis=1), found)
    return found


def kernel(cols, order, shard, pos_count, lane_block, layout, *refs):
    levels = len(order)
    place_ref, table_ref = refs[:2]
    ids_refs = refs[2:4]
    pieces = refs[4 : 4 + len(layout)]
    out_ref, embed_ref, score_ref, own_ref, target_ref, stat_ref = refs[4 + len(layout) :]
    total = embed_ref.shape[0]
    me = place_ref[0]
    my_col = place_ref[1]
    pair = lane_block // 128
    small = total <= 1024
    row_chunk = min(512, total)

    for piece, slots in zip(pieces, layout):
        for spot, slot in enumerate(slots):
            embed_ref[slot * shard : (slot + 1) * shard, :] = piece[spot * shard : (spot + 1) * shard, :]

    group = cols * shard
    for line in range(2 * levels):
        for begin in range(0, group, 128):
            ids_ref = ids_refs[line % 2]
            size = ids_ref.shape[0] // levels
            at = order.index(line // 2) * size
            ids = ids_ref[at : at + size, begin : begin + 128]
            ids = jnp.concatenate([ids] * (8 // size), axis=0)
            found = lookup(table_ref, ids) ^ me
            lane = lax.broadcasted_iota(jnp.int32, found.shape, 1)
            found = jnp.take_along_axis(found, lane ^ (my_col % 128), axis=1)
            start = line * group + (begin ^ (my_col - my_col % 128))
            target_ref[:, pl.ds(pl.multiple_of(start, 128), 128)] = found

    def score_chunk(anchors, start, buffer, chunk, picked):
        row = chunk * row_chunk
        scores = half_scale * lax.dot_general(
            embed_ref[aligned(row, row_chunk), :],
            anchors,
            (((1,), (1,)), ((), ())),
            preferred_element_type=jnp.float32,
        )
        score_ref[buffer, aligned(row, row_chunk), :] = scores
        picked = list(picked)
        for half in range(pair):
            targets = target_ref[:, aligned(start + half * 128, 128)]
            near = (targets - row) >> 3
            sub = targets & 7
            for step in range(row_chunk // 8):
                tile = scores[step * 8 : (step + 1) * 8, half * 128 : (half + 1) * 128]
                tile = jnp.take_along_axis(tile, sub, axis=0)
                picked[half] = jnp.where(near == step, tile, picked[half])
        return tuple(picked)

    def rank_chunk(pos, buffer, chunk, sums):
        row = chunk * row_chunk
        sums = list(sums)
        for half in range(pair):
            for part in range(row_chunk // 32):
                scores = score_ref[buffer, aligned(row + part * 32, 32), half * 128 : (half + 1) * 128]
                scores = scores.reshape(4, 8, 128)
                for m in range(pos_count):
                    at = half * pos_count + m
                    bent = jnp.tanh(scores - pos[at][None])
                    sums[2 * at] = sums[2 * at] + jnp.sum(bent, axis=0)
                    sums[2 * at + 1] = sums[2 * at + 1] + jnp.sum(bent * bent, axis=0)
        return tuple(sums)

    def over_chunks(step, have):
        if not small:
            return lax.fori_loop(0, chunks, step, have)
        for chunk in range(chunks):
            have = step(chunk, have)
        return have

    chunks = total // row_chunk
    nothing = (jnp.zeros((8, 128), jnp.float32),) * pair
    zero = (jnp.zeros((8, 128), jnp.float32),) * (2 * pos_count * pair)

    def split(start, buffer, picked):
        inside = (buffer, aligned(start, lane_block), slice(None))
        index = lax.broadcasted_iota(jnp.int32, (lane_block, lane_block), 0)
        lane = lax.broadcasted_iota(jnp.int32, (lane_block, lane_block), 1)
        score_ref[inside] = jnp.where(index == lane, masked, score_ref[inside])
        pos = []
        for half in range(pair):
            lanes = aligned(start + half * 128, 128)
            own_ref[:, lanes] = score_ref[buffer, 0:shard, half * 128 : (half + 1) * 128]
            stat_ref[0:8, lanes] = picked[half]
            for m in range(pos_count):
                pos.append(jnp.broadcast_to(picked[half][m : m + 1, :], (8, 128)))
        return tuple(pos)

    def finish(start, sums):
        for half in range(pair):
            lanes = aligned(start + half * 128, 128)
            for m in range(pos_count):
                at = (half * pos_count + m) * 2
                stat_ref[8 + m : 9 + m, lanes] = jnp.sum(sums[at], axis=0, keepdims=True)
                stat_ref[16 + m : 17 + m, lanes] = jnp.sum(sums[at + 1], axis=0, keepdims=True)

    first = embed_ref[0:lane_block, :]
    picked = over_chunks(lambda chunk, have: score_chunk(first, 0, 0, chunk, have), nothing)

    def block_step(block, pos):
        start = block * lane_block
        following = start + lane_block
        buffer = block % 2
        anchors = embed_ref[aligned(following, lane_block), :]

        def both(chunk, carry):
            picked, sums = carry
            picked = score_chunk(anchors, following, 1 - buffer, chunk, picked)
            return picked, rank_chunk(pos, buffer, chunk, sums)

        picked, sums = over_chunks(both, (nothing, zero))
        finish(start, sums)
        return split(following, 1 - buffer, picked)

    last = total // lane_block - 1
    pos = split(0, 0, picked)
    if small:
        for block in range(last):
            pos = block_step(block, pos)
    else:
        pos = lax.fori_loop(0, last, block_step, pos)
    sums = over_chunks(lambda chunk, have: rank_chunk(pos, last % 2, chunk, have), zero)
    finish(last * lane_block, sums)

    def turned(values, steps):
        return jnp.concatenate([values[steps:], values[:steps]], axis=0)

    spot = stat_ref[0:pos_count, :]
    ranks = 0.5 + 0.5 * (total + stat_ref[8 : 8 + pos_count, :])
    slopes = 0.25 * (total - stat_ref[16 : 16 + pos_count, :])
    factor = 1.0 / (pos_count * total)
    pulls = -factor / ranks
    prank = 1.0
    pulled = 0.0
    for steps in range(1, pos_count):
        bent = jnp.tanh(turned(spot, steps) - spot)
        prank = prank + 0.5 * (1.0 + bent)
        pulled = pulled + (turned(pulls, steps) - pulls) * (0.25 * (1.0 - bent * bent))
    weight = prank / (ranks * ranks) * (factor / logistic_sharpness)
    stat_ref[8 : 8 + pos_count, :] = 0.25 * weight
    stat_ref[16 : 16 + pos_count, :] = pulled / logistic_sharpness - weight * slopes

    scores = own_ref[...]
    lane = lax.broadcasted_iota(jnp.int32, (shard, total), 1)
    line = lax.broadcasted_iota(jnp.int32, (shard, total), 0)
    columns = jnp.transpose(
        jnp.concatenate(
            [stat_ref[:, 0:128], target_ref[:, 0:128].astype(jnp.float32)], axis=0
        )
    )[0:shard, :]
    grads = [jnp.zeros((shard, total), jnp.float32) for _ in range(2)]
    for m in range(pos_count):
        bent = jnp.tanh(scores - stat_ref[m : m + 1, :])
        grads[0] = grads[0] + stat_ref[8 + m : 9 + m, :] * (1.0 - bent * bent)
        bent = jnp.tanh(scores - columns[:, m : m + 1])
        grads[1] = grads[1] + columns[:, 8 + m : 9 + m] * (1.0 - bent * bent)
    for m in range(pos_count):
        found = line == target_ref[m : m + 1, :]
        grads[0] = grads[0] + jnp.where(found, stat_ref[16 + m : 17 + m, :], 0.0)
        found = lane == columns[:, 24 + m : 25 + m].astype(jnp.int32)
        grads[1] = grads[1] + jnp.where(found, columns[:, 16 + m : 17 + m], 0.0)
    both = jnp.concatenate(grads, axis=0).astype(jnp.bfloat16)
    product = jnp.dot(both, embed_ref[...], preferred_element_type=jnp.float32)
    out_ref[...] = product[:shard, :] + product[shard:, :]


def body(embed, positives, placement):
    shard, width = embed.shape
    axes = ("row", "col")
    rows = lax.axis_size("row")
    cols = lax.axis_size("col")
    levels = rows // 2
    total = shard * rows * cols
    pos_count = positives.shape[1]
    lane_block = 256 if total <= 4096 else 128

    def swap(array, axis, mask):
        size = lax.axis_size(axis)
        return lax.ppermute(array, axis, [(i, i ^ mask) for i in range(size)])

    def join(parts):
        return parts[0] if len(parts) == 1 else jnp.concatenate(parts, axis=0)

    order = [0]
    steps = [1 << b for b in reversed(range(levels.bit_length() - 1))]

    def spread(ids):
        if not steps:
            return ids
        bit = steps.pop(0)
        order.extend([d ^ bit for d in order])
        return jnp.concatenate([ids, swap(ids, "row", 2 * bit)], axis=0)

    line = {d: swap(embed, "row", 2 * d) for d in range(1, levels)}
    far = levels - 1
    ranking = [far // 2 + 1, far] + [d for d in range(1, far) if d != far // 2 + 1]
    corner = cols - 1
    early = swap(embed, "col", corner)
    ids = positives.T
    ids = spread(ids)
    parts, ids = lax.optimization_barrier(([line[d] for d in ranking], ids))
    line = dict(zip(ranking, parts))
    tall = join([embed] + [line[d] for d in range(1, levels)])

    plane = {0: tall}
    plane.update({p: swap(tall, "col", p) for p in range(1, corner)})
    beyond = {d: swap(early, "row", 2 * d) for d in range(1, levels)}
    while steps:
        ids = spread(ids)
    plane[corner] = join([early] + [beyond[d] for d in range(1, levels)])

    here, ids = lax.optimization_barrier((tall, ids))
    other = {0: swap(here, "row", 1)}
    other.update({p: swap(plane[p], "row", 1) for p in range(1, cols)})
    ids = (ids, swap(ids, "row", 1))
    pieces = []
    layout = []
    for p in range(cols):
        for c, part in enumerate((plane[p], other[p])):
            pieces.append(part)
            layout.append([(d * 2 + c) * cols + p for d in range(levels)])

    place = jnp.stack([lax.axis_index(axes) * shard, lax.axis_index("col") * shard])
    vmem = pl.BlockSpec(memory_space=pltpu.VMEM)
    return pl.pallas_call(
        functools.partial(kernel, cols, order, shard, pos_count, lane_block, layout),
        out_shape=jax.ShapeDtypeStruct((shard, width), jnp.float32),
        in_specs=[pl.BlockSpec(memory_space=pltpu.SMEM)] + [vmem] * (3 + len(pieces)),
        out_specs=vmem,
        scratch_shapes=[
            pltpu.VMEM((total, width), jnp.bfloat16),
            pltpu.VMEM((2, total, lane_block), jnp.float32),
            pltpu.VMEM((shard, total), jnp.float32),
            pltpu.VMEM((8, total), jnp.int32),
            pltpu.VMEM((24, total), jnp.float32),
        ],
        compiler_params=pltpu.CompilerParams(vmem_limit_bytes=4 * total * width + 8 * total * lane_block + (16 << 20)),
        cost_estimate=pl.CostEstimate(
            flops=2 * total * total * width,
            bytes_accessed=2 * total * width,
            transcendentals=4 * total * total,
        ),
    )(
        place.astype(jnp.int32),
        placement.reshape(-1, 128),
        *ids,
        *pieces,
    )


def solution(mesh):
    return jax.shard_map(
        body,
        mesh=mesh,
        in_specs=(P(("row", "col"), None), P("row", None), P()),
        out_specs=P(("row", "col"), None),
        check_vma=False,
    )
```

```python
import functools

import jax
import jax.numpy as jnp
from jax import lax
from jax.experimental import pallas as pl
from jax.experimental.pallas import tpu as pltpu
from jax.sharding import PartitionSpec as P

logistic_sharpness = 0.02
half_scale = 0.5 / logistic_sharpness
masked = -1e30


def aligned(start, size):
    if isinstance(start, int):
        return slice(start, start + size)
    return pl.ds(pl.multiple_of(start, size), size)


def lookup(table_ref, ids):
    low = ids % 128
    high = ids // 128
    found = jnp.zeros(ids.shape, jnp.int32)
    for line in range(table_ref.shape[0]):
        entries = jnp.broadcast_to(table_ref[line : line + 1, :], ids.shape)
        found = jnp.where(high == line, jnp.take_along_axis(entries, low, axis=1), found)
    return found


def kernel(cols, shard, pos_count, lane_block, layout, *refs):
    place_ref, table_ref = refs[:2]
    pieces = refs[2 : 2 + len(layout)]
    out_ref, embed_ref, score_ref, own_ref, target_ref, stat_ref = refs[2 + len(layout) :]
    total = embed_ref.shape[0]
    me = place_ref[0]
    my_col = place_ref[1]
    pair = lane_block // 128
    small = total <= 1024
    row_chunk = min(512, total)

    width = embed_ref.shape[1]
    group = cols * shard
    for piece, slots in zip(pieces, layout):
        for spot, slot in enumerate(slots):
            rows = slice(spot * shard, (spot + 1) * shard)
            embed_ref[slot * shard : (slot + 1) * shard, :] = piece[rows, 0:width]
            if piece.shape[1] == width:
                continue
            tail = piece[rows, width : width + 128].astype(jnp.float32).astype(jnp.int32)
            for begin in range(0, group, 128):
                lines = [k * (group // 128) + begin // 128 for k in range(2 * pos_count)]
                parts = jnp.concatenate([tail[k : k + 1, :] for k in lines], axis=0)
                ids = parts[0:pos_count] * 256 + parts[pos_count : 2 * pos_count]
                ids = jnp.concatenate([ids] * (8 // pos_count), axis=0)
                found = lookup(table_ref, ids) ^ me
                lane = lax.broadcasted_iota(jnp.int32, found.shape, 1)
                found = jnp.take_along_axis(found, lane ^ (my_col % 128), axis=1)
                start = slot // cols * group + (begin ^ (my_col - my_col % 128))
                target_ref[:, pl.ds(pl.multiple_of(start, 128), 128)] = found

    def score_chunk(anchors, start, buffer, chunk, picked):
        row = chunk * row_chunk
        scores = half_scale * lax.dot_general(
            embed_ref[aligned(row, row_chunk), :],
            anchors,
            (((1,), (1,)), ((), ())),
            preferred_element_type=jnp.float32,
        )
        score_ref[buffer, aligned(row, row_chunk), :] = scores
        picked = list(picked)
        for half in range(pair):
            targets = target_ref[:, aligned(start + half * 128, 128)]
            near = (targets - row) >> 3
            sub = targets & 7
            for step in range(row_chunk // 8):
                tile = scores[step * 8 : (step + 1) * 8, half * 128 : (half + 1) * 128]
                tile = jnp.take_along_axis(tile, sub, axis=0)
                picked[half] = jnp.where(near == step, tile, picked[half])
        return tuple(picked)

    def rank_chunk(pos, buffer, chunk, sums):
        row = chunk * row_chunk
        sums = list(sums)
        for half in range(pair):
            for part in range(row_chunk // 32):
                scores = score_ref[buffer, aligned(row + part * 32, 32), half * 128 : (half + 1) * 128]
                scores = scores.reshape(4, 8, 128)
                for m in range(pos_count):
                    at = half * pos_count + m
                    bent = jnp.tanh(scores - pos[at][None])
                    sums[2 * at] = sums[2 * at] + jnp.sum(bent, axis=0)
                    sums[2 * at + 1] = sums[2 * at + 1] + jnp.sum(bent * bent, axis=0)
        return tuple(sums)

    def over_chunks(step, have):
        if not small:
            return lax.fori_loop(0, chunks, step, have)
        for chunk in range(chunks):
            have = step(chunk, have)
        return have

    chunks = total // row_chunk
    nothing = (jnp.zeros((8, 128), jnp.float32),) * pair
    zero = (jnp.zeros((8, 128), jnp.float32),) * (2 * pos_count * pair)

    def split(start, buffer, picked):
        inside = (buffer, aligned(start, lane_block), slice(None))
        index = lax.broadcasted_iota(jnp.int32, (lane_block, lane_block), 0)
        lane = lax.broadcasted_iota(jnp.int32, (lane_block, lane_block), 1)
        score_ref[inside] = jnp.where(index == lane, masked, score_ref[inside])
        pos = []
        for half in range(pair):
            lanes = aligned(start + half * 128, 128)
            own_ref[:, lanes] = score_ref[buffer, 0:shard, half * 128 : (half + 1) * 128]
            stat_ref[0:8, lanes] = picked[half]
            for m in range(pos_count):
                pos.append(jnp.broadcast_to(picked[half][m : m + 1, :], (8, 128)))
        return tuple(pos)

    def finish(start, sums):
        for half in range(pair):
            lanes = aligned(start + half * 128, 128)
            for m in range(pos_count):
                at = (half * pos_count + m) * 2
                stat_ref[8 + m : 9 + m, lanes] = jnp.sum(sums[at], axis=0, keepdims=True)
                stat_ref[16 + m : 17 + m, lanes] = jnp.sum(sums[at + 1], axis=0, keepdims=True)

    first = embed_ref[0:lane_block, :]
    picked = over_chunks(lambda chunk, have: score_chunk(first, 0, 0, chunk, have), nothing)

    def block_step(block, pos):
        start = block * lane_block
        following = start + lane_block
        buffer = block % 2
        anchors = embed_ref[aligned(following, lane_block), :]

        def both(chunk, carry):
            picked, sums = carry
            picked = score_chunk(anchors, following, 1 - buffer, chunk, picked)
            return picked, rank_chunk(pos, buffer, chunk, sums)

        picked, sums = over_chunks(both, (nothing, zero))
        finish(start, sums)
        return split(following, 1 - buffer, picked)

    last = total // lane_block - 1
    pos = split(0, 0, picked)
    if small:
        for block in range(last):
            pos = block_step(block, pos)
    else:
        pos = lax.fori_loop(0, last, block_step, pos)
    sums = over_chunks(lambda chunk, have: rank_chunk(pos, last % 2, chunk, have), zero)
    finish(last * lane_block, sums)

    def turned(values, steps):
        return jnp.concatenate([values[steps:], values[:steps]], axis=0)

    spot = stat_ref[0:pos_count, :]
    ranks = 0.5 + 0.5 * (total + stat_ref[8 : 8 + pos_count, :])
    slopes = 0.25 * (total - stat_ref[16 : 16 + pos_count, :])
    factor = 1.0 / (pos_count * total)
    pulls = -factor / ranks
    prank = 1.0
    pulled = 0.0
    for steps in range(1, pos_count):
        bent = jnp.tanh(turned(spot, steps) - spot)
        prank = prank + 0.5 * (1.0 + bent)
        pulled = pulled + (turned(pulls, steps) - pulls) * (0.25 * (1.0 - bent * bent))
    weight = prank / (ranks * ranks) * (factor / logistic_sharpness)
    stat_ref[8 : 8 + pos_count, :] = 0.25 * weight
    stat_ref[16 : 16 + pos_count, :] = pulled / logistic_sharpness - weight * slopes

    scores = own_ref[...]
    lane = lax.broadcasted_iota(jnp.int32, (shard, total), 1)
    line = lax.broadcasted_iota(jnp.int32, (shard, total), 0)
    columns = jnp.transpose(
        jnp.concatenate(
            [stat_ref[:, 0:128], target_ref[:, 0:128].astype(jnp.float32)], axis=0
        )
    )[0:shard, :]
    grads = [jnp.zeros((shard, total), jnp.float32) for _ in range(2)]
    for m in range(pos_count):
        bent = jnp.tanh(scores - stat_ref[m : m + 1, :])
        grads[0] = grads[0] + stat_ref[8 + m : 9 + m, :] * (1.0 - bent * bent)
        bent = jnp.tanh(scores - columns[:, m : m + 1])
        grads[1] = grads[1] + columns[:, 8 + m : 9 + m] * (1.0 - bent * bent)
    for m in range(pos_count):
        found = line == target_ref[m : m + 1, :]
        grads[0] = grads[0] + jnp.where(found, stat_ref[16 + m : 17 + m, :], 0.0)
        found = lane == columns[:, 24 + m : 25 + m].astype(jnp.int32)
        grads[1] = grads[1] + jnp.where(found, columns[:, 16 + m : 17 + m], 0.0)
    both = jnp.concatenate(grads, axis=0).astype(jnp.bfloat16)
    product = jnp.dot(both, embed_ref[...], preferred_element_type=jnp.float32)
    out_ref[...] = product[:shard, :] + product[shard:, :]


def body(embed, positives, placement):
    shard, width = embed.shape
    axes = ("row", "col")
    rows = lax.axis_size("row")
    cols = lax.axis_size("col")
    levels = rows // 2
    total = shard * rows * cols
    pos_count = positives.shape[1]
    lane_block = 256 if total <= 4096 else 128

    def swap(array, axis, mask):
        size = lax.axis_size(axis)
        return lax.ppermute(array, axis, [(i, i ^ mask) for i in range(size)])

    def join(parts):
        return parts[0] if len(parts) == 1 else jnp.concatenate(parts, axis=0)

    line = {d: swap(embed, "row", 2 * d) for d in range(1, levels)}
    far = levels - 1
    middle = far // 2 + 1
    ranking = [middle, far] + [d for d in range(1, far) if d != middle]
    corner = cols - 1
    early = swap(embed, "col", corner)
    parts = lax.optimization_barrier([line[d] for d in ranking])
    line = dict(zip(ranking, parts))
    tall = join([embed] + [line[d] for d in range(1, levels)])

    ids = positives.T
    ids = jnp.concatenate([ids // 256, ids % 256], axis=0).astype(jnp.bfloat16).reshape(-1, 128)
    ids = jnp.concatenate([ids, jnp.zeros((shard - ids.shape[0], 128), ids.dtype)], axis=0)
    early = jnp.concatenate([early, ids], axis=1)

    plane = {0: tall}
    plane.update({p: swap(tall, "col", p) for p in range(1, corner)})
    beyond = {d: swap(early, "row", 2 * d) for d in range(1, levels)}
    plane[corner] = join([early] + [beyond[d] for d in range(1, levels)])

    other = {p: swap(plane[p], "row", 1) for p in range(cols)}
    pieces = []
    layout = []
    for p in range(cols):
        for c, part in enumerate((plane[p], other[p])):
            pieces.append(part)
            layout.append([(d * 2 + c) * cols + p for d in range(levels)])

    place = jnp.stack([lax.axis_index(axes) * shard, lax.axis_index("col") * shard])
    vmem = pl.BlockSpec(memory_space=pltpu.VMEM)
    return pl.pallas_call(
        functools.partial(kernel, cols, shard, pos_count, lane_block, layout),
        out_shape=jax.ShapeDtypeStruct((shard, width), jnp.float32),
        in_specs=[pl.BlockSpec(memory_space=pltpu.SMEM)] + [vmem] * (1 + len(pieces)),
        out_specs=vmem,
        scratch_shapes=[
            pltpu.VMEM((total, width), jnp.bfloat16),
            pltpu.VMEM((2, total, lane_block), jnp.float32),
            pltpu.VMEM((shard, total), jnp.float32),
            pltpu.VMEM((8, total), jnp.int32),
            pltpu.VMEM((24, total), jnp.float32),
        ],
        compiler_params=pltpu.CompilerParams(vmem_limit_bytes=4 * total * width + 8 * total * lane_block + (16 << 20)),
        cost_estimate=pl.CostEstimate(
            flops=2 * total * total * width,
            bytes_accessed=2 * total * width,
            transcendentals=4 * total * total,
        ),
    )(
        place.astype(jnp.int32),
        placement.reshape(-1, 128),
        *pieces,
    )


def solution(mesh):
    return jax.shard_map(
        body,
        mesh=mesh,
        in_specs=(P(("row", "col"), None), P("row", None), P()),
        out_specs=P(("row", "col"), None),
        check_vma=False,
    )
```

```python
import functools

import jax
import jax.numpy as jnp
from jax import lax
from jax.experimental import pallas as pl
from jax.experimental.pallas import tpu as pltpu
from jax.sharding import PartitionSpec as P

logistic_sharpness = 0.02
half_scale = 0.5 / logistic_sharpness
masked = -1e30


def aligned(start, size):
    if isinstance(start, int):
        return slice(start, start + size)
    return pl.ds(pl.multiple_of(start, size), size)


def lookup(table_ref, ids):
    low = ids % 128
    high = ids // 128
    found = jnp.zeros(ids.shape, jnp.int32)
    for line in range(table_ref.shape[0]):
        entries = jnp.broadcast_to(table_ref[line : line + 1, :], ids.shape)
        found = jnp.where(high == line, jnp.take_along_axis(entries, low, axis=1), found)
    return found


def kernel(cols, shard, pos_count, lane_block, layout, *refs):
    place_ref, table_ref = refs[:2]
    pieces = refs[2 : 2 + len(layout)]
    out_ref, embed_ref, score_ref, own_ref, target_ref, stat_ref = refs[2 + len(layout) :]
    total = embed_ref.shape[0]
    me = place_ref[0]
    my_col = place_ref[1]
    pair = lane_block // 128
    small = total <= 1024
    row_chunk = min(512, total)

    width = embed_ref.shape[1]
    group = cols * shard
    for piece, slots in zip(pieces, layout):
        for spot, slot in enumerate(slots):
            rows = slice(spot * shard, (spot + 1) * shard)
            embed_ref[slot * shard : (slot + 1) * shard, :] = piece[rows, 0:width]
            if piece.shape[1] == width:
                continue
            tail = piece[rows, width : width + 128].astype(jnp.float32).astype(jnp.int32)
            for begin in range(0, group, 128):
                lines = [k * (group // 128) + begin // 128 for k in range(2 * pos_count)]
                parts = jnp.concatenate([tail[k : k + 1, :] for k in lines], axis=0)
                ids = parts[0:pos_count] * 256 + parts[pos_count : 2 * pos_count]
                ids = jnp.concatenate([ids] * (8 // pos_count), axis=0)
                found = lookup(table_ref, ids) ^ me
                lane = lax.broadcasted_iota(jnp.int32, found.shape, 1)
                found = jnp.take_along_axis(found, lane ^ (my_col % 128), axis=1)
                start = slot // cols * group + (begin ^ (my_col - my_col % 128))
                target_ref[:, pl.ds(pl.multiple_of(start, 128), 128)] = found

    def score_chunk(anchors, start, buffer, chunk, picked):
        row = chunk * row_chunk
        scores = half_scale * lax.dot_general(
            embed_ref[aligned(row, row_chunk), :],
            anchors,
            (((1,), (1,)), ((), ())),
            preferred_element_type=jnp.float32,
        )
        score_ref[buffer, aligned(row, row_chunk), :] = scores
        picked = list(picked)
        for half in range(pair):
            targets = target_ref[:, aligned(start + half * 128, 128)]
            near = (targets - row) >> 3
            sub = targets & 7
            for step in range(row_chunk // 8):
                tile = scores[step * 8 : (step + 1) * 8, half * 128 : (half + 1) * 128]
                tile = jnp.take_along_axis(tile, sub, axis=0)
                picked[half] = jnp.where(near == step, tile, picked[half])
        return tuple(picked)

    def rank_chunk(pos, buffer, chunk, sums):
        row = chunk * row_chunk
        sums = list(sums)
        for half in range(pair):
            for part in range(row_chunk // 32):
                scores = score_ref[buffer, aligned(row + part * 32, 32), half * 128 : (half + 1) * 128]
                scores = scores.reshape(4, 8, 128)
                for m in range(pos_count):
                    at = half * pos_count + m
                    bent = jnp.tanh(scores - pos[at][None])
                    sums[2 * at] = sums[2 * at] + jnp.sum(bent, axis=0)
                    sums[2 * at + 1] = sums[2 * at + 1] + jnp.sum(bent * bent, axis=0)
        return tuple(sums)

    def over_chunks(step, have):
        if not small:
            return lax.fori_loop(0, chunks, step, have)
        for chunk in range(chunks):
            have = step(chunk, have)
        return have

    chunks = total // row_chunk
    nothing = (jnp.zeros((8, 128), jnp.float32),) * pair
    zero = (jnp.zeros((8, 128), jnp.float32),) * (2 * pos_count * pair)

    def split(start, buffer, picked):
        inside = (buffer, aligned(start, lane_block), slice(None))
        index = lax.broadcasted_iota(jnp.int32, (lane_block, lane_block), 0)
        lane = lax.broadcasted_iota(jnp.int32, (lane_block, lane_block), 1)
        score_ref[inside] = jnp.where(index == lane, masked, score_ref[inside])
        pos = []
        for half in range(pair):
            lanes = aligned(start + half * 128, 128)
            own_ref[:, lanes] = score_ref[buffer, 0:shard, half * 128 : (half + 1) * 128]
            stat_ref[0:8, lanes] = picked[half]
            for m in range(pos_count):
                pos.append(jnp.broadcast_to(picked[half][m : m + 1, :], (8, 128)))
        return tuple(pos)

    def finish(start, sums):
        for half in range(pair):
            lanes = aligned(start + half * 128, 128)
            for m in range(pos_count):
                at = (half * pos_count + m) * 2
                stat_ref[8 + m : 9 + m, lanes] = jnp.sum(sums[at], axis=0, keepdims=True)
                stat_ref[16 + m : 17 + m, lanes] = jnp.sum(sums[at + 1], axis=0, keepdims=True)

    first = embed_ref[0:lane_block, :]
    picked = over_chunks(lambda chunk, have: score_chunk(first, 0, 0, chunk, have), nothing)

    def block_step(block, pos):
        start = block * lane_block
        following = start + lane_block
        buffer = block % 2
        anchors = embed_ref[aligned(following, lane_block), :]

        def both(chunk, carry):
            picked, sums = carry
            picked = score_chunk(anchors, following, 1 - buffer, chunk, picked)
            return picked, rank_chunk(pos, buffer, chunk, sums)

        picked, sums = over_chunks(both, (nothing, zero))
        finish(start, sums)
        return split(following, 1 - buffer, picked)

    last = total // lane_block - 1
    pos = split(0, 0, picked)
    if small:
        for block in range(last):
            pos = block_step(block, pos)
    else:
        pos = lax.fori_loop(0, last, block_step, pos)
    sums = over_chunks(lambda chunk, have: rank_chunk(pos, last % 2, chunk, have), zero)
    finish(last * lane_block, sums)

    def turned(values, steps):
        return jnp.concatenate([values[steps:], values[:steps]], axis=0)

    spot = stat_ref[0:pos_count, :]
    ranks = 0.5 + 0.5 * (total + stat_ref[8 : 8 + pos_count, :])
    slopes = 0.25 * (total - stat_ref[16 : 16 + pos_count, :])
    factor = 1.0 / (pos_count * total)
    pulls = -factor / ranks
    prank = 1.0
    pulled = 0.0
    for steps in range(1, pos_count):
        bent = jnp.tanh(turned(spot, steps) - spot)
        prank = prank + 0.5 * (1.0 + bent)
        pulled = pulled + (turned(pulls, steps) - pulls) * (0.25 * (1.0 - bent * bent))
    weight = prank / (ranks * ranks) * (factor / logistic_sharpness)
    stat_ref[8 : 8 + pos_count, :] = 0.25 * weight
    stat_ref[16 : 16 + pos_count, :] = pulled / logistic_sharpness - weight * slopes

    scores = own_ref[...]
    lane = lax.broadcasted_iota(jnp.int32, (shard, total), 1)
    line = lax.broadcasted_iota(jnp.int32, (shard, total), 0)
    columns = jnp.transpose(
        jnp.concatenate(
            [stat_ref[:, 0:128], target_ref[:, 0:128].astype(jnp.float32)], axis=0
        )
    )[0:shard, :]
    grads = [jnp.zeros((shard, total), jnp.float32) for _ in range(2)]
    for m in range(pos_count):
        bent = jnp.tanh(scores - stat_ref[m : m + 1, :])
        grads[0] = grads[0] + stat_ref[8 + m : 9 + m, :] * (1.0 - bent * bent)
        bent = jnp.tanh(scores - columns[:, m : m + 1])
        grads[1] = grads[1] + columns[:, 8 + m : 9 + m] * (1.0 - bent * bent)
    for m in range(pos_count):
        found = line == target_ref[m : m + 1, :]
        grads[0] = grads[0] + jnp.where(found, stat_ref[16 + m : 17 + m, :], 0.0)
        found = lane == columns[:, 24 + m : 25 + m].astype(jnp.int32)
        grads[1] = grads[1] + jnp.where(found, columns[:, 16 + m : 17 + m], 0.0)
    both = jnp.concatenate(grads, axis=0).astype(jnp.bfloat16)
    product = jnp.dot(both, embed_ref[...], preferred_element_type=jnp.float32)
    out_ref[...] = product[:shard, :] + product[shard:, :]


def body(embed, positives, placement):
    shard, width = embed.shape
    axes = ("row", "col")
    rows = lax.axis_size("row")
    cols = lax.axis_size("col")
    levels = rows // 2
    total = shard * rows * cols
    pos_count = positives.shape[1]
    lane_block = 256 if total <= 4096 else 128

    def swap(array, axis, mask):
        size = lax.axis_size(axis)
        return lax.ppermute(array, axis, [(i, i ^ mask) for i in range(size)])

    def join(parts):
        return parts[0] if len(parts) == 1 else jnp.concatenate(parts, axis=0)

    line = {d: swap(embed, "row", 2 * d) for d in range(1, levels)}
    far = levels - 1
    middle = far // 2 + 1
    ranking = [middle, far] + [d for d in range(1, far) if d != middle]
    corner = cols - 1
    early = swap(embed, "col", corner)
    parts = lax.optimization_barrier([line[d] for d in ranking])
    line = dict(zip(ranking, parts))
    tall = join([embed] + [line[d] for d in range(1, levels)])

    ids = positives.T
    ids = jnp.concatenate([ids // 256, ids % 256], axis=0).astype(jnp.bfloat16).reshape(-1, 128)
    ids = jnp.concatenate([ids, jnp.zeros((shard - ids.shape[0], 128), ids.dtype)], axis=0)
    early = jnp.concatenate([early, ids], axis=1)

    plane = {0: tall}
    plane.update({p: swap(tall, "col", p) for p in range(1, corner)})
    beyond = {d: swap(early, "row", 2 * d) for d in range(1, levels)}
    near = [p for p in range(1, corner)]
    tied = lax.optimization_barrier((plane[near[0]], [plane[p] for p in near[1:]], [beyond[d] for d in ranking]))
    plane[near[0]] = tied[0]
    plane.update(zip(near[1:], tied[1]))
    beyond = dict(zip(ranking, tied[2]))
    plane[corner] = join([early] + [beyond[d] for d in range(1, levels)])

    other = {p: swap(plane[p], "row", 1) for p in range(cols)}
    pieces = []
    layout = []
    for p in range(cols):
        for c, part in enumerate((plane[p], other[p])):
            pieces.append(part)
            layout.append([(d * 2 + c) * cols + p for d in range(levels)])

    place = jnp.stack([lax.axis_index(axes) * shard, lax.axis_index("col") * shard])
    vmem = pl.BlockSpec(memory_space=pltpu.VMEM)
    return pl.pallas_call(
        functools.partial(kernel, cols, shard, pos_count, lane_block, layout),
        out_shape=jax.ShapeDtypeStruct((shard, width), jnp.float32),
        in_specs=[pl.BlockSpec(memory_space=pltpu.SMEM)] + [vmem] * (1 + len(pieces)),
        out_specs=vmem,
        scratch_shapes=[
            pltpu.VMEM((total, width), jnp.bfloat16),
            pltpu.VMEM((2, total, lane_block), jnp.float32),
            pltpu.VMEM((shard, total), jnp.float32),
            pltpu.VMEM((8, total), jnp.int32),
            pltpu.VMEM((24, total), jnp.float32),
        ],
        compiler_params=pltpu.CompilerParams(vmem_limit_bytes=4 * total * width + 8 * total * lane_block + (16 << 20)),
        cost_estimate=pl.CostEstimate(
            flops=2 * total * total * width,
            bytes_accessed=2 * total * width,
            transcendentals=4 * total * total,
        ),
    )(
        place.astype(jnp.int32),
        placement.reshape(-1, 128),
        *pieces,
    )


def solution(mesh):
    return jax.shard_map(
        body,
        mesh=mesh,
        in_specs=(P(("row", "col"), None), P("row", None), P()),
        out_specs=P(("row", "col"), None),
        check_vma=False,
    )
```

```python
import functools

import jax
import jax.numpy as jnp
from jax import lax
from jax.experimental import pallas as pl
from jax.experimental.pallas import tpu as pltpu
from jax.sharding import PartitionSpec as P

logistic_sharpness = 0.02
half_scale = 0.5 / logistic_sharpness
masked = -1e30


def aligned(start, size):
    if isinstance(start, int):
        return slice(start, start + size)
    return pl.ds(pl.multiple_of(start, size), size)


def lookup(table_ref, ids):
    low = ids % 128
    high = ids // 128
    found = jnp.zeros(ids.shape, jnp.int32)
    for line in range(table_ref.shape[0]):
        entries = jnp.broadcast_to(table_ref[line : line + 1, :], ids.shape)
        found = jnp.where(high == line, jnp.take_along_axis(entries, low, axis=1), found)
    return found


def kernel(cols, shard, pos_count, lane_block, layout, *refs):
    place_ref, table_ref = refs[:2]
    pieces = refs[2 : 2 + len(layout)]
    out_ref, embed_ref, score_ref, own_ref, target_ref, stat_ref = refs[2 + len(layout) :]
    total = embed_ref.shape[0]
    me = place_ref[0]
    my_col = place_ref[1]
    pair = lane_block // 128
    small = total <= 1024
    row_chunk = min(512, total)

    width = embed_ref.shape[1]
    group = cols * shard
    for piece, slots in zip(pieces, layout):
        for spot, slot in enumerate(slots):
            rows = slice(spot * shard, (spot + 1) * shard)
            embed_ref[slot * shard : (slot + 1) * shard, :] = piece[rows, 0:width]
            if piece.shape[1] == width:
                continue
            tail = piece[rows, width : width + 128].astype(jnp.float32).astype(jnp.int32)
            for begin in range(0, group, 128):
                lines = [k * (group // 128) + begin // 128 for k in range(2 * pos_count)]
                parts = jnp.concatenate([tail[k : k + 1, :] for k in lines], axis=0)
                ids = parts[0:pos_count] * 256 + parts[pos_count : 2 * pos_count]
                ids = jnp.concatenate([ids] * (8 // pos_count), axis=0)
                found = lookup(table_ref, ids) ^ me
                lane = lax.broadcasted_iota(jnp.int32, found.shape, 1)
                found = jnp.take_along_axis(found, lane ^ (my_col % 128), axis=1)
                start = slot // cols * group + (begin ^ (my_col - my_col % 128))
                target_ref[:, pl.ds(pl.multiple_of(start, 128), 128)] = found

    def score_chunk(anchors, start, buffer, chunk, picked):
        row = chunk * row_chunk
        scores = half_scale * lax.dot_general(
            embed_ref[aligned(row, row_chunk), :],
            anchors,
            (((1,), (1,)), ((), ())),
            preferred_element_type=jnp.float32,
        )
        score_ref[buffer, aligned(row, row_chunk), :] = scores
        picked = list(picked)
        for half in range(pair):
            targets = target_ref[:, aligned(start + half * 128, 128)]
            near = (targets - row) >> 3
            sub = targets & 7
            for step in range(row_chunk // 8):
                tile = scores[step * 8 : (step + 1) * 8, half * 128 : (half + 1) * 128]
                tile = jnp.take_along_axis(tile, sub, axis=0)
                picked[half] = jnp.where(near == step, tile, picked[half])
        return tuple(picked)

    def rank_chunk(pos, buffer, chunk, sums):
        row = chunk * row_chunk
        sums = list(sums)
        for half in range(pair):
            for part in range(row_chunk // 32):
                scores = score_ref[buffer, aligned(row + part * 32, 32), half * 128 : (half + 1) * 128]
                scores = scores.reshape(4, 8, 128)
                for m in range(pos_count):
                    at = half * pos_count + m
                    bent = jnp.tanh(scores - pos[at][None])
                    sums[2 * at] = sums[2 * at] + jnp.sum(bent, axis=0)
                    sums[2 * at + 1] = sums[2 * at + 1] + jnp.sum(bent * bent, axis=0)
        return tuple(sums)

    def over_chunks(step, have):
        if not small:
            return lax.fori_loop(0, chunks, step, have)
        for chunk in range(chunks):
            have = step(chunk, have)
        return have

    chunks = total // row_chunk
    nothing = (jnp.zeros((8, 128), jnp.float32),) * pair
    zero = (jnp.zeros((8, 128), jnp.float32),) * (2 * pos_count * pair)

    def split(start, buffer, picked):
        inside = (buffer, aligned(start, lane_block), slice(None))
        index = lax.broadcasted_iota(jnp.int32, (lane_block, lane_block), 0)
        lane = lax.broadcasted_iota(jnp.int32, (lane_block, lane_block), 1)
        score_ref[inside] = jnp.where(index == lane, masked, score_ref[inside])
        pos = []
        for half in range(pair):
            lanes = aligned(start + half * 128, 128)
            own_ref[:, lanes] = score_ref[buffer, 0:shard, half * 128 : (half + 1) * 128]
            stat_ref[0:8, lanes] = picked[half]
            for m in range(pos_count):
                pos.append(jnp.broadcast_to(picked[half][m : m + 1, :], (8, 128)))
        return tuple(pos)

    def finish(start, sums):
        for half in range(pair):
            lanes = aligned(start + half * 128, 128)
            for m in range(pos_count):
                at = (half * pos_count + m) * 2
                stat_ref[8 + m : 9 + m, lanes] = jnp.sum(sums[at], axis=0, keepdims=True)
                stat_ref[16 + m : 17 + m, lanes] = jnp.sum(sums[at + 1], axis=0, keepdims=True)

    first = embed_ref[0:lane_block, :]
    picked = over_chunks(lambda chunk, have: score_chunk(first, 0, 0, chunk, have), nothing)

    def block_step(block, pos):
        start = block * lane_block
        following = start + lane_block
        buffer = block % 2
        anchors = embed_ref[aligned(following, lane_block), :]

        def both(chunk, carry):
            picked, sums = carry
            picked = score_chunk(anchors, following, 1 - buffer, chunk, picked)
            return picked, rank_chunk(pos, buffer, chunk, sums)

        picked, sums = over_chunks(both, (nothing, zero))
        finish(start, sums)
        return split(following, 1 - buffer, picked)

    last = total // lane_block - 1
    pos = split(0, 0, picked)
    if small:
        for block in range(last):
            pos = block_step(block, pos)
    else:
        pos = lax.fori_loop(0, last, block_step, pos)
    sums = over_chunks(lambda chunk, have: rank_chunk(pos, last % 2, chunk, have), zero)
    finish(last * lane_block, sums)

    def turned(values, steps):
        return jnp.concatenate([values[steps:], values[:steps]], axis=0)

    spot = stat_ref[0:pos_count, :]
    ranks = 0.5 + 0.5 * (total + stat_ref[8 : 8 + pos_count, :])
    slopes = 0.25 * (total - stat_ref[16 : 16 + pos_count, :])
    factor = 1.0 / (pos_count * total)
    pulls = -factor / ranks
    prank = 1.0
    pulled = 0.0
    for steps in range(1, pos_count):
        bent = jnp.tanh(turned(spot, steps) - spot)
        prank = prank + 0.5 * (1.0 + bent)
        pulled = pulled + (turned(pulls, steps) - pulls) * (0.25 * (1.0 - bent * bent))
    weight = prank / (ranks * ranks) * (factor / logistic_sharpness)
    stat_ref[8 : 8 + pos_count, :] = 0.25 * weight
    stat_ref[16 : 16 + pos_count, :] = pulled / logistic_sharpness - weight * slopes

    scores = own_ref[...]
    lane = lax.broadcasted_iota(jnp.int32, (shard, total), 1)
    line = lax.broadcasted_iota(jnp.int32, (shard, total), 0)
    columns = jnp.transpose(
        jnp.concatenate(
            [stat_ref[:, 0:128], target_ref[:, 0:128].astype(jnp.float32)], axis=0
        )
    )[0:shard, :]
    grads = [jnp.zeros((shard, total), jnp.float32) for _ in range(2)]
    for m in range(pos_count):
        bent = jnp.tanh(scores - stat_ref[m : m + 1, :])
        grads[0] = grads[0] + stat_ref[8 + m : 9 + m, :] * (1.0 - bent * bent)
        bent = jnp.tanh(scores - columns[:, m : m + 1])
        grads[1] = grads[1] + columns[:, 8 + m : 9 + m] * (1.0 - bent * bent)
    for m in range(pos_count):
        found = line == target_ref[m : m + 1, :]
        grads[0] = grads[0] + jnp.where(found, stat_ref[16 + m : 17 + m, :], 0.0)
        found = lane == columns[:, 24 + m : 25 + m].astype(jnp.int32)
        grads[1] = grads[1] + jnp.where(found, columns[:, 16 + m : 17 + m], 0.0)
    both = jnp.concatenate(grads, axis=0).astype(jnp.bfloat16)
    product = jnp.dot(both, embed_ref[...], preferred_element_type=jnp.float32)
    out_ref[...] = product[:shard, :] + product[shard:, :]


def body(embed, positives, placement):
    shard, width = embed.shape
    axes = ("row", "col")
    rows = lax.axis_size("row")
    cols = lax.axis_size("col")
    levels = rows // 2
    total = shard * rows * cols
    pos_count = positives.shape[1]
    lane_block = 256 if total <= 4096 else 128

    def swap(array, axis, mask):
        size = lax.axis_size(axis)
        return lax.ppermute(array, axis, [(i, i ^ mask) for i in range(size)])

    def join(parts):
        return parts[0] if len(parts) == 1 else jnp.concatenate(parts, axis=0)

    line = {d: swap(embed, "row", 2 * d) for d in range(1, levels)}
    far = levels - 1
    middle = far // 2 + 1
    ranking = [middle, far] + [d for d in range(1, far) if d != middle]
    corner = cols - 1
    early = swap(embed, "col", corner)
    parts = lax.optimization_barrier([line[middle], line[far], early] + [line[d] for d in ranking[2:]])
    early_after = parts.pop(2)
    line = dict(zip([middle, far] + ranking[2:], parts))
    tall = join([embed] + [line[d] for d in range(1, levels)])

    ids = positives.T
    ids = jnp.concatenate([ids // 256, ids % 256], axis=0).astype(jnp.bfloat16).reshape(-1, 128)
    ids = jnp.concatenate([ids, jnp.zeros((shard - ids.shape[0], 128), ids.dtype)], axis=0)
    early = jnp.concatenate([early, ids], axis=1)

    plane = {0: tall}
    plane.update({p: swap(tall, "col", p) for p in range(1, corner)})
    beyond = {d: swap(early, "row", 2 * d) for d in range(1, levels)}
    corner_rows = jnp.concatenate([early_after, ids], axis=1)
    plane[corner] = join([corner_rows] + [beyond[d] for d in range(1, levels)])

    other = {p: swap(plane[p], "row", 1) for p in range(cols)}
    pieces = []
    layout = []
    for p in range(cols):
        for c, part in enumerate((plane[p], other[p])):
            pieces.append(part)
            layout.append([(d * 2 + c) * cols + p for d in range(levels)])

    place = jnp.stack([lax.axis_index(axes) * shard, lax.axis_index("col") * shard])
    vmem = pl.BlockSpec(memory_space=pltpu.VMEM)
    return pl.pallas_call(
        functools.partial(kernel, cols, shard, pos_count, lane_block, layout),
        out_shape=jax.ShapeDtypeStruct((shard, width), jnp.float32),
        in_specs=[pl.BlockSpec(memory_space=pltpu.SMEM)] + [vmem] * (1 + len(pieces)),
        out_specs=vmem,
        scratch_shapes=[
            pltpu.VMEM((total, width), jnp.bfloat16),
            pltpu.VMEM((2, total, lane_block), jnp.float32),
            pltpu.VMEM((shard, total), jnp.float32),
            pltpu.VMEM((8, total), jnp.int32),
            pltpu.VMEM((24, total), jnp.float32),
        ],
        compiler_params=pltpu.CompilerParams(vmem_limit_bytes=4 * total * width + 8 * total * lane_block + (16 << 20)),
        cost_estimate=pl.CostEstimate(
            flops=2 * total * total * width,
            bytes_accessed=2 * total * width,
            transcendentals=4 * total * total,
        ),
    )(
        place.astype(jnp.int32),
        placement.reshape(-1, 128),
        *pieces,
    )


def solution(mesh):
    return jax.shard_map(
        body,
        mesh=mesh,
        in_specs=(P(("row", "col"), None), P("row", None), P()),
        out_specs=P(("row", "col"), None),
        check_vma=False,
    )
```

```python
import functools

import jax
import jax.numpy as jnp
from jax import lax
from jax.experimental import pallas as pl
from jax.experimental.pallas import tpu as pltpu
from jax.sharding import PartitionSpec as P

logistic_sharpness = 0.02
half_scale = 0.5 / logistic_sharpness
masked = -1e30


def aligned(start, size):
    if isinstance(start, int):
        return slice(start, start + size)
    return pl.ds(pl.multiple_of(start, size), size)


def lookup(table_ref, ids):
    low = ids % 128
    high = ids // 128
    found = jnp.zeros(ids.shape, jnp.int32)
    for line in range(table_ref.shape[0]):
        entries = jnp.broadcast_to(table_ref[line : line + 1, :], ids.shape)
        found = jnp.where(high == line, jnp.take_along_axis(entries, low, axis=1), found)
    return found


def kernel(cols, shard, pos_count, lane_block, layout, *refs):
    place_ref, table_ref = refs[:2]
    pieces = refs[2 : 2 + len(layout)]
    out_ref, embed_ref, score_ref, own_ref, target_ref, stat_ref = refs[2 + len(layout) :]
    total = embed_ref.shape[0]
    me = place_ref[0]
    my_col = place_ref[1]
    pair = lane_block // 128
    small = total <= 1024
    row_chunk = min(512, total)

    width = embed_ref.shape[1]
    group = cols * shard
    for piece, slots in zip(pieces, layout):
        for spot, slot in enumerate(slots):
            rows = slice(spot * shard, (spot + 1) * shard)
            embed_ref[slot * shard : (slot + 1) * shard, :] = piece[rows, 0:width]
            if piece.shape[1] == width:
                continue
            tail = piece[rows, width : width + 128].astype(jnp.float32).astype(jnp.int32)
            for begin in range(0, group, 128):
                lines = [k * (group // 128) + begin // 128 for k in range(2 * pos_count)]
                parts = jnp.concatenate([tail[k : k + 1, :] for k in lines], axis=0)
                ids = parts[0:pos_count] * 256 + parts[pos_count : 2 * pos_count]
                ids = jnp.concatenate([ids] * (8 // pos_count), axis=0)
                found = lookup(table_ref, ids) ^ me
                lane = lax.broadcasted_iota(jnp.int32, found.shape, 1)
                found = jnp.take_along_axis(found, lane ^ (my_col % 128), axis=1)
                start = slot // cols * group + (begin ^ (my_col - my_col % 128))
                target_ref[:, pl.ds(pl.multiple_of(start, 128), 128)] = found

    def score_chunk(anchors, start, buffer, chunk, picked):
        row = chunk * row_chunk
        scores = half_scale * lax.dot_general(
            embed_ref[aligned(row, row_chunk), :],
            anchors,
            (((1,), (1,)), ((), ())),
            preferred_element_type=jnp.float32,
        )
        score_ref[buffer, aligned(row, row_chunk), :] = scores
        picked = list(picked)
        for half in range(pair):
            targets = target_ref[:, aligned(start + half * 128, 128)]
            near = (targets - row) >> 3
            sub = targets & 7
            for step in range(row_chunk // 8):
                tile = scores[step * 8 : (step + 1) * 8, half * 128 : (half + 1) * 128]
                tile = jnp.take_along_axis(tile, sub, axis=0)
                picked[half] = jnp.where(near == step, tile, picked[half])
        return tuple(picked)

    def rank_chunk(pos, buffer, chunk, sums):
        row = chunk * row_chunk
        sums = list(sums)
        for half in range(pair):
            for part in range(row_chunk // 32):
                scores = score_ref[buffer, aligned(row + part * 32, 32), half * 128 : (half + 1) * 128]
                scores = scores.reshape(4, 8, 128)
                for m in range(pos_count):
                    at = half * pos_count + m
                    bent = jnp.tanh(scores - pos[at][None])
                    sums[2 * at] = sums[2 * at] + jnp.sum(bent, axis=0)
                    sums[2 * at + 1] = sums[2 * at + 1] + jnp.sum(bent * bent, axis=0)
        return tuple(sums)

    def over_chunks(step, have):
        if not small:
            return lax.fori_loop(0, chunks, step, have)
        for chunk in range(chunks):
            have = step(chunk, have)
        return have

    chunks = total // row_chunk
    nothing = (jnp.zeros((8, 128), jnp.float32),) * pair
    zero = (jnp.zeros((8, 128), jnp.float32),) * (2 * pos_count * pair)

    def split(start, buffer, picked):
        inside = (buffer, aligned(start, lane_block), slice(None))
        index = lax.broadcasted_iota(jnp.int32, (lane_block, lane_block), 0)
        lane = lax.broadcasted_iota(jnp.int32, (lane_block, lane_block), 1)
        score_ref[inside] = jnp.where(index == lane, masked, score_ref[inside])
        pos = []
        for half in range(pair):
            lanes = aligned(start + half * 128, 128)
            own_ref[:, lanes] = score_ref[buffer, 0:shard, half * 128 : (half + 1) * 128]
            stat_ref[0:8, lanes] = picked[half]
            for m in range(pos_count):
                pos.append(jnp.broadcast_to(picked[half][m : m + 1, :], (8, 128)))
        return tuple(pos)

    def finish(start, sums):
        for half in range(pair):
            lanes = aligned(start + half * 128, 128)
            for m in range(pos_count):
                at = (half * pos_count + m) * 2
                stat_ref[8 + m : 9 + m, lanes] = jnp.sum(sums[at], axis=0, keepdims=True)
                stat_ref[16 + m : 17 + m, lanes] = jnp.sum(sums[at + 1], axis=0, keepdims=True)

    first = embed_ref[0:lane_block, :]
    picked = over_chunks(lambda chunk, have: score_chunk(first, 0, 0, chunk, have), nothing)

    def block_step(block, pos):
        start = block * lane_block
        following = start + lane_block
        buffer = block % 2
        anchors = embed_ref[aligned(following, lane_block), :]

        def both(chunk, carry):
            picked, sums = carry
            picked = score_chunk(anchors, following, 1 - buffer, chunk, picked)
            return picked, rank_chunk(pos, buffer, chunk, sums)

        picked, sums = over_chunks(both, (nothing, zero))
        finish(start, sums)
        return split(following, 1 - buffer, picked)

    last = total // lane_block - 1
    pos = split(0, 0, picked)
    if small:
        for block in range(last):
            pos = block_step(block, pos)
    else:
        pos = lax.fori_loop(0, last, block_step, pos)
    sums = over_chunks(lambda chunk, have: rank_chunk(pos, last % 2, chunk, have), zero)
    finish(last * lane_block, sums)

    def turned(values, steps):
        return jnp.concatenate([values[steps:], values[:steps]], axis=0)

    spot = stat_ref[0:pos_count, :]
    ranks = 0.5 + 0.5 * (total + stat_ref[8 : 8 + pos_count, :])
    slopes = 0.25 * (total - stat_ref[16 : 16 + pos_count, :])
    factor = 1.0 / (pos_count * total)
    pulls = -factor / ranks
    prank = 1.0
    pulled = 0.0
    for steps in range(1, pos_count):
        bent = jnp.tanh(turned(spot, steps) - spot)
        prank = prank + 0.5 * (1.0 + bent)
        pulled = pulled + (turned(pulls, steps) - pulls) * (0.25 * (1.0 - bent * bent))
    weight = prank / (ranks * ranks) * (factor / logistic_sharpness)
    stat_ref[8 : 8 + pos_count, :] = 0.25 * weight
    stat_ref[16 : 16 + pos_count, :] = pulled / logistic_sharpness - weight * slopes

    scores = own_ref[...]
    lane = lax.broadcasted_iota(jnp.int32, (shard, total), 1)
    line = lax.broadcasted_iota(jnp.int32, (shard, total), 0)
    columns = jnp.transpose(
        jnp.concatenate(
            [stat_ref[:, 0:128], target_ref[:, 0:128].astype(jnp.float32)], axis=0
        )
    )[0:shard, :]
    grads = [jnp.zeros((shard, total), jnp.float32) for _ in range(2)]
    for m in range(pos_count):
        bent = jnp.tanh(scores - stat_ref[m : m + 1, :])
        grads[0] = grads[0] + stat_ref[8 + m : 9 + m, :] * (1.0 - bent * bent)
        bent = jnp.tanh(scores - columns[:, m : m + 1])
        grads[1] = grads[1] + columns[:, 8 + m : 9 + m] * (1.0 - bent * bent)
    for m in range(pos_count):
        found = line == target_ref[m : m + 1, :]
        grads[0] = grads[0] + jnp.where(found, stat_ref[16 + m : 17 + m, :], 0.0)
        found = lane == columns[:, 24 + m : 25 + m].astype(jnp.int32)
        grads[1] = grads[1] + jnp.where(found, columns[:, 16 + m : 17 + m], 0.0)
    both = jnp.concatenate(grads, axis=0).astype(jnp.bfloat16)
    product = jnp.dot(both, embed_ref[...], preferred_element_type=jnp.float32)
    out_ref[...] = product[:shard, :] + product[shard:, :]


def body(embed, positives, placement):
    shard, width = embed.shape
    axes = ("row", "col")
    rows = lax.axis_size("row")
    cols = lax.axis_size("col")
    levels = rows // 2
    total = shard * rows * cols
    pos_count = positives.shape[1]
    lane_block = 256 if total <= 4096 else 128

    def swap(array, axis, mask):
        size = lax.axis_size(axis)
        return lax.ppermute(array, axis, [(i, i ^ mask) for i in range(size)])

    def join(parts):
        return parts[0] if len(parts) == 1 else jnp.concatenate(parts, axis=0)

    line = {d: swap(embed, "row", 2 * d) for d in range(1, levels)}
    far = levels - 1
    middle = far // 2 + 1
    ranking = [middle, far] + [d for d in range(1, far) if d != middle]
    corner = cols - 1
    early = swap(embed, "col", corner)
    early_first, again = lax.optimization_barrier((early, embed))
    mine = {p: swap(again, "col", p) for p in range(1, corner)}
    parts, mine = lax.optimization_barrier(
        ([line[middle], line[far], early] + [line[d] for d in ranking[2:]], mine)
    )
    early_after = parts.pop(2)
    line = dict(zip([middle, far] + ranking[2:], parts))
    tall = join([embed] + [line[d] for d in range(1, levels)])

    ids = positives.T
    ids = jnp.concatenate([ids // 256, ids % 256], axis=0).astype(jnp.bfloat16).reshape(-1, 128)
    ids = jnp.concatenate([ids, jnp.zeros((shard - ids.shape[0], 128), ids.dtype)], axis=0)
    early = jnp.concatenate([early_first, ids], axis=1)

    plane = {0: tall}
    plane.update({p: join([mine[p], swap(tall[shard:], "col", p)]) for p in range(1, corner)})
    beyond = {d: swap(early, "row", 2 * d) for d in range(1, levels)}
    corner_rows = jnp.concatenate([early_after, ids], axis=1)
    plane[corner] = join([corner_rows] + [beyond[d] for d in range(1, levels)])

    other = {p: swap(plane[p], "row", 1) for p in range(cols)}
    pieces = []
    layout = []
    for p in range(cols):
        for c, part in enumerate((plane[p], other[p])):
            pieces.append(part)
            layout.append([(d * 2 + c) * cols + p for d in range(levels)])

    place = jnp.stack([lax.axis_index(axes) * shard, lax.axis_index("col") * shard])
    vmem = pl.BlockSpec(memory_space=pltpu.VMEM)
    return pl.pallas_call(
        functools.partial(kernel, cols, shard, pos_count, lane_block, layout),
        out_shape=jax.ShapeDtypeStruct((shard, width), jnp.float32),
        in_specs=[pl.BlockSpec(memory_space=pltpu.SMEM)] + [vmem] * (1 + len(pieces)),
        out_specs=vmem,
        scratch_shapes=[
            pltpu.VMEM((total, width), jnp.bfloat16),
            pltpu.VMEM((2, total, lane_block), jnp.float32),
            pltpu.VMEM((shard, total), jnp.float32),
            pltpu.VMEM((8, total), jnp.int32),
            pltpu.VMEM((24, total), jnp.float32),
        ],
        compiler_params=pltpu.CompilerParams(vmem_limit_bytes=4 * total * width + 8 * total * lane_block + (16 << 20)),
        cost_estimate=pl.CostEstimate(
            flops=2 * total * total * width,
            bytes_accessed=2 * total * width,
            transcendentals=4 * total * total,
        ),
    )(
        place.astype(jnp.int32),
        placement.reshape(-1, 128),
        *pieces,
    )


def solution(mesh):
    return jax.shard_map(
        body,
        mesh=mesh,
        in_specs=(P(("row", "col"), None), P("row", None), P()),
        out_specs=P(("row", "col"), None),
        check_vma=False,
    )
```
